32 devices in a mesh: batch: 32 (over z, y, x, core).
Axes of the slice: x: 2, y: 2, z: 4, core: 2. Of those that a mesh axis runs over, the one named last changes fastest.
Arguments:
- tokens: bfloat16 [32, 8, 128, 768], P('batch'), may hold values from -6 to 6
- lengths: int32 [64], replicated, may hold values from 256 to 512, as said below
- cotangent: bfloat16 [32, 8, 64, 768], P('batch'), may hold values from -6 to 6
- query_weight: bfloat16 [768, 768], replicated, may hold values from -0.21875 to 0.21875
- query_bias: float32 [768], replicated, may hold values from -3 to 3
- key_weight: bfloat16 [768, 768], replicated, may hold values from -0.21875 to 0.21875
- value_weight: bfloat16 [768, 768], replicated, may hold values from -0.21875 to 0.21875
- value_bias: float32 [768], replicated, may hold values from -0.3125 to 0.3125
- content_bias: float32 [768], replicated, may hold values from -3 to 3
- position_bias: float32 [768], replicated, may hold values from -3 to 3
- position_weight: float32 [12, 64, 64], replicated, may hold values from -0.75 to 0.75
- out_weight: bfloat16 [768, 768], replicated, may hold values from -1.75 to 1.75
- out_bias: float32 [768], replicated, may hold values from -3 to 3
- inner_gain: float32 [768], replicated, may hold values from 0.5 to 1.5
- inner_shift: float32 [768], replicated, may hold values from -3 to 3
- up_weight: bfloat16 [768, 3072], replicated, may hold values from -0.21875 to 0.21875
- up_bias: float32 [3072], replicated, may hold values from -3 to 3
- down_weight: bfloat16 [3072, 768], replicated, may hold values from -0.109375 to 0.109375
- down_bias: float32 [768], replicated, may hold values from -3 to 3
- outer_gain: float32 [768], replicated, may hold values from 0.5 to 1.5
- outer_shift: float32 [768], replicated, may hold values from -3 to 3
Outputs:
- layer_output: bfloat16 [32, 8, 64, 768], P('batch')
- tokens_grad: float32 [32, 8, 128, 768], P('batch')
- query_weight_grad: float32 [768, 768], replicated
- query_bias_grad: float32 [768], replicated
- key_weight_grad: float32 [768, 768], replicated
- value_weight_grad: float32 [768, 768], replicated
- value_bias_grad: float32 [768], replicated
- content_bias_grad: float32 [768], replicated
- position_bias_grad: float32 [768], replicated
- position_weight_grad: float32 [12, 64, 64], replicated
- out_weight_grad: float32 [768, 768], replicated
- out_bias_grad: float32 [768], replicated
- inner_gain_grad: float32 [768], replicated
- inner_shift_grad: float32 [768], replicated
- up_weight_grad: float32 [768, 3072], replicated
- up_bias_grad: float32 [3072], replicated
- down_weight_grad: float32 [3072, 768], replicated
- down_bias_grad: float32 [768], replicated
- outer_gain_grad: float32 [768], replicated
- outer_shift_grad: float32 [768], replicated
The draws below stay inside these ranges and needn't reach their ends.
Inputs may be any that keep to these rules, and one draw needn't show every extreme that they name: `lengths`: each entry is 256 or 512; among the 8 rows of each group (rows g * 8 to g * 8 + 7) at least one has 512.
All inputs are finite; a program needn't handle non-finite values.
Results may differ from the reference program's by a relative error of at most 0.014.
The reference program's roundings to bfloat16 on the way count: a program that leaves them out, or rounds other values in their place, can miss the bound.
Values may be sent and summed in bfloat16 or wider, within the bound.
No kernel may reach another device: no remote copies, remote signals or barrier semaphores. Data moves between devices by JAX's collectives and lax.ppermute only.
A program may use at most 192 MiB of HBM per device.

```python
import math
import jax
import jax.numpy as jnp
from jax import lax

D = 768
H = 12
DH = 64
FF = 3072
SEQ = 512
G = 4
RPG = 8
SEG = 128
PS = 64
POOLED = 256
GROUPS = 8
N_BATCH = 32


def draw_lengths(key, part):
    key = jax.random.fold_in(key, 7)
    coin_key, pick_key = jax.random.split(key)
    coin_flips = jax.random.randint(coin_key, (GROUPS, RPG), 0, 2)
    chosen = jax.random.randint(pick_key, (GROUPS, 1), 0, RPG)
    forced = (jnp.arange(RPG, dtype=jnp.int32)[None, :] == chosen).astype(jnp.int32)
    full_rows = jnp.maximum(coin_flips, forced)
    return (POOLED + POOLED * full_rows).reshape(GROUPS * RPG).astype(jnp.int32)


def levels(rng, extent, shards, least, largest):
    def one(axis_at, shards_of):
        steps = jax.random.uniform(jax.random.fold_in(jax.random.fold_in(rng, 6), axis_at), (shards_of,), jnp.float32, least / len(shards), largest / len(shards))
        return jnp.repeat(jnp.exp(steps), extent[axis_at] // shards_of).reshape((-1,) + (1,) * (len(extent) - axis_at - 1))

    level = one(*shards[0])
    for cut in shards[1:]:
        level = level * one(*cut)
    return level


def normal_values(rng, dims, width, most, cuts=(), kind=jnp.bfloat16):
    drawn = width * jax.random.normal(rng, dims, jnp.float32)
    if cuts:
        drawn = drawn * levels(rng, dims, cuts, -0.22, 0.18)
    return jnp.clip(drawn, -most, most).astype(kind)


def setup_inputs(seed: int = 0) -> dict:
    keys = jax.random.split(jax.random.key(seed), 22)
    tokens = normal_values(keys[0], (N_BATCH, RPG, SEG, D), 1.0, 6.0, ((0, 32),))
    lengths = draw_lengths(jax.random.fold_in(keys[21], 71), 0)
    cotangent = normal_values(keys[2], (N_BATCH, RPG, PS, D), 1.0, 6.0, ((0, 32),))
    query_weight = normal_values(keys[3], (D, D), D ** -0.5, 0.21875)
    query_bias = normal_values(keys[4], (D,), 0.5, 3.0, (), jnp.float32)
    key_weight = normal_values(keys[5], (D, D), D ** -0.5, 0.21875)
    value_weight = normal_values(keys[6], (D, D), D ** -0.5, 0.21875)
    value_bias = normal_values(keys[7], (D,), 0.05, 0.3125, (), jnp.float32)
    content_bias = normal_values(keys[8], (D,), 0.5, 3.0, (), jnp.float32)
    position_bias = normal_values(keys[9], (D,), 0.5, 3.0, (), jnp.float32)
    position_weight = normal_values(keys[10], (H, DH, DH), DH ** -0.5, 0.75, (), jnp.float32)
    out_weight = normal_values(keys[11], (D, D), (max(D // 64, 1)) ** -0.5, 1.75)
    out_bias = normal_values(keys[12], (D,), 0.5, 3.0, (), jnp.float32)
    inner_gain = jnp.clip(1.0 + 0.1 * jax.random.normal(keys[13], (D,), jnp.float32), 0.5, 1.5)
    inner_shift = normal_values(keys[14], (D,), 0.5, 3.0, (), jnp.float32)
    up_weight = normal_values(keys[15], (D, FF), D ** -0.5, 0.21875)
    up_bias = normal_values(keys[16], (FF,), 0.5, 3.0, (), jnp.float32)
    down_weight = normal_values(keys[17], (FF, D), FF ** -0.5, 0.109375)
    down_bias = normal_values(keys[18], (D,), 0.5, 3.0, (), jnp.float32)
    outer_gain = jnp.clip(1.0 + 0.1 * jax.random.normal(keys[19], (D,), jnp.float32), 0.5, 1.5)
    outer_shift = normal_values(keys[20], (D,), 0.5, 3.0, (), jnp.float32)
    return dict(tokens=tokens, lengths=lengths, cotangent=cotangent, query_weight=query_weight, query_bias=query_bias, key_weight=key_weight, value_weight=value_weight, value_bias=value_bias, content_bias=content_bias, position_bias=position_bias, position_weight=position_weight, out_weight=out_weight, out_bias=out_bias, inner_gain=inner_gain, inner_shift=inner_shift, up_weight=up_weight, up_bias=up_bias, down_weight=down_weight, down_bias=down_bias, outer_gain=outer_gain, outer_shift=outer_shift)


@jax.custom_vjp
def low(v):
    return lax.optimization_barrier(v.astype(jnp.bfloat16)).astype(jnp.float32)

@jax.custom_vjp
def low_back(v):
    return v

def low_keep(v):
    return (low(v), None)

def low_pass(kept, grad):
    return (grad,)

def back_keep(v):
    return (v, None)

def back_low(kept, grad):
    return (low(grad),)
low.defvjp(low_keep, low_pass)
low_back.defvjp(back_keep, back_low)

def product(former, latter):
    return jnp.dot(former, latter, precision=lax.Precision.HIGHEST)

def contract(pattern, former, latter):
    return jnp.einsum(pattern, former, latter, precision=lax.Precision.HIGHEST)

def layer_norm(inputs, norm_gain, norm_shift):
    center = inputs - lax.optimization_barrier(jnp.mean(inputs, axis=-1, keepdims=True))
    spread = lax.optimization_barrier(jnp.mean(center * center, axis=-1, keepdims=True))
    return center * lax.rsqrt(spread + 1e-05) * norm_gain + norm_shift

def frequencies(number):
    indices = jnp.arange(number, dtype=jnp.float32)
    return jnp.exp(indices * (-math.log(10000.0) / number))

def query_side(project, cosines, sines):
    middle = project.shape[-1] // 2
    first_half = project[..., :middle]
    second_half = project[..., middle:]
    return jnp.concatenate([first_half * sines + second_half * cosines, second_half * sines - first_half * cosines], axis=-1)

def key_table(length, frequency):
    angles = jnp.arange(length, dtype=jnp.float32)[:, None] * frequency[None, :]
    return jnp.concatenate([jnp.cos(angles), jnp.sin(angles)], axis=-1)

def block_rows(params, row_block, row_lengths):
    query_weight, query_bias, key_weight, value_weight, value_bias, content_bias, position_bias, position_weight, out_weight, out_bias, inner_gain, inner_shift, up_weight, up_bias, down_weight, down_bias, outer_gain, outer_shift = params
    row_count = row_block.shape[0]
    pooled = 0.5 * (row_block[:, 0::2] + row_block[:, 1::2])
    queries = low_back(product(low(pooled), query_weight) + query_bias)
    key_all = low(product(row_block, key_weight)).reshape(row_count, SEQ, H, DH)
    value_all = low(product(row_block, value_weight) + value_bias).reshape(row_count, SEQ, H, DH)
    by_head = queries.reshape(row_count, POOLED, H, DH)
    content = low(by_head + content_bias.reshape(H, DH))
    project = contract('rphd,hde->rphe', by_head + position_bias.reshape(H, DH), position_weight)
    frequency = frequencies(DH // 2)
    angles = (2.0 * jnp.arange(POOLED, dtype=jnp.float32))[:, None] * frequency[None, :]
    query_pos = low(query_side(project, jnp.cos(angles)[:, None, :], jnp.sin(angles)[:, None, :]))
    key_pos = low(key_table(SEQ, frequency))
    allowed = jnp.arange(SEQ, dtype=jnp.int32)[None, :] < row_lengths[:, None]
    pieces = []
    for block in range(G):
        start = block * PS
        key_heads = low_back(key_all)
        value_heads = low_back(value_all)
        content_part = content[:, start:start + PS]
        query_part = query_pos[:, start:start + PS]
        scores = (contract('rphd,rkhd->rhpk', content_part, key_heads) + contract('rphd,kd->rhpk', query_part, key_pos)) * DH ** (-0.5)
        scores = low_back(jnp.where(allowed[:, None, None, :], scores, -1000000000.0))
        highest = lax.optimization_barrier(jnp.max(scores, axis=-1, keepdims=True))
        raised = jnp.exp(scores - highest)
        weights = raised / lax.optimization_barrier(jnp.sum(raised, axis=-1, keepdims=True))
        pieces.append(contract('rhpk,rkhd->rphd', low(weights), value_heads))
    context = jnp.concatenate(pieces, axis=1).reshape(row_count, POOLED, D)
    context = low(low_back(context))
    attended = low_back(product(context, out_weight) + out_bias)
    normed = layer_norm(pooled + attended, inner_gain, inner_shift)
    hidden = low_back(product(low(normed), up_weight) + up_bias)
    branch = low_back(product(low(jax.nn.gelu(hidden, approximate=False)), down_weight) + down_bias)
    return layer_norm(normed + branch, outer_gain, outer_shift)

def to_rows(blocks, seg_width):
    return blocks.reshape(GROUPS, G, RPG, seg_width, D).transpose(0, 2, 1, 3, 4).reshape(GROUPS, RPG, G * seg_width, D)

def to_devices(blocks, seg_width):
    return blocks.reshape(GROUPS, RPG, G, seg_width, D).transpose(0, 2, 1, 3, 4).reshape(GROUPS * G, RPG, seg_width, D)

def reference(tokens, lengths, cotangent, query_weight, query_bias, key_weight, value_weight, value_bias, content_bias, position_bias, position_weight, out_weight, out_bias, inner_gain, inner_shift, up_weight, up_bias, down_weight, down_bias, outer_gain, outer_shift):
    params = tuple((argument.astype(jnp.float32) for argument in (query_weight, query_bias, key_weight, value_weight, value_bias, content_bias, position_bias, position_weight, out_weight, out_bias, inner_gain, inner_shift, up_weight, up_bias, down_weight, down_bias, outer_gain, outer_shift)))
    row_blocks = to_rows(tokens.astype(jnp.float32), SEG)
    back_blocks = to_rows(cotangent.astype(jnp.float32), PS)
    length_blocks = lengths.reshape(GROUPS, RPG)

    def forward(weights_all, inputs):

        def one_group(member):
            return jax.checkpoint(block_rows)(weights_all, member[0], member[1])
        return lax.map(one_group, (inputs, length_blocks))
    result, pull_back = jax.vjp(forward, params, row_blocks)
    param_grads, input_grads = pull_back(back_blocks)
    query_weight_grad, query_bias_grad, key_weight_grad, value_weight_grad, value_bias_grad, content_bias_grad, position_bias_grad, position_weight_grad, out_weight_grad, out_bias_grad, inner_gain_grad, inner_shift_grad, up_weight_grad, up_bias_grad, down_weight_grad, down_bias_grad, outer_gain_grad, outer_shift_grad = param_grads
    return (to_devices(result, PS).astype(jnp.bfloat16), to_devices(input_grads, SEG), query_weight_grad, query_bias_grad, key_weight_grad, value_weight_grad, value_bias_grad, content_bias_grad, position_bias_grad, position_weight_grad, out_weight_grad, out_bias_grad, inner_gain_grad, inner_shift_grad, up_weight_grad, up_bias_grad, down_weight_grad, down_bias_grad, outer_gain_grad, outer_shift_grad)
```

```python
import functools
import math

import jax
import jax.numpy as jnp
from jax import lax
from jax.experimental import pallas as pl
from jax.experimental.pallas import tpu as pltpu
from jax.sharding import PartitionSpec as P

G = 4
F32 = jnp.float32
BF = jnp.bfloat16
VM = pl.BlockSpec(memory_space=pltpu.VMEM)
SM = pl.BlockSpec(memory_space=pltpu.SMEM)
BLK = 16
CH = 512


def nn(a, b):
    return lax.dot_general(a, b, (((1,), (0,)), ((), ())), preferred_element_type=F32)


def nt(a, b):
    return lax.dot_general(a, b, (((1,), (1,)), ((), ())), preferred_element_type=F32)


def tn(a, b):
    return lax.dot_general(a, b, (((0,), (0,)), ((), ())), preferred_element_type=F32)


def split(a):
    hi = a.astype(BF)
    return hi, (a - hi.astype(F32)).astype(BF)


def three(dot, a_hi, a_lo, b_hi, b_lo):
    return dot(a_hi, b_hi) + (dot(a_hi, b_lo) + dot(a_lo, b_hi))


def params(mib):
    return pltpu.CompilerParams(vmem_limit_bytes=mib << 20)


def cost(flops, bytes_accessed, transcendentals=0):
    return pl.CostEstimate(
        flops=flops, bytes_accessed=bytes_accessed, transcendentals=transcendentals
    )


def attn_fwd_kernel(
    x0, x1, x2, x3, wq, wk, wv, qb, cb, pb, vb, wph, wpl, sin4, cos4, kfa, kfb,
    k_out, v_out, kt_out, xt_out, qc_out, qf_out, qht_out, qlt_out, pt_out, pooled_out,
    ctx_out, ctxt_out, lse_out,
    x_s, vt_s,
):
    rows = lax.broadcasted_iota(jnp.int32, (64, 128), 0)
    cols = lax.broadcasted_iota(jnp.int32, (64, 128), 1)
    pair = jnp.where(cols // 2 == rows, 0.5, 0.0).astype(BF)
    for d, piece in enumerate((x0, x1, x2, x3)):
        x_s[d * 128 : d * 128 + 128, :] = piece[...]
        pooled_out[d * 64 : d * 64 + 64, :] = nn(pair, piece[...])
    pooled_low = pooled_out[...].astype(BF)
    pt_out[...] = pooled_low.T
    x = x_s[...]
    xt_out[...] = x.T
    q = nn(pooled_low, wq[...]) + qb[...]
    k = nn(x, wk[...]).astype(BF)
    k_out[...] = k
    kt_out[...] = k.T
    v = (nn(x, wv[...]) + vb[...]).astype(BF)
    v_out[...] = v
    vt_s[...] = v.T
    qc_out[...] = (q + cb[...]).astype(BF) * 0.125
    hi, lo = split(q + pb[...])
    qht_out[...] = hi.T
    qlt_out[...] = lo.T
    for g in range(3):
        at = slice(256 * g, 256 * g + 256)
        both = three(nn, hi[:, at], lo[:, at], wph[g], wpl[g])
        side = both[:, :256] * sin4[...] + both[:, 256:] * cos4[...]
        qf_out[:, at] = side.astype(BF) * 0.125
    lane = lax.broadcasted_iota(jnp.int32, (256, 128), 1)
    zero = jnp.zeros((256, 128), BF)
    one_a = (lane == 64).astype(F32).astype(BF)
    one_b = (lane == 0).astype(F32).astype(BF)

    def one_pair(i, carry):
        at = pl.ds(pl.multiple_of(i * 128, 128), 128)
        k_pair = k_out[:, at]
        qc_pair = qc_out[:, at]
        qf_pair = qf_out[:, at]
        for s in range(2):
            mine = (lane < 64) if s == 0 else (lane >= 64)
            left = jnp.concatenate([k_pair, (kfa, kfb)[s][...]], axis=1)
            right = jnp.concatenate(
                [jnp.where(mine, qc_pair, zero), jnp.where(mine, qf_pair, (one_a, one_b)[s])], axis=1
            )
            scores = nt(left, right)
            highest = jnp.max(scores, axis=0, keepdims=True)
            raised = jnp.exp(scores - highest)
            total = jnp.sum(raised, axis=0, keepdims=True)
            weights = (raised * (1.0 / total)).astype(BF)
            head = pl.ds(pl.multiple_of(i * 128 + s * 64, 64), 64)
            ctxt_out[head, :] = nn(vt_s[head, :], weights).astype(BF)
            lse_out[i * 2 + s] = highest + jnp.log(total)
        return carry

    lax.fori_loop(0, 6, one_pair, 0)
    ctx_out[...] = ctxt_out[...].T


def attn_fwd(pieces, w):
    b16 = lambda *s: jax.ShapeDtypeStruct(s, BF)
    f32 = lambda *s: jax.ShapeDtypeStruct(s, F32)
    return pl.pallas_call(
        attn_fwd_kernel,
        out_shape=(
            b16(512, 768), b16(512, 768), b16(768, 512), b16(768, 512), b16(256, 768), b16(256, 768),
            b16(768, 256), b16(768, 256), b16(768, 256), f32(256, 768), b16(256, 768), b16(768, 256),
            f32(12, 1, 256),
        ),
        in_specs=[VM] * 17,
        out_specs=[VM] * 13,
        scratch_shapes=[pltpu.VMEM((512, 768), BF), pltpu.VMEM((768, 512), BF)],
        compiler_params=params(40),
        cost_estimate=cost(4 * 10**9, 12 * 10**6, 12 * 512 * 256),
        name="attn_fwd",
    )(*pieces, *w)


def layer_stats(a):
    center = a - jnp.mean(a, axis=-1, keepdims=True)
    rs = lax.rsqrt(jnp.mean(center * center, axis=-1, keepdims=True) + 1e-05)
    return center * rs, rs


def layer_back(dn, n, rs):
    return rs * (dn - jnp.mean(dn, axis=-1, keepdims=True) - n * jnp.mean(dn * n, axis=-1, keepdims=True))


def ffn_kernel(
    masks, ctx0, ctx1, ctxt0, ctxt1, pooled0, pooled1, c0, c1, c2, c3, wo, wu, wd, ob, ig, ish, ub, db, og, osh,
    out0, out1, out2, out3, d1_out, dctx_out, wog_out, kd_out, sd_out, ku_out, su_out, vec_out, upb_out,
    gp_s, act_s, acc_s, x1_s, n1_s, x1t_s, df_s, rs_s, g_s, u_s,
):
    ctx = jnp.concatenate([ctx0[...], ctx1[...]], axis=0)
    pooled = jnp.concatenate([pooled0[...], pooled1[...]], axis=0)
    n1, rs1 = layer_stats(pooled + (nn(ctx, wo[...]) + ob[...]))
    n1_s[...] = n1
    rs_s[...] = rs1
    x1 = n1 * ig[...] + ish[...]
    x1_s[...] = x1.astype(BF)
    x1t_s[...] = x1.astype(BF).T
    acc_s[...] = x1 + db[...]

    def up_chunk(c, carry):
        at = pl.ds(pl.multiple_of(c * CH, CH), CH)
        z = nn(x1_s[...], wu[:, at]) + ub[:, at]
        phi = 0.5 + 0.5 * lax.erf(z * math.sqrt(0.5))
        gp_s[:, at] = phi + z * (jnp.exp(-0.5 * z * z) * (1.0 / math.sqrt(2.0 * math.pi)))
        act = (z * phi).astype(BF)
        act_s[:, at] = act
        acc_s[...] += nn(act, wd[at, :])
        return carry

    lax.fori_loop(0, 6, up_chunk, 0)
    n2, rs2 = layer_stats(acc_s[...])
    result = (n2 * og[...] + osh[...]).astype(BF)
    for d, out in enumerate((out0, out1, out2, out3)):
        for r in range(2):
            out[r] = result[r * 256 + d * 64 : r * 256 + d * 64 + 64, :]
    cot = jnp.concatenate([c[r] for r in range(2) for c in (c0, c1, c2, c3)], axis=0).astype(F32)
    vec_out[0:1, :] = jnp.sum(cot * n2, axis=0, keepdims=True)
    vec_out[1:2, :] = jnp.sum(cot, axis=0, keepdims=True)
    d2 = layer_back(cot * og[...], n2, rs2)
    df = d2.astype(BF)
    df_s[...] = df
    vec_out[2:3, :] = jnp.sum(df.astype(F32), axis=0, keepdims=True)
    acc_s[...] = d2

    def back_chunk(c, carry):
        at = pl.ds(pl.multiple_of(c * CH, CH), CH)
        df = df_s[...]
        dz = (nt(df, wd[at, :]) * gp_s[:, at]).astype(BF)
        upb_out[:, at] = jnp.sum(dz.astype(F32), axis=0, keepdims=True)
        acc_s[...] += nt(dz, wu[:, at])
        g_s[...] = tn(act_s[:, at], df)
        u_s[...] = nn(x1t_s[...], dz)
        which = c // 3
        slab = (c % 3) * 6
        me = masks[which]
        for r in range(32):
            place = r ^ me
            row = pl.ds(pl.multiple_of(place * 16, 16), 16)
            urow = pl.multiple_of((place // 4) * 96, 32)
            ucol = pl.ds(pl.multiple_of((place % 4) * 128, 128), 128)
            down = (kd_out, sd_out)[r // 16]
            up = (ku_out, su_out)[r // 16]
            for j in range(6):
                down[which, r % 16, slab + j] = g_s[row, j * 128 : j * 128 + 128].astype(BF)
                up[which, r % 16, slab + j] = u_s[pl.ds(urow + 16 * j, 16), ucol].astype(BF)
        return carry

    lax.fori_loop(0, 6, back_chunk, 0)
    dx1 = acc_s[...]
    n1 = n1_s[...]
    vec_out[3:4, :] = jnp.sum(dx1 * n1, axis=0, keepdims=True)
    vec_out[4:5, :] = jnp.sum(dx1, axis=0, keepdims=True)
    d1 = layer_back(dx1 * ig[...], n1, rs_s[...])
    d1_out[...] = d1
    do = d1.astype(BF)
    vec_out[5:6, :] = jnp.sum(do.astype(F32), axis=0, keepdims=True)
    dctx_out[...] = nt(do, wo[...]).astype(BF)
    wog_out[...] = nn(jnp.concatenate([ctxt0[...], ctxt1[...]], axis=1), do)


def ffn(args):
    b16 = lambda *s: jax.ShapeDtypeStruct(s, BF)
    f32 = lambda *s: jax.ShapeDtypeStruct(s, F32)
    grad = b16(2, 16, 18, 16, 128)
    return pl.pallas_call(
        ffn_kernel,
        out_shape=(
            b16(2, 64, 768), b16(2, 64, 768), b16(2, 64, 768), b16(2, 64, 768), f32(512, 768), b16(512, 768),
            f32(768, 768), grad, grad, grad, grad, f32(8, 768), f32(1, 3072),
        ),
        in_specs=[SM] + [VM] * 20,
        out_specs=[VM] * 13,
        scratch_shapes=[
            pltpu.VMEM((512, 3072), F32), pltpu.VMEM((512, 3072), BF), pltpu.VMEM((512, 768), F32),
            pltpu.VMEM((512, 768), BF), pltpu.VMEM((512, 768), F32), pltpu.VMEM((768, 512), BF),
            pltpu.VMEM((512, 768), BF), pltpu.VMEM((512, 1), F32), pltpu.VMEM((512, 768), F32),
            pltpu.VMEM((768, 512), F32),
        ],
        compiler_params=params(60),
        cost_estimate=cost(16 * 10**9, 40 * 10**6, 3 * 10**6),
        name="ffn",
    )(*args)


def attn_bwd_kernel(
    k, v, kt, qc, qf, qht, qlt, lse, dctx, kfa, kfb, kst, sint, cost_t, wph, wpl,
    dk_out, dv_out, dq_out, pwg_out, vec_out,
    dqct_s, dpt_s,
):
    lane = lax.broadcasted_iota(jnp.int32, (256, 128), 1)
    zero = jnp.zeros((256, 128), BF)
    one_a = (lane == 64).astype(F32).astype(BF)
    one_b = (lane == 0).astype(F32).astype(BF)

    def one_pair(i, carry):
        at = pl.ds(pl.multiple_of(i * 128, 128), 128)
        k_pair = k[:, at]
        v_pair = v[:, at]
        qc_pair = qc[:, at]
        qf_pair = qf[:, at]
        dc_pair = dctx[:, at]
        for s in range(2):
            mine = (lane < 64) if s == 0 else (lane >= 64)
            left = jnp.concatenate([k_pair, (kfa, kfb)[s][...]], axis=1)
            qc_mine = jnp.where(mine, qc_pair, zero)
            dc_mine = jnp.where(mine, dc_pair, zero)
            right = jnp.concatenate([qc_mine, jnp.where(mine, qf_pair, (one_a, one_b)[s])], axis=1)
            weights = jnp.exp(nt(left, right) - lse[i * 2 + s])
            dweights = nt(v_pair, dc_mine)
            inner = jnp.sum(weights * dweights, axis=0, keepdims=True)
            dscore = (weights * (dweights - inner)).astype(BF)
            dv_part = nn(weights.astype(BF), dc_mine)
            dk_part = nn(dscore, qc_mine)
            if s == 0:
                dv_first, dk_first = dv_part, dk_part
            head = pl.ds(pl.multiple_of(i * 128 + s * 64, 64), 64)
            side = nn(jnp.concatenate([kt[head, :], kst[...]], axis=0), dscore)
            dqct_s[head, :] = side[0:64] * 0.125
            dpt_s[head, :] = (side[64:128] * sint[...] + side[128:192] * cost_t[...]) * 0.125
        dv_out[:, at] = (dv_first + dv_part).astype(BF)
        dk_out[:, at] = (dk_first + dk_part).astype(BF)
        return carry

    lax.fori_loop(0, 6, one_pair, 0)
    ones = jnp.ones((8, 256), BF)
    for g in range(3):
        at = slice(256 * g, 256 * g + 256)
        hi, lo = split(dpt_s[at, :])
        pwg_out[g] = three(nt, qht[at, :], qlt[at, :], hi, lo)
        shift = three(nn, wph[g][:, :256], wpl[g][:, :256], hi, lo)
        content = dqct_s[at, :]
        dq = (content + shift).T.astype(BF)
        dq_out[:, at] = dq
        shi, slo = split(shift)
        chi, clo = split(content)
        vec_out[0:1, at] = (nt(ones, chi) + nt(ones, clo))[0:1]
        vec_out[1:2, at] = (nt(ones, shi) + nt(ones, slo))[0:1]
        vec_out[2:3, at] = jnp.sum(dq.astype(F32), axis=0, keepdims=True)
    vec_out[3:4, :] = jnp.sum(dv_out[...].astype(F32), axis=0, keepdims=True)


def attn_bwd(args):
    b16 = lambda *s: jax.ShapeDtypeStruct(s, BF)
    f32 = lambda *s: jax.ShapeDtypeStruct(s, F32)
    return pl.pallas_call(
        attn_bwd_kernel,
        out_shape=(b16(512, 768), b16(512, 768), b16(256, 768), f32(3, 256, 256), f32(8, 768)),
        in_specs=[VM] * 16,
        out_specs=[VM] * 5,
        scratch_shapes=[pltpu.VMEM((768, 256), F32), pltpu.VMEM((768, 256), F32)],
        compiler_params=params(40),
        cost_estimate=cost(8 * 10**9, 12 * 10**6, 12 * 512 * 256),
        name="attn_bwd",
    )(*args)


def proj_kernel(
    masks, xt0, xt1, pt0, pt1, dk0, dk1, dv0, dv1, dq0, dq1, d1, wq, wk, wv, wog, smalls,
    t0, t1, t2, t3, ka_out, sa_out, kb_out, sb_out,
    g_s, tok_s,
):
    rows = lax.broadcasted_iota(jnp.int32, (512, 256), 0)
    cols = lax.broadcasted_iota(jnp.int32, (512, 256), 1)
    spread = jnp.where(rows // 2 == cols, 0.5, 0.0).astype(BF)
    for r, (dk, dv, dq) in enumerate(((dk0, dv0, dq0), (dk1, dv1, dq1))):
        hi, lo = split(d1[r * 256 : r * 256 + 256, :] + nt(dq[...], wq[...]))
        tok_s[...] = (nt(dk[...], wk[...]) + nt(dv[...], wv[...])) + (nn(spread, hi) + nn(spread, lo))
        for d, out in enumerate((t0, t1, t2, t3)):
            out[r] = tok_s[d * 128 : d * 128 + 128, :].astype(BF)
    g_s[0:768, :] = wog[...]
    g_s[768:1536, :] = nn(pt0[...], dq0[...]) + nn(pt1[...], dq1[...])
    g_s[1536:2304, :] = nn(xt0[...], dk0[...]) + nn(xt1[...], dk1[...])
    g_s[2304:3072, :] = nn(xt0[...], dv0[...]) + nn(xt1[...], dv1[...])
    me = (masks[0], masks[1])

    def one_block(r, carry):
        for which in range(2):
            place = r ^ me[which]
            near = (ka_out, kb_out)[which]
            far = (sa_out, sb_out)[which]
            for half, out in enumerate((near, far)):
                at = place ^ (16 * half)
                for c in range(3):
                    row = pl.ds(pl.multiple_of((which * 3 + c) * 512 + at * 16, 16), 16)
                    for j in range(6):
                        out[r, c * 6 + j] = g_s[row, j * 128 : j * 128 + 128].astype(BF)
                if which == 1:
                    row = pl.ds(pl.multiple_of(at * 16, 16), 16)
                    out[r, 18] = smalls[row, :].astype(BF)
        return carry

    lax.fori_loop(0, 16, one_block, 0)


def proj(args):
    b16 = lambda *s: jax.ShapeDtypeStruct(s, BF)
    piece = b16(2, 128, 768)
    return pl.pallas_call(
        proj_kernel,
        out_shape=(
            piece, piece, piece, piece, b16(16, 18, 16, 128), b16(16, 18, 16, 128), b16(16, 19, 16, 128),
            b16(16, 19, 16, 128),
        ),
        in_specs=[SM] + [VM] * 16,
        out_specs=[VM] * 8,
        scratch_shapes=[pltpu.VMEM((3072, 768), F32), pltpu.VMEM((512, 768), F32)],
        compiler_params=params(56),
        cost_estimate=cost(9 * 10**9, 25 * 10**6),
        name="proj_back",
    )(*args)


def partner(x, bit):
    size = lax.axis_size("batch")
    return lax.ppermute(x, "batch", [(i, i ^ bit) for i in range(size)])


def plus(a, b):
    return (a.astype(F32) + b.astype(F32)).astype(BF)


def sum_over(keep_a, keep_b, send_a, send_b, bits):
    core, first, second, third, fourth, others = bits
    a = plus(keep_a, partner(send_a, core))
    b = plus(keep_b, partner(send_b, core))
    a, b = plus(a[:8], partner(a[8:], first)), plus(b[:8], partner(b[8:], second))
    a, b = plus(a[:4], partner(a[4:], second)), plus(b[:4], partner(b[4:], first))
    n = a.shape[1]
    both = jnp.concatenate([a, b], axis=1)
    both = plus(both[:2], partner(both[2:], third))
    both = plus(both[:1], partner(both[1:], fourth))
    for bit in others:
        both = plus(both, partner(both, bit))
    both = jnp.concatenate([both, partner(both, fourth)], axis=0)
    both = jnp.concatenate([both, partner(both, third)], axis=0)
    a, b = both[:, :n], both[:, n:]
    a, b = jnp.concatenate([a, partner(a, second)]), jnp.concatenate([b, partner(b, first)])
    a, b = jnp.concatenate([a, partner(a, first)]), jnp.concatenate([b, partner(b, second)])
    return (a, b), (partner(a, core), partner(b, core))


def rows_kernel(masks, a0, b0, a1, b1, out):
    which = pl.program_id(0) // 3
    me = masks[which]
    slab = (pl.program_id(0) % 3) * 6
    for w, halves in enumerate(((a0, a1), (b0, b1))):

        @pl.when(which == w)
        def _():
            for r in range(32):
                row = pl.ds(pl.multiple_of((r ^ me) * 16, 16), 16)
                for j in range(6):
                    out[row, j * 128 : j * 128 + 128] = halves[r // 16][r % 16, slab + j].astype(F32)


def assemble_rows(masks, near, far):
    return pl.pallas_call(
        rows_kernel,
        out_shape=jax.ShapeDtypeStruct((3072, 768), F32),
        grid=(6,),
        in_specs=[SM] + [VM] * 4,
        out_specs=pl.BlockSpec((512, 768), lambda c: (c, 0)),
        compiler_params=params(24),
        cost_estimate=cost(0, 14 * 10**6),
        name="assemble_rows",
    )(masks, *near, *far)


def up_kernel(masks, a0, b0, a1, b1, out):
    which = pl.program_id(0) // 3
    me = masks[which]
    slab = (pl.program_id(0) % 3) * 6
    for w, halves in enumerate(((a0, a1), (b0, b1))):

        @pl.when(which == w)
        def _():
            for r in range(32):
                place = r ^ me
                row = pl.multiple_of((place // 4) * 96, 32)
                col = pl.ds(pl.multiple_of((place % 4) * 128, 128), 128)
                for j in range(6):
                    out[pl.ds(row + 16 * j, 16), col] = halves[r // 16][r % 16, slab + j].astype(F32)


def assemble_up(masks, near, far):
    return pl.pallas_call(
        up_kernel,
        out_shape=jax.ShapeDtypeStruct((768, 3072), F32),
        grid=(6,),
        in_specs=[SM] + [VM] * 4,
        out_specs=pl.BlockSpec((768, 512), lambda c: (0, c)),
        compiler_params=params(24),
        cost_estimate=cost(0, 14 * 10**6),
        name="assemble_up",
    )(masks, *near, *far)


def four_kernel(masks, a0, b0, a1, b1, o_out, q_out, k_out, v_out, s_out):
    outs = (o_out, q_out, k_out, v_out)
    me = (masks[0], masks[1])
    for w, halves in enumerate(((a0, a1), (b0, b1))):
        for r in range(32):
            place = r ^ me[w]
            for c in range(3):
                block = (w * 3 + c) * 32 + place
                source = halves[r // 16]
                matrix = block // 48
                row = pl.ds(pl.multiple_of((block % 48) * 16, 16), 16)
                first = ((w * 3 + c) * 32) // 48
                last = ((w * 3 + c) * 32 + 31) // 48
                for m in range(first, last + 1):

                    def store(m=m):
                        for j in range(6):
                            outs[m][row, j * 128 : j * 128 + 128] = source[r % 16, c * 6 + j].astype(F32)

                    if first == last:
                        store()
                    else:
                        pl.when(matrix == m)(store)
            if w == 1:
                row = pl.ds(pl.multiple_of(place * 16, 16), 16)
                s_out[row, :] = halves[r // 16][r % 16, 18].astype(F32)


def assemble_four(masks, near, far):
    f32 = lambda *s: jax.ShapeDtypeStruct(s, F32)
    return pl.pallas_call(
        four_kernel,
        out_shape=(f32(768, 768),) * 4 + (f32(512, 128),),
        in_specs=[SM] + [VM] * 4,
        out_specs=[VM] * 5,
        compiler_params=params(40),
        cost_estimate=cost(0, 15 * 10**6),
        name="assemble_four",
    )(masks, *near, *far)


def tokens_kernel(place, p0, p1, p2, p3, out):
    j = place[0]
    for d, piece in enumerate((p0, p1, p2, p3)):
        out[j ^ d] = piece[...].astype(F32)


def assemble_tokens(place, pieces):
    return pl.pallas_call(
        tokens_kernel,
        out_shape=jax.ShapeDtypeStruct((4, 2, 128, 768), F32),
        in_specs=[SM] + [VM] * 4,
        out_specs=VM,
        compiler_params=params(16),
        cost_estimate=cost(0, 5 * 10**6),
        name="assemble_tokens",
    )(place, *pieces)


def swapped(table):
    half = table.shape[-1] // 2
    return jnp.concatenate([table[..., half:], table[..., :half]], axis=-1)


def on_device(
    tokens, lengths, cotangent, query_weight, query_bias, key_weight, value_weight, value_bias, content_bias,
    position_bias, position_weight, out_weight, out_bias, inner_gain, inner_shift, up_weight, up_bias, down_weight,
    down_bias, outer_gain, outer_shift,
):
    size = lax.axis_size("batch")
    me = lax.axis_index("batch")
    j = me % G
    group = me // G
    core, first, second, third, fourth = 1, 2, 4, 8, 16
    others = [1 << b for b in range(5, size.bit_length() - 1)]
    bits = (core, first, second, third, fourth, others)
    has = lambda bit: (me // bit) % 2
    low = has(third) * 2 + has(fourth)
    masks = jnp.stack(
        [
            has(core) * 16 + has(first) * 8 + has(second) * 4 + low,
            has(core) * 16 + has(second) * 8 + has(first) * 4 + low,
        ]
    ).astype(jnp.int32)

    by_owner = tokens[0].reshape(4, 2, 128, 768)
    cot_owner = cotangent[0].reshape(4, 2, 64, 768)
    pick = lambda a, d: lax.dynamic_index_in_dim(a, j ^ d, 0, keepdims=False)
    sends = [pick(by_owner, d) for d in range(4)]
    x = [[sends[0][r]] + [None] * 3 for r in range(2)]
    for r in range(2):
        for d in (2, 3, 1):
            x[r][d] = partner(sends[d][r], d)
    cot = [pick(cot_owner, 0)] + [partner(pick(cot_owner, d), d) for d in (1, 2, 3)]

    w = jnp.exp(jnp.arange(32, dtype=F32) * (-math.log(10000.0) / 32))
    segs = j ^ jnp.arange(4, dtype=jnp.int32)
    q_pos = (2 * (segs[:, None] * 64 + jnp.arange(64, dtype=jnp.int32)[None, :])).reshape(256)
    k_pos = (segs[:, None] * 128 + jnp.arange(128, dtype=jnp.int32)[None, :]).reshape(512)
    theta = q_pos.astype(F32)[:, None] * w[None, :]
    sin, cos = jnp.sin(theta), jnp.cos(theta)
    sin4 = jnp.tile(sin, (1, 8))
    cos4 = jnp.tile(jnp.concatenate([cos, -cos], axis=1), (1, 4))
    sint = jnp.concatenate([sin, sin], axis=1).T
    cost_t = jnp.concatenate([-cos, cos], axis=1).T
    angle = k_pos.astype(F32)[:, None] * w[None, :]
    kf = jnp.concatenate([jnp.cos(angle), jnp.sin(angle)], axis=1).astype(BF)
    kst = jnp.concatenate([kf, swapped(kf)], axis=1).T
    kfa, kfb = [], []
    for r in range(2):
        length = lax.dynamic_index_in_dim(lengths, group * 8 + 2 * j + r, 0, keepdims=False)
        bias = jnp.where(k_pos < length, 0.0, -1.0e9).astype(BF)[:, None]
        rest = jnp.concatenate([bias, jnp.zeros((512, 63), BF)], axis=1)
        kfa.append(jnp.concatenate([kf, rest], axis=1))
        kfb.append(jnp.concatenate([rest, kf], axis=1))
    eye = jnp.eye(4, dtype=F32)
    heads = position_weight.reshape(3, 4, 64, 64)
    block = lambda a: (a[:, :, :, None, :] * eye[None, :, None, :, None]).reshape(3, 256, 256)
    wph, wpl = split(jnp.concatenate([block(heads), block(swapped(heads))], axis=2))

    vec = lambda a: a[None, :]
    fwd = []
    for r in range(2):
        fwd.append(
            attn_fwd(
                x[r],
                (
                    query_weight, key_weight, value_weight, vec(query_bias), vec(content_bias), vec(position_bias),
                    vec(value_bias), wph, wpl, sin4, cos4, kfa[r], kfb[r],
                ),
            )
        )
    k, v, kt, xt, qc, qf, qht, qlt, pt, pooled, ctx, ctxt, lse = zip(*fwd)
    (
        out0, out1, out2, out3, d1, dctx, wog, keep_d, send_d, keep_u, send_u, ffn_vec, up_bias_grad,
    ) = ffn(
        (
            masks, *ctx, *ctxt, *pooled, *cot, out_weight, up_weight, down_weight, vec(out_bias), vec(inner_gain),
            vec(inner_shift), vec(up_bias), vec(down_bias), vec(outer_gain), vec(outer_shift),
        )
    )
    back = [out0] + [partner(out, d) for d, out in ((1, out1), (2, out2), (3, out3))]
    stacked = jnp.stack(back)
    order = j ^ jnp.arange(4, dtype=jnp.int32)
    layer_output = jnp.take(stacked, order, axis=0).reshape(1, 8, 64, 768)

    down = sum_over(keep_d[0], keep_d[1], send_d[0], send_d[1], bits)
    up = sum_over(keep_u[0], keep_u[1], send_u[0], send_u[1], bits)

    bwd = []
    for r in range(2):
        bwd.append(
            attn_bwd(
                (
                    k[r], v[r], kt[r], qc[r], qf[r], qht[r], qlt[r], lse[r], dctx[r * 256 : r * 256 + 256], kfa[r],
                    kfb[r], kst, sint, cost_t, wph, wpl,
                )
            )
        )
    dk, dv, dq, pwg, attn_vec = zip(*bwd)
    attn_vec = attn_vec[0] + attn_vec[1]
    pwg = (pwg[0] + pwg[1]).reshape(3, 4, 64, 4, 64)
    pwg = jnp.stack([pwg[:, h, :, h] for h in range(4)], axis=1)
    smalls = jnp.concatenate(
        [ffn_vec[:6].reshape(-1), up_bias_grad.reshape(-1), attn_vec[:4].reshape(-1), pwg.reshape(-1)]
    )
    smalls = jnp.pad(smalls, (0, 65536 - smalls.size)).reshape(512, 128)
    t0, t1, t2, t3, keep_a, send_a, keep_b, send_b = proj(
        (
            masks, *xt, *pt, *[a for pair in (dk, dv, dq) for a in pair], d1, query_weight, key_weight, value_weight,
            wog, smalls,
        )
    )
    pieces = [t0] + [partner(t, d) for d, t in ((1, t1), (2, t2), (3, t3))]
    four = sum_over(keep_a, keep_b, send_a, send_b, bits)

    tokens_grad = assemble_tokens(j.reshape(1).astype(jnp.int32), pieces).reshape(1, 8, 128, 768)
    down_weight_grad = assemble_rows(masks, *down)
    up_weight_grad = assemble_up(masks, *up)
    out_weight_grad, query_weight_grad, key_weight_grad, value_weight_grad, flat = assemble_four(masks, *four)
    flat = flat.reshape(-1)
    line = lambda i: flat[768 * i : 768 * i + 768]
    return (
        layer_output, tokens_grad, query_weight_grad, line(12), key_weight_grad, value_weight_grad, line(13), line(10),
        line(11), flat[10752 : 10752 + 49152].reshape(12, 64, 64), out_weight_grad, line(5), line(3), line(4),
        up_weight_grad, flat[4608 : 4608 + 3072], down_weight_grad, line(2), line(0), line(1),
    )


def solution(mesh):
    in_specs = (P("batch", None, None, None), P(), P("batch", None, None, None)) + (P(),) * 18
    out_specs = (P("batch", None, None, None),) * 2 + (P(),) * 18
    return jax.shard_map(on_device, mesh=mesh, in_specs=in_specs, out_specs=out_specs, check_vma=False)
```

```python
import functools
import math

import jax
import jax.numpy as jnp
from jax import lax
from jax.experimental import pallas as pl
from jax.experimental.pallas import tpu as pltpu
from jax.sharding import PartitionSpec as P

G = 4
F32 = jnp.float32
BF = jnp.bfloat16
VM = pl.BlockSpec(memory_space=pltpu.VMEM)
SM = pl.BlockSpec(memory_space=pltpu.SMEM)
ANY = pl.BlockSpec(memory_space=pl.ANY)
HBM = pl.BlockSpec(memory_space=pltpu.HBM)
BLK = 16
NA = 12
CH = 512


def nn(a, b):
    return lax.dot_general(a, b, (((1,), (0,)), ((), ())), preferred_element_type=F32)


def nt(a, b):
    return lax.dot_general(a, b, (((1,), (1,)), ((), ())), preferred_element_type=F32)


def tn(a, b):
    return lax.dot_general(a, b, (((0,), (0,)), ((), ())), preferred_element_type=F32)


def split(a):
    hi = a.astype(BF)
    return hi, (a - hi.astype(F32)).astype(BF)


def three(dot, a_hi, a_lo, b_hi, b_lo):
    return dot(a_hi, b_hi) + (dot(a_hi, b_lo) + dot(a_lo, b_hi))


def params(mib):
    return pltpu.CompilerParams(vmem_limit_bytes=mib << 20)


def cost(flops, bytes_accessed, transcendentals=0):
    return pl.CostEstimate(
        flops=flops, bytes_accessed=bytes_accessed, transcendentals=transcendentals
    )


def b16(*shape):
    return jax.ShapeDtypeStruct(shape, BF)


def f32(*shape):
    return jax.ShapeDtypeStruct(shape, F32)


TOKEN = (8, 128)


def call(
    kernel, name, scalars, args, outs, scratch=(), after=(), mib=16, flops=0, moved=0, far_outs=(), last=False, far_args=(),
    aliases=(),
):
    waits = len(after)
    at = waits + len(scalars) + len(args) + len(outs)

    def body(*refs):
        refs[at][...] = jnp.zeros(TOKEN, F32)
        kernel(*refs[waits:at], *refs[at + 1 :])

    place = lambda i, o: o if last else (pltpu.HBM if i in far_outs else pltpu.VMEM)(o.shape, o.dtype)
    space = lambda i: pltpu.HBM if i in far_args else pltpu.VMEM
    near = [a if last else pltpu.with_memory_space_constraint(a, space(i)) for i, a in enumerate(args)]
    return pl.pallas_call(
        body,
        out_shape=tuple(place(i, o) for i, o in enumerate(outs)) + (pltpu.VMEM(TOKEN, F32),),
        in_specs=[ANY] * waits + [SM] * len(scalars) + [HBM if i in far_args else VM for i in range(len(args))],
        out_specs=tuple(HBM if i in far_outs else VM for i in range(len(outs))) + (VM,),
        scratch_shapes=list(scratch),
        compiler_params=params(mib),
        cost_estimate=cost(flops, moved),
        input_output_aliases={waits + len(scalars) + i: o for i, o in aliases},
        name=name,
    )(*after, *scalars, *near)


def gate(arrays, after):
    n = len(arrays)
    outs = tuple(jax.ShapeDtypeStruct(a.shape, a.dtype) for a in arrays)
    return call(lambda *refs: None, "gate", (), arrays, outs, after=after, mib=4, aliases=[(i, i) for i in range(n)])


def call_grid(kernel, name, steps, scalars, args, outs, out_specs, after, mib, moved):
    waits = len(after)
    at = waits + len(scalars) + len(args) + len(outs)

    def body(*refs):
        refs[at][...] = jnp.zeros(TOKEN, F32)
        kernel(*refs[waits:at])

    return pl.pallas_call(
        body,
        out_shape=(*outs, pltpu.VMEM(TOKEN, F32)),
        grid=(steps,),
        in_specs=[ANY] * waits + [SM] * len(scalars) + [VM] * len(args),
        out_specs=(*out_specs, VM),
        compiler_params=params(mib),
        cost_estimate=cost(0, moved),
        name=name,
    )(*after, *scalars, *args)


def sems(n):
    return pltpu.SemaphoreType.DMA((n,))


def vs(*shape, dtype=F32):
    return pltpu.VMEM(shape, dtype)


def tables_kernel(scalars, lengths, near_q, far_q, kst, kf_out):
    j = scalars[0]
    exponent = -math.log(10000.0) / 32

    def positions(shape, size, step):
        row = lax.broadcasted_iota(jnp.int32, shape, 0)
        return step * (((row // size) ^ j) * size + row % size)

    def angles(shape, size, step):
        lane = lax.broadcasted_iota(jnp.int32, shape, 1)
        w = jnp.exp((lane % 32).astype(F32) * exponent)
        return positions(shape, size, step).astype(F32) * w, lane % 64 < 32

    theta, early = angles((256, 128), 64, 2)
    sin, cos = jnp.sin(theta), jnp.cos(theta)
    signed = jnp.where(early, cos, -cos)
    near_q[:, :128] = sin
    near_q[:, 128:] = signed
    far_q[:64] = sin.T[:64]
    far_q[64:] = -signed.T[:64]
    angle, early = angles((512, 128), 128, 1)
    sin, cos = jnp.sin(angle), jnp.cos(angle)
    kf = jnp.where(early, cos, sin)
    lane = lax.broadcasted_iota(jnp.int32, (512, 128), 1)
    kst[...] = jnp.where(lane < 64, kf, jnp.where(early, sin, cos)).astype(BF).T
    place = positions((512, 128), 128, 1)
    for r in range(2):
        bias = jnp.where(place < lengths[scalars[1] + r], 0.0, -1.0e9)
        kf_out[r, 0] = jnp.where(lane < 64, kf, jnp.where(lane == 64, bias, 0.0)).astype(BF)
        kf_out[r, 1] = jnp.where(lane >= 64, kf, jnp.where(lane == 0, bias, 0.0)).astype(BF)


def tables(scalars, lengths, after):
    outs = (f32(256, 256), f32(128, 256), b16(128, 512), b16(2, 2, 512, 128))
    return call(tables_kernel, "tables", (scalars, lengths), (), outs, after=after)


def spread_heads(weight, high, low, sides):
    for g in range(3):
        high[g] = jnp.zeros((256, 256 * sides), BF)
        low[g] = jnp.zeros((256, 256 * sides), BF)
        for a in range(4):
            hi, lo = split(weight[4 * g + a])
            at = slice(64 * a, 64 * a + 64)
            high[g, at, at] = hi
            low[g, at, at] = lo
            if sides == 2:
                there = slice(256 + 64 * a, 256 + 64 * a + 64)
                high[g, at, there] = jnp.concatenate([hi[:, 32:], hi[:, :32]], axis=1)
                low[g, at, there] = jnp.concatenate([lo[:, 32:], lo[:, :32]], axis=1)


def attn_fwd_kernel(
    r,
    x0, x1, x2, x3, wq, wk, wv, vecs, pw, near_q, kf,
    k_far, v_far, kt_far, xt_far, qc_far, qf_far, qht_far, qlt_far, pt_far, pooled_out, ctx_out, ctxt_out, lse_out,
    x_s, vt_s, wph, wpl, k_out, v_out, kt_out, xt_out, qc_out, qf_out, qht_out, qlt_out, pt_out, sem,
):
    copies = []

    def send(here, there):
        copies.append(pltpu.make_async_copy(here, there, sem.at[len(copies)]))
        copies[-1].start()

    qb, cb, pb, vb = (vecs[i : i + 1, :] for i in range(4))
    spread_heads(pw, wph, wpl, 2)
    rows = lax.broadcasted_iota(jnp.int32, (64, 128), 0)
    cols = lax.broadcasted_iota(jnp.int32, (64, 128), 1)
    pair = jnp.where(cols // 2 == rows, 0.5, 0.0).astype(BF)
    for d, piece in enumerate((x0, x1, x2, x3)):
        x_s[d * 128 : d * 128 + 128, :] = piece[...]
        pooled_out[d * 64 : d * 64 + 64, :] = nn(pair, piece[...])
    pooled_low = pooled_out[...].astype(BF)
    pt_out[...] = pooled_low.T
    send(pt_out, pt_far)
    x = x_s[...]
    xt_out[...] = x.T
    send(xt_out, xt_far)
    q = nn(pooled_low, wq[...]) + qb
    k = nn(x, wk[...]).astype(BF)
    k_out[...] = k
    kt_out[...] = k.T
    send(k_out, k_far)
    send(kt_out, kt_far)
    v = (nn(x, wv[...]) + vb).astype(BF)
    v_out[...] = v
    send(v_out, v_far)
    vt_s[...] = v.T
    qc_out[...] = (q + cb).astype(BF) * 0.125
    hi, lo = split(q + pb)
    qht_out[...] = hi.T
    qlt_out[...] = lo.T
    send(qc_out, qc_far)
    send(qht_out, qht_far)
    send(qlt_out, qlt_far)
    sin4 = jnp.concatenate([near_q[:, :128]] * 2, axis=1)
    cos4 = jnp.concatenate([near_q[:, 128:]] * 2, axis=1)
    for g in range(3):
        at = slice(256 * g, 256 * g + 256)
        both = three(nn, hi[:, at], lo[:, at], wph[g], wpl[g])
        side = both[:, :256] * sin4 + both[:, 256:] * cos4
        qf_out[:, at] = side.astype(BF) * 0.125
    send(qf_out, qf_far)
    lane = lax.broadcasted_iota(jnp.int32, (256, 128), 1)
    zero = jnp.zeros((256, 128), BF)
    one_a = (lane == 64).astype(F32).astype(BF)
    one_b = (lane == 0).astype(F32).astype(BF)

    def one_pair(i, carry):
        at = pl.ds(pl.multiple_of(i * 128, 128), 128)
        k_pair = k_out[:, at]
        qc_pair = qc_out[:, at]
        qf_pair = qf_out[:, at]
        for s in range(2):
            mine = (lane < 64) if s == 0 else (lane >= 64)
            left = jnp.concatenate([k_pair, kf[r, s]], axis=1)
            right = jnp.concatenate(
                [jnp.where(mine, qc_pair, zero), jnp.where(mine, qf_pair, (one_a, one_b)[s])], axis=1
            )
            scores = nt(left, right)
            highest = jnp.max(scores, axis=0, keepdims=True)
            raised = jnp.exp(scores - highest)
            total = jnp.sum(raised, axis=0, keepdims=True)
            weights = (raised * (1.0 / total)).astype(BF)
            head = pl.ds(pl.multiple_of(i * 128 + s * 64, 64), 64)
            ctxt_out[head, :] = nn(vt_s[head, :], weights).astype(BF)
            lse_out[i * 2 + s] = highest + jnp.log(total)
        return carry

    lax.fori_loop(0, 6, one_pair, 0)
    ctx_out[...] = ctxt_out[...].T
    for copy in copies:
        copy.wait()


def attn_fwd(r, args, after=()):
    return call(
        functools.partial(attn_fwd_kernel, r), "attn_fwd", (), args,
        (
            b16(512, 768), b16(512, 768), b16(768, 512), b16(768, 512), b16(256, 768), b16(256, 768),
            b16(768, 256), b16(768, 256), b16(768, 256), f32(256, 768), b16(256, 768), b16(768, 256),
            f32(12, 1, 256),
        ),
        (
            vs(512, 768, dtype=BF), vs(768, 512, dtype=BF), vs(3, 256, 512, dtype=BF), vs(3, 256, 512, dtype=BF),
            vs(512, 768, dtype=BF), vs(512, 768, dtype=BF), vs(768, 512, dtype=BF), vs(768, 512, dtype=BF),
            vs(256, 768, dtype=BF), vs(256, 768, dtype=BF), vs(768, 256, dtype=BF), vs(768, 256, dtype=BF),
            vs(768, 256, dtype=BF), sems(9),
        ),
        after, mib=20, far_outs=range(9), flops=4 * 10**9, moved=12 * 10**6,
    )


def layer_stats(a):
    center = a - jnp.mean(a, axis=-1, keepdims=True)
    rs = lax.rsqrt(jnp.mean(center * center, axis=-1, keepdims=True) + 1e-05)
    return center * rs, rs


def layer_back(dn, n, rs):
    return rs * (dn - jnp.mean(dn, axis=-1, keepdims=True) - n * jnp.mean(dn * n, axis=-1, keepdims=True))


def put_blocks(source, near, far, me, slabs, first):
    for r in range(16):
        for half, out in enumerate((near, far)):
            place = (r ^ me) ^ (16 * half)
            row = pl.multiple_of((place // 2) * 48, 16)
            col = pl.multiple_of((place % 2) * 384, 128)
            for to, s in slabs:
                at = pl.ds(row + (s // 9 * 768 + s % 9 // 3 * 16), 16)
                out[r, first + to] = source[at, pl.ds(col + s % 3 * 128, 128)].astype(BF)


def ffn_down_kernel(
    masks, ctx0, ctx1, pooled0, pooled1, c0, c1, c2, c3, wo, wu, wd, vecs, ub,
    out0, out1, out23, d2_out, df_out, x1t_out, n1_out, rs_out, gp_out, near, far, vec_out,
    act_s, acc_s, x1_s, g_s,
):
    def chunk(c):
        return pl.ds(pl.multiple_of(c * CH, CH), CH)

    ob, ig, ish, db, og, osh = (vecs[i : i + 1, :] for i in range(4, 10))
    ctx = jnp.concatenate([ctx0[...], ctx1[...]], axis=0)
    pooled = jnp.concatenate([pooled0[...], pooled1[...]], axis=0)
    n1, rs1 = layer_stats(pooled + (nn(ctx, wo[...]) + ob))
    n1_out[...] = n1
    rs_out[...] = rs1
    x1 = n1 * ig + ish
    x1_s[...] = x1.astype(BF)
    x1t_out[...] = x1.astype(BF).T
    acc_s[...] = x1 + db

    def up_chunk(c, carry):
        at = chunk(c)
        z = nn(x1_s[...], wu[:, at]) + ub[:, at]
        phi = 0.5 + 0.5 * lax.erf(z * math.sqrt(0.5))
        gp_out[:, at] = phi + z * (jnp.exp(-0.5 * z * z) * (1.0 / math.sqrt(2.0 * math.pi)))
        act = (z * phi).astype(BF)
        act_s[:, at] = act
        acc_s[...] += nn(act, wd[at, :])
        return carry

    lax.fori_loop(0, 6, up_chunk, 0)
    n2, rs2 = layer_stats(acc_s[...])
    result = (n2 * og + osh).astype(BF)
    for d, out in enumerate((out0, out1, out23.at[0], out23.at[1])):
        for r in range(2):
            out[r] = result[r * 256 + d * 64 : r * 256 + d * 64 + 64, :]
    cot = jnp.concatenate([c[r] for r in range(2) for c in (c0, c1, c2, c3)], axis=0).astype(F32)
    vec_out[0:1, :] = jnp.sum(cot * n2, axis=0, keepdims=True)
    vec_out[1:2, :] = jnp.sum(cot, axis=0, keepdims=True)
    d2 = layer_back(cot * og, n2, rs2)
    df = d2.astype(BF)
    df_out[...] = df
    vec_out[2:3, :] = jnp.sum(df.astype(F32), axis=0, keepdims=True)
    d2_out[...] = d2

    def down_chunk(which, i, carry):
        c = which * 3 + i
        g_s[...] = tn(act_s[:, chunk(c)], df_out[...])
        slab = c * 6
        me = masks[2 + which]
        for r in range(32):
            row = pl.ds(pl.multiple_of((r ^ me) * 16, 16), 16)
            for j in range(6):
                (near, far)[r // 16][r % 16, slab + j] = g_s[row, j * 128 : j * 128 + 128].astype(BF)
        return carry

    for which in range(2):
        lax.fori_loop(0, 3, functools.partial(down_chunk, which), 0)


def ffn_down(masks, args, after=()):
    grad = b16(16, 36, 16, 128)
    return call(
        ffn_down_kernel, "ffn_down", (masks,), args,
        (
            b16(2, 64, 768), b16(2, 64, 768), b16(2, 2, 64, 768), f32(512, 768), b16(512, 768),
            b16(768, 512), f32(512, 768), f32(512, 1), f32(512, 3072), grad, grad, f32(8, 768),
        ),
        (vs(512, 3072, dtype=BF), vs(512, 768), vs(512, 768, dtype=BF), vs(512, 768)),
        after, mib=18, flops=8 * 10**9, moved=25 * 10**6,
    )


def hidden_back(masks, which, df_in, gp, x1t, wu, wd, near, far, upb_out, acc_s, u_s):
    me = masks[2 + which]

    def up_chunk(i, carry):
        at = pl.ds(pl.multiple_of((which * 3 + i) * CH, CH), CH)
        dz = (nt(df_in[...], wd[at, :]) * gp[:, at]).astype(BF)
        upb_out[:, pl.ds(pl.multiple_of(i * CH, CH), CH)] = jnp.sum(dz.astype(F32), axis=0, keepdims=True)
        acc_s[...] += nt(dz, wu[:, at])
        u_s[...] = nn(x1t[...], dz)
        slab = (which * 3 + i) * 6
        for r in range(32):
            place = r ^ me
            row = pl.multiple_of((place // 4) * 96, 32)
            col = pl.ds(pl.multiple_of((place % 4) * 128, 128), 128)
            for j in range(6):
                (near, far)[r // 16][r % 16, slab + j] = u_s[pl.ds(row + 16 * j, 16), col].astype(BF)
        return carry

    lax.fori_loop(0, 3, up_chunk, 0)


def ffn_up_a_kernel(masks, df_in, d2, gp, x1t, wu, wd, acc, near, far, upb_out, u_s):
    acc[...] = d2[...]
    hidden_back(masks, 0, df_in, gp, x1t, wu, wd, near, far, upb_out, acc, u_s)


def ffn_up_a(masks, args, after=()):
    return call(
        ffn_up_a_kernel, "ffn_up_a", (masks,), args,
        (f32(512, 768), b16(16, 45, 16, 128), b16(16, 45, 16, 128), f32(1, 1536)),
        (vs(768, 512),), after, mib=14, flops=4 * 10**9, moved=12 * 10**6,
    )


def ffn_up_b_kernel(
    masks, df_in, acc, gp, x1t, n1, rs, ctxt0, ctxt1, wo, wu, wd, vecs, near_in, far_in,
    d1_out, dctx_out, near, far, vec_out, upb_out,
    acc_s, u_s, o_s,
):
    ig = vecs[5:6, :]
    acc_s[...] = acc[...]
    hidden_back(masks, 1, df_in, gp, x1t, wu, wd, near, far, upb_out, acc_s, u_s)
    dx1 = acc_s[...]
    vec_out[0:1, :] = jnp.sum(dx1 * n1[...], axis=0, keepdims=True)
    vec_out[1:2, :] = jnp.sum(dx1, axis=0, keepdims=True)
    d1 = layer_back(dx1 * ig, n1[...], rs[...])
    d1_out[...] = d1
    do = d1.astype(BF)
    vec_out[2:3, :] = jnp.sum(do.astype(F32), axis=0, keepdims=True)
    dctx = nt(do, wo[...]).astype(BF)
    for r in range(2):
        dctx_out[r] = dctx[r * 256 : r * 256 + 256]
    o_s[...] = nn(ctxt0[...], do[:256]) + nn(ctxt1[...], do[256:])
    put_blocks(o_s, near, far, masks[3], [(i, i) for i in range(9)], 36)


def ffn_up_b(masks, args, after=()):
    return call(
        ffn_up_b_kernel, "ffn_up_b", (masks,), args,
        (f32(512, 768), b16(2, 256, 768), b16(16, 45, 16, 128), b16(16, 45, 16, 128), f32(8, 768), f32(1, 1536)),
        (vs(512, 768), vs(768, 512), vs(768, 768)),
        after, mib=16, flops=5 * 10**9, moved=14 * 10**6, aliases=((12, 2), (13, 3)),
    )


def attn_bwd_kernel(
    r,
    k, v, kt, qc, qf, qht, qlt, lse, dctx, kf, kst, far_q, pw,
    dk_out, dv_out, dq_out, pwg_out, vec_out,
    dqct_s, dpt_s, wph, wpl,
):
    spread_heads(pw, wph, wpl, 1)
    lane = lax.broadcasted_iota(jnp.int32, (256, 128), 1)
    zero = jnp.zeros((256, 128), BF)
    one_a = (lane == 64).astype(F32).astype(BF)
    one_b = (lane == 0).astype(F32).astype(BF)

    def one_pair(i, carry):
        at = pl.ds(pl.multiple_of(i * 128, 128), 128)
        k_pair = k[:, at]
        v_pair = v[:, at]
        qc_pair = qc[:, at]
        qf_pair = qf[:, at]
        dc_pair = dctx[r, :, at]
        for s in range(2):
            mine = (lane < 64) if s == 0 else (lane >= 64)
            left = jnp.concatenate([k_pair, kf[r, s]], axis=1)
            qc_mine = jnp.where(mine, qc_pair, zero)
            dc_mine = jnp.where(mine, dc_pair, zero)
            right = jnp.concatenate([qc_mine, jnp.where(mine, qf_pair, (one_a, one_b)[s])], axis=1)
            weights = jnp.exp(nt(left, right) - lse[i * 2 + s])
            dweights = nt(v_pair, dc_mine)
            inner = jnp.sum(weights * dweights, axis=0, keepdims=True)
            dscore = (weights * (dweights - inner)).astype(BF)
            dv_part = nn(weights.astype(BF), dc_mine)
            dk_part = nn(dscore, qc_mine)
            if s == 0:
                dv_first, dk_first = dv_part, dk_part
            head = pl.ds(pl.multiple_of(i * 128 + s * 64, 64), 64)
            side = nn(jnp.concatenate([kt[head, :], kst[...]], axis=0), dscore)
            dqct_s[head, :] = side[0:64] * 0.125
            dpt_s[head, :] = (side[64:128] * far_q[:64] + side[128:192] * far_q[64:]) * 0.125
        dv_out[:, at] = (dv_first + dv_part).astype(BF)
        dk_out[:, at] = (dk_first + dk_part).astype(BF)
        return carry

    lax.fori_loop(0, 6, one_pair, 0)
    ones = jnp.ones((8, 256), BF)
    for g in range(3):
        at = slice(256 * g, 256 * g + 256)
        hi, lo = split(dpt_s[at, :])
        pwg = three(nt, qht[at, :], qlt[at, :], hi, lo)
        early = lax.broadcasted_iota(jnp.int32, (64, 128), 1) < 64
        for i in range(2):
            m = 128 * i
            mixed = jnp.where(early, pwg[m : m + 64, m : m + 128], pwg[m + 64 : m + 128, m : m + 128])
            pwg_out[(2 * g + i) * 64 : (2 * g + i) * 64 + 64, :] = mixed
        shift = three(nn, wph[g], wpl[g], hi, lo)
        content = dqct_s[at, :]
        dq = (content + shift).T.astype(BF)
        dq_out[:, at] = dq
        shi, slo = split(shift)
        chi, clo = split(content)
        vec_out[0:1, at] = (nt(ones, chi) + nt(ones, clo))[0:1]
        vec_out[1:2, at] = (nt(ones, shi) + nt(ones, slo))[0:1]
        vec_out[2:3, at] = jnp.sum(dq.astype(F32), axis=0, keepdims=True)
    vec_out[3:4, :] = jnp.sum(dv_out[...].astype(F32), axis=0, keepdims=True)


def attn_bwd(r, args, after=()):
    return call(
        functools.partial(attn_bwd_kernel, r), "attn_bwd", (), args,
        (b16(512, 768), b16(512, 768), b16(256, 768), f32(384, 128), f32(8, 768)),
        (vs(768, 256), vs(768, 256), vs(3, 256, 256, dtype=BF), vs(3, 256, 256, dtype=BF)),
        after, mib=14, flops=8 * 10**9, moved=12 * 10**6,
    )


def tokens_back_kernel(dk0, dk1, dv0, dv1, dq0, dq1, d1, wq, wk, wv, t0, t1, t23, tok_s):
    rows = lax.broadcasted_iota(jnp.int32, (512, 256), 0)
    cols = lax.broadcasted_iota(jnp.int32, (512, 256), 1)
    spread = jnp.where(rows // 2 == cols, 0.5, 0.0).astype(BF)
    for r, (dk, dv, dq) in enumerate(((dk0, dv0, dq0), (dk1, dv1, dq1))):
        hi, lo = split(d1[r * 256 : r * 256 + 256, :] + nt(dq[...], wq[...]))
        tok_s[...] = (nt(dk[...], wk[...]) + nt(dv[...], wv[...])) + (nn(spread, hi) + nn(spread, lo))
        for d, out in enumerate((t0, t1, t23.at[0], t23.at[1])):
            out[r] = tok_s[d * 128 : d * 128 + 128, :].astype(BF)


def weights_back_kernel(
    masks, xt0, xt1, pt0, pt1, dk0, dk1, dv0, dv1, dq0, dq1, pwg0, pwg1, av0, av1, vec_d, vec_u, upb_a, upb_b,
    near, far, g_s, smalls,
):
    smalls[0:384, :] = pwg0[...] + pwg1[...]
    attn = av0[...] + av1[...]
    lines = [vec_d[i : i + 1, :] for i in range(3)] + [vec_u[i : i + 1, :] for i in range(3)]
    lines += [upb[:, 768 * i : 768 * i + 768] for upb in (upb_a, upb_b) for i in range(2)] + [attn[i : i + 1, :] for i in range(4)]
    for i, line in enumerate(lines):
        for t in range(6):
            row = 384 + 6 * i + t
            smalls[row : row + 1, :] = line[:, 128 * t : 128 * t + 128]
    smalls[468:512, :] = jnp.zeros((44, 128), F32)
    g_s[0:768, :] = nn(pt0[...], dq0[...]) + nn(pt1[...], dq1[...])
    g_s[768:1536, :] = nn(xt0[...], dk0[...]) + nn(xt1[...], dk1[...])
    g_s[1536:2304, :] = nn(xt0[...], dv0[...]) + nn(xt1[...], dv1[...])
    put_blocks(g_s, near, far, masks[2], [(i, i) for i in range(NA)], 0)
    put_blocks(g_s, near, far, masks[3], [(i, i) for i in range(NA, 27)], 0)
    for r in range(16):
        for half, out in enumerate((near, far)):
            row = pl.ds(pl.multiple_of((r ^ masks[3] ^ (16 * half)) * 16, 16), 16)
            out[r, 27] = smalls[row, :].astype(BF)


def last_back_kernel(
    scalars, k, v, kt, qc, qf, qht, qlt, lse, dctx, kf, kst, far_q, pw, xt0, xt1, pt0, pt1, dk0, dv0, dq0, pwg0, av0, vec_d,
    vec_u, upb_a, upb_b, d1, wq, wk, wv,
    near, far, t0, t1, t23,
    dqct_s, dpt_s, wph, wpl, dk1, dv1, dq1, pwg1, av1, g_s, smalls, tok_s,
):
    attn_bwd_kernel(
        1, k, v, kt, qc, qf, qht, qlt, lse, dctx, kf, kst, far_q, pw, dk1, dv1, dq1, pwg1, av1, dqct_s, dpt_s, wph, wpl
    )
    weights_back_kernel(
        scalars, xt0, xt1, pt0, pt1, dk0, dk1, dv0, dv1, dq0, dq1, pwg0, pwg1, av0, av1, vec_d, vec_u, upb_a, upb_b, near, far,
        g_s, smalls,
    )
    tokens_back_kernel(dk0, dk1, dv0, dv1, dq0, dq1, d1, wq, wk, wv, t0, t1, t23, tok_s)


def last_back(scalars, args, after=()):
    grad = b16(16, 28, 16, 128)
    return call(
        last_back_kernel, "last_back", (scalars,), args,
        (grad, grad, b16(2, 128, 768), b16(2, 128, 768), b16(2, 2, 128, 768)),
        (
            vs(768, 256), vs(768, 256), vs(3, 256, 256, dtype=BF), vs(3, 256, 256, dtype=BF), vs(512, 768, dtype=BF),
            vs(512, 768, dtype=BF), vs(256, 768, dtype=BF), vs(384, 128), vs(8, 768), vs(2304, 768), vs(512, 128),
            vs(512, 768),
        ),
        after, mib=28, flops=17 * 10**9, moved=30 * 10**6,
    )


def partner(x, bit):
    size = lax.axis_size("batch")
    return lax.ppermute(x, "batch", [(i, i ^ bit) for i in range(size)])


def add_kernel(step, cuts, parts, *refs):
    here, came, outs = refs[:parts], refs[parts : 2 * parts], refs[2 * parts :]
    if step < 5:
        pieces = 2 if step < 4 else 1
        at = 0
        for p in range(parts):
            rows, slabs = here[p].shape[:2]
            half = rows // pieces

            def add(r, carry, p=p, at=at, half=half, slabs=slabs):
                for h in range(pieces):
                    total = (here[p][h * half + r].astype(F32) + came[p][h * half + r].astype(F32)).astype(BF)
                    if len(outs) == pieces:
                        outs[h][r, at : at + slabs] = total
                    elif parts == 2:
                        outs[pieces * p + h][r] = total
                    else:
                        outs[h][r] = total[:cuts]
                        outs[pieces + h][r] = total[cuts:]
                return carry

            lax.fori_loop(0, half, add, 0)
            at += slabs
    else:
        at = 0
        for p in range(parts):
            rows, slabs = here[p].shape[:2]
            for source, to in ((here[p], slice(0, rows)), (came[p], slice(rows, 2 * rows))):
                if len(outs) == 1:
                    outs[0][to, at : at + slabs] = source[...]
                elif parts == 2:
                    outs[p][to] = source[...]
                else:
                    outs[0][to] = source[:, :cuts]
                    outs[1][to] = source[:, cuts:]
            at += slabs


class Order:
    def __init__(self):
        self.last = ()

    def run(self, function, *args, also=()):
        *results, token = function(*args, (*self.last, *also))
        self.last = (token,)
        return results


class Sum:
    def __init__(self, order, keep, sends, cuts, bits):
        core, first, second, third, fourth, self.others = bits
        self.bits = [(core,) * len(keep), (first, second), (second, first), (third,), (fourth,)]
        self.bits += [(fourth,), (third,), (second, first), (first, second), (core,)]
        self.cuts, self.slabs = cuts, sum(k.shape[1] for k in keep)
        self.order, self.keep, self.sends, self.step = order, keep, sends, 0

    def start(self):
        self.got = [partner(s, b) for s, b in zip(self.sends, self.bits[self.step])]
        return self

    def finish(self):
        step, a, b = self.step, self.cuts, self.slabs - self.cuts
        here = self.keep if step < 5 else self.sends
        if step < 9:
            rows = (8, 4, 2, 1, 1, 2, 4, 8, 16)[step]
            shapes = [(a,), (b,)] if step in (0, 1, 6, 7) else [(a + b,)]
            copies = 2 if step < 4 else 1
            outs = [b16(rows, *s, 16, 128) for s in shapes for _ in range(copies)]

            def add(after):
                return call(
                    functools.partial(add_kernel, step, a, len(here)), "sum_step", (), (*here, *self.got), outs,
                    after=after, mib=8, moved=10**6,
                )

            outs = self.order.run(add)
            if step < 4:
                self.keep, self.sends = outs[::2], outs[1::2]
            else:
                self.sends = outs
            if step == 4:
                for bit in self.others:
                    self.sends = [(s.astype(F32) + partner(s, bit).astype(F32)).astype(BF) for s in self.sends]
        else:
            self.sends = (*self.sends, *self.got)
        self.step += 1
        return self


def get_blocks(me, halves, slabs, outs):
    for half, source in enumerate(halves):
        for r in range(16):
            place = (r ^ me) ^ (16 * half)
            row = pl.multiple_of((place // 2) * 48, 16)
            col = pl.multiple_of((place % 2) * 384, 128)
            for at, s in slabs:
                to = pl.ds(row + s % 9 // 3 * 16, 16)
                outs[s // 9][to, pl.ds(col + s % 3 * 128, 128)] = source[r, at].astype(F32)


def rows_kernel(masks, near, far, out):
    c = pl.program_id(0)
    me = masks[2 + c // 3]
    for r in range(32):
        row = pl.ds(pl.multiple_of((r ^ me) * 16, 16), 16)
        for j in range(6):
            out[row, j * 128 : j * 128 + 128] = (near, far)[r // 16][r % 16, c * 6 + j].astype(F32)


def assemble_rows(masks, halves, after=()):
    return call_grid(
        rows_kernel, "assemble_rows", 6, (masks,), halves, (f32(3072, 768),), (pl.BlockSpec((512, 768), lambda c: (c, 0)),),
        after, 24, 14 * 10**6,
    )


def up_kernel(masks, near, far, out, o_out):
    c = pl.program_id(0)
    me = masks[2 + c // 3]
    for r in range(32):
        place = r ^ me
        row = pl.multiple_of((place // 4) * 96, 32)
        col = pl.ds(pl.multiple_of((place % 4) * 128, 128), 128)
        for j in range(6):
            out[pl.ds(row + 16 * j, 16), col] = (near, far)[r // 16][r % 16, c * 6 + j].astype(F32)

    @pl.when(c == 0)
    def _():
        get_blocks(masks[3], (near, far), [(36 + i, i) for i in range(9)], (o_out,))


def assemble_up(masks, halves, after=()):
    return call_grid(
        up_kernel, "assemble_up", 6, (masks,), halves, (f32(768, 3072), f32(768, 768)),
        (pl.BlockSpec((768, 512), lambda c: (0, c)), VM), after, 28, 18 * 10**6,
    )


def three_kernel(masks, near, far, q_out, k_out, v_out, w_out, l_out, s_out):
    outs = (q_out, k_out, v_out)
    get_blocks(masks[2], (near, far), [(i, i) for i in range(NA)], outs)
    get_blocks(masks[3], (near, far), [(i, i) for i in range(NA, 27)], outs)
    for half, source in enumerate((near, far)):
        for r in range(16):
            row = pl.ds(pl.multiple_of((r ^ masks[3] ^ (16 * half)) * 16, 16), 16)
            s_out[row, :] = source[r, 27].astype(F32)
    for h in range(12):
        w_out[h] = s_out[h // 2 * 64 : h // 2 * 64 + 64, h % 2 * 64 : h % 2 * 64 + 64]
    for i in range(14):
        for t in range(6):
            row = 384 + 6 * i + t
            l_out[i : i + 1, 128 * t : 128 * t + 128] = s_out[row : row + 1, :]


def assemble_three(masks, halves, after=()):
    return call(
        three_kernel, "assemble_three", (masks,), halves, (f32(768, 768),) * 3 + (f32(12, 64, 64), f32(16, 768)),
        (vs(512, 128),), after, mib=36, moved=11 * 10**6, last=True,
    )


def owners_kernel(scalars, p0, p2, p13, out):
    j = scalars[0]
    out[j] = p0[...].astype(out.dtype)
    out[j ^ 2] = p2[0].astype(out.dtype)
    out[j ^ 1] = p13[0].astype(out.dtype)
    out[j ^ 3] = p13[1].astype(out.dtype)


def assemble_owners(name, dtype, scalars, pieces, after=()):
    shape = (4, *pieces[0].shape)
    return call(
        owners_kernel, name, (scalars,), pieces, (jax.ShapeDtypeStruct(shape, dtype),), after=after, moved=5 * 10**6,
        last=True,
    )


def join_pieces(own, came, after=()):
    def kernel(a, b, out):
        out[0] = a[...]
        out[1] = b[1]

    return call(kernel, "join", (), (own, came), (jax.ShapeDtypeStruct(came.shape, came.dtype),), after=after, moved=10**6)


def pick_kernel(row, scalars, blocks, o0, o1, o2, o3, sem):
    copies = []
    for d, out in enumerate((o0, o1, o2, o3)):
        source = blocks.at[scalars[0] ^ d] if row is None else blocks.at[scalars[0] ^ d, row]
        copies.append(pltpu.make_async_copy(source, out, sem.at[d]))
        copies[-1].start()
    for copy in copies:
        copy.wait()


def pick(row, scalars, blocks, after=()):
    shape = blocks.shape[1:] if row is None else blocks.shape[2:]
    return call(
        functools.partial(pick_kernel, row), "pick", (scalars,), (blocks,), (b16(*shape),) * 4, (sems(4),), after=after,
        mib=4, moved=2 * 10**6, far_args=(0,),
    )


def on_device(
    tokens, lengths, cotangent, query_weight, query_bias, key_weight, value_weight, value_bias, content_bias,
    position_bias, position_weight, out_weight, out_bias, inner_gain, inner_shift, up_weight, up_bias, down_weight,
    down_bias, outer_gain, outer_shift,
):
    size = lax.axis_size("batch")
    me = lax.axis_index("batch").astype(jnp.int32)
    j = me % G
    core, first, second, third, fourth = 1, 2, 4, 8, 16
    others = [1 << b for b in range(5, size.bit_length() - 1)]
    bits = (core, first, second, third, fourth, others)
    has = lambda bit: (me // bit) % 2
    low = has(core) * 16 + has(third) * 2 + has(fourth)
    scalars = jnp.stack(
        [j, me // G * 8 + 2 * j, low + has(first) * 8 + has(second) * 4, low + has(second) * 8 + has(first) * 4]
    )
    order = Order()

    by_owner = tokens[0].reshape(4, 2, 128, 768)
    cot_owner = cotangent[0].reshape(4, 2, 64, 768)

    def trade(pieces):
        return [pieces[0]] + [partner(pieces[d], d) for d in (1, 2, 3)]

    x0 = trade(order.run(pick, 0, scalars, by_owner))
    near_q, far_q, kst, kf = order.run(tables, scalars, lengths)
    vecs = jnp.stack(
        [
            query_bias, content_bias, position_bias, value_bias, out_bias, inner_gain, inner_shift, down_bias,
            outer_gain, outer_shift,
        ]
    )
    s1 = order.run(pick, 1, scalars, by_owner)
    sc = order.run(pick, None, scalars, cot_owner)
    x1 = trade(order.run(gate, s1, also=x0[1:]))

    def forward(r, x):
        return order.run(
            attn_fwd, r, (*x, query_weight, key_weight, value_weight, vecs, position_weight, near_q, kf)
        )

    fwd = [forward(0, x0)]
    cot = trade(order.run(gate, sc, also=x1[1:]))
    fwd.append(forward(1, x1))
    k, v, kt, xt, qc, qf, qht, qlt, pt, pooled, ctx, ctxt, lse = zip(*fwd)
    outs = order.run(
        ffn_down, scalars, (*ctx, *pooled, *cot, out_weight, up_weight, down_weight, vecs, up_bias[None, :])
    )
    out0, out1, out23, d2, df, x1t, n1, rs1, gp, near, far, vec_d = outs
    far, out23 = order.run(gate, (far, out23))
    down = Sum(order, (near,), (far,), 18, bits).start()
    back23 = partner(out23, 2)
    acc, near, far, upb_a = order.run(ffn_up_a, scalars, (df, d2, gp, x1t, up_weight, down_weight))
    down.finish().start()
    (out13,) = order.run(join_pieces, out1, back23)
    back13 = partner(out13, 1)
    d1, dctx, near, far, vec_u, upb_b = order.run(
        ffn_up_b, scalars, (df, acc, gp, x1t, n1, rs1, *ctxt, out_weight, up_weight, down_weight, vecs, near, far)
    )
    down.finish().start()
    (far,) = order.run(gate, (far,))
    up = Sum(order, (near,), (far,), 18, bits).start()

    def backward(r):
        return k[r], v[r], kt[r], qc[r], qf[r], qht[r], qlt[r], lse[r], dctx, kf, kst, far_q, position_weight

    dk, dv, dq, pwg, attn_vec = order.run(attn_bwd, 0, backward(0))
    down.finish().start()
    up.finish().start()
    near, far, t0, t1, t23 = order.run(
        last_back, scalars,
        (
            *backward(1), *xt, *pt, dk, dv, dq, pwg, attn_vec, vec_d, vec_u, upb_a, upb_b, d1, query_weight, key_weight,
            value_weight,
        ),
    )
    up.finish().start()
    down.finish().start()
    (far,) = order.run(gate, (far,))
    three = Sum(order, (near,), (far,), NA, bits).start()
    layer_output = order.run(assemble_owners, "layer_output", BF, scalars, (out0, back23, back13))[0]
    three.finish().start()
    down.finish().start()
    up.finish().start()
    down.finish().start()
    (t23,) = order.run(gate, (t23,))
    u23 = partner(t23, 2)
    three.finish().start()
    up.finish().start()
    three.finish().start()
    down.finish().start()
    up.finish().start()
    three.finish().start()
    up.finish().start()
    down.finish().start()
    three.finish().start()
    u13 = partner(order.run(join_pieces, t1, u23)[0], 1)
    up.finish().start()
    three.finish().start()
    down.finish().start()
    up.finish().start()
    three.finish().start()
    down.finish()
    down_weight_grad = order.run(assemble_rows, scalars, down.sends)[0]
    tokens_grad = order.run(assemble_owners, "tokens_grad", F32, scalars, (t0, u23, u13))[0]
    three.finish().start()
    up.finish().start()
    three.finish().start()
    up.finish()
    up_weight_grad, out_weight_grad = order.run(assemble_up, scalars, up.sends)
    three.finish()
    query_weight_grad, key_weight_grad, value_weight_grad, position_weight_grad, lines = order.run(
        assemble_three, scalars, three.sends
    )
    layer_output = layer_output.reshape(1, 8, 64, 768)
    tokens_grad = tokens_grad.reshape(1, 8, 128, 768)
    line = lambda i: lines[i]
    return (
        layer_output, tokens_grad, query_weight_grad, line(12), key_weight_grad, value_weight_grad, line(13), line(10),
        line(11), position_weight_grad, out_weight_grad, line(5), line(3), line(4),
        up_weight_grad, lines[6:10].reshape(3072), down_weight_grad, line(2), line(0), line(1),
    )


def solution(mesh):
    in_specs = (P("batch", None, None, None), P(), P("batch", None, None, None)) + (P(),) * 18
    out_specs = (P("batch", None, None, None),) * 2 + (P(),) * 18
    return jax.shard_map(on_device, mesh=mesh, in_specs=in_specs, out_specs=out_specs, check_vma=False)
```

```python
import functools
import math

import jax
import jax.numpy as jnp
from jax import lax
from jax.experimental import pallas as pl
from jax.experimental.pallas import tpu as pltpu
from jax.sharding import PartitionSpec as P

G = 4
F32 = jnp.float32
BF = jnp.bfloat16
VM = pl.BlockSpec(memory_space=pltpu.VMEM)
SM = pl.BlockSpec(memory_space=pltpu.SMEM)
ANY = pl.BlockSpec(memory_space=pl.ANY)
HBM = pl.BlockSpec(memory_space=pltpu.HBM)
BLK = 16
NA = 12
CH = 512


def nn(a, b):
    return lax.dot_general(a, b, (((1,), (0,)), ((), ())), preferred_element_type=F32)


def nt(a, b):
    return lax.dot_general(a, b, (((1,), (1,)), ((), ())), preferred_element_type=F32)


def tn(a, b):
    return lax.dot_general(a, b, (((0,), (0,)), ((), ())), preferred_element_type=F32)


def split(a):
    hi = a.astype(BF)
    return hi, (a - hi.astype(F32)).astype(BF)


def three(dot, a_hi, a_lo, b_hi, b_lo):
    return dot(a_hi, b_hi) + (dot(a_hi, b_lo) + dot(a_lo, b_hi))


def params(mib):
    return pltpu.CompilerParams(vmem_limit_bytes=mib << 20)


def cost(flops, bytes_accessed, transcendentals=0):
    return pl.CostEstimate(
        flops=flops, bytes_accessed=bytes_accessed, transcendentals=transcendentals
    )


def b16(*shape):
    return jax.ShapeDtypeStruct(shape, BF)


def f32(*shape):
    return jax.ShapeDtypeStruct(shape, F32)


TOKEN = (8, 128)


def call(
    kernel, name, scalars, args, outs, scratch=(), after=(), mib=16, flops=0, moved=0, far_outs=(), last=False, far_args=(),
    aliases=(), free=(),
):
    waits = len(after)
    at = waits + len(scalars) + len(args) + len(outs)

    def body(*refs):
        refs[at][...] = jnp.zeros(TOKEN, F32)
        kernel(*refs[waits:at], *refs[at + 1 :])

    place = lambda i, o: o if last else (pltpu.HBM if i in far_outs else pltpu.VMEM)(o.shape, o.dtype)
    space = lambda i: pltpu.HBM if i in far_args else pltpu.VMEM
    near = [a if last or i in free else pltpu.with_memory_space_constraint(a, space(i)) for i, a in enumerate(args)]
    return pl.pallas_call(
        body,
        out_shape=tuple(place(i, o) for i, o in enumerate(outs)) + (pltpu.VMEM(TOKEN, F32),),
        in_specs=[ANY] * waits + [SM] * len(scalars) + [HBM if i in far_args else VM for i in range(len(args))],
        out_specs=tuple(HBM if i in far_outs else VM for i in range(len(outs))) + (VM,),
        scratch_shapes=list(scratch),
        compiler_params=params(mib),
        cost_estimate=cost(flops, moved),
        input_output_aliases={waits + len(scalars) + i: o for i, o in aliases},
        name=name,
    )(*after, *scalars, *near)


def gate(arrays, after):
    n = len(arrays)
    outs = tuple(jax.ShapeDtypeStruct(a.shape, a.dtype) for a in arrays)
    return call(lambda *refs: None, "gate", (), arrays, outs, after=after, mib=4, aliases=[(i, i) for i in range(n)])


def call_grid(kernel, name, steps, scalars, args, outs, out_specs, after, mib, moved):
    waits = len(after)
    at = waits + len(scalars) + len(args) + len(outs)

    def body(*refs):
        refs[at][...] = jnp.zeros(TOKEN, F32)
        kernel(*refs[waits:at])

    return pl.pallas_call(
        body,
        out_shape=(*outs, pltpu.VMEM(TOKEN, F32)),
        grid=(steps,),
        in_specs=[ANY] * waits + [SM] * len(scalars) + [VM] * len(args),
        out_specs=(*out_specs, VM),
        compiler_params=params(mib),
        cost_estimate=cost(0, moved),
        name=name,
    )(*after, *scalars, *args)


def sems(n):
    return pltpu.SemaphoreType.DMA((n,))


def vs(*shape, dtype=F32):
    return pltpu.VMEM(shape, dtype)


def tables_kernel(count, scalars, lengths, *refs):
    lines, (near_q, far_q, kst, kf_out, vecs) = refs[:10], refs[count:]
    for i, line in enumerate(lines):
        vecs[i : i + 1, :] = line[...].reshape(1, 768)
    j = scalars[0]
    exponent = -math.log(10000.0) / 32

    def positions(shape, size, step):
        row = lax.broadcasted_iota(jnp.int32, shape, 0)
        return step * (((row // size) ^ j) * size + row % size)

    def angles(shape, size, step):
        lane = lax.broadcasted_iota(jnp.int32, shape, 1)
        w = jnp.exp((lane % 32).astype(F32) * exponent)
        return positions(shape, size, step).astype(F32) * w, lane % 64 < 32

    theta, early = angles((256, 128), 64, 2)
    sin, cos = jnp.sin(theta), jnp.cos(theta)
    signed = jnp.where(early, cos, -cos)
    near_q[:, :128] = sin
    near_q[:, 128:] = signed
    far_q[:64] = sin.T[:64]
    far_q[64:] = -signed.T[:64]
    angle, early = angles((512, 128), 128, 1)
    sin, cos = jnp.sin(angle), jnp.cos(angle)
    kf = jnp.where(early, cos, sin)
    lane = lax.broadcasted_iota(jnp.int32, (512, 128), 1)
    kst[...] = jnp.where(lane < 64, kf, jnp.where(early, sin, cos)).astype(BF).T
    place = positions((512, 128), 128, 1)
    for r in range(2):
        bias = jnp.where(place < lengths[scalars[1] + r], 0.0, -1.0e9)
        kf_out[r, 0] = jnp.where(lane < 64, kf, jnp.where(lane == 64, bias, 0.0)).astype(BF)
        kf_out[r, 1] = jnp.where(lane >= 64, kf, jnp.where(lane == 0, bias, 0.0)).astype(BF)


def tables(scalars, lengths, lines, weights, after):
    outs = (f32(256, 256), f32(128, 256), b16(128, 512), b16(2, 2, 512, 128), f32(10, 768))
    kernel = functools.partial(tables_kernel, 10 + len(weights))
    return call(kernel, "tables", (scalars, lengths), (*lines, *weights), outs, after=after, free=range(10))


def spread_heads(weight, high, low, sides):
    for g in range(3):
        high[g] = jnp.zeros((256, 256 * sides), BF)
        low[g] = jnp.zeros((256, 256 * sides), BF)
        for a in range(4):
            hi, lo = split(weight[4 * g + a])
            at = slice(64 * a, 64 * a + 64)
            high[g, at, at] = hi
            low[g, at, at] = lo
            if sides == 2:
                there = slice(256 + 64 * a, 256 + 64 * a + 64)
                high[g, at, there] = jnp.concatenate([hi[:, 32:], hi[:, :32]], axis=1)
                low[g, at, there] = jnp.concatenate([lo[:, 32:], lo[:, :32]], axis=1)


def attn_fwd_kernel(
    r,
    x0, x1, x2, x3, wq, wk, wv, vecs, pw, near_q, kf,
    k_far, v_far, kt_far, xt_far, qc_far, qf_far, qht_far, qlt_far, pt_far, pooled_out, ctx_out, ctxt_out, lse_out,
    x_s, vt_s, wph, wpl, k_out, v_out, kt_out, xt_out, qc_out, qf_out, qht_out, qlt_out, pt_out, sem,
):
    copies = []

    def send(here, there):
        copies.append(pltpu.make_async_copy(here, there, sem.at[len(copies)]))
        copies[-1].start()

    qb, cb, pb, vb = (vecs[i : i + 1, :] for i in range(4))
    spread_heads(pw, wph, wpl, 2)
    rows = lax.broadcasted_iota(jnp.int32, (64, 128), 0)
    cols = lax.broadcasted_iota(jnp.int32, (64, 128), 1)
    pair = jnp.where(cols // 2 == rows, 0.5, 0.0).astype(BF)
    for d, piece in enumerate((x0, x1, x2, x3)):
        x_s[d * 128 : d * 128 + 128, :] = piece[...]
        pooled_out[d * 64 : d * 64 + 64, :] = nn(pair, piece[...])
    pooled_low = pooled_out[...].astype(BF)
    pt_out[...] = pooled_low.T
    send(pt_out, pt_far)
    x = x_s[...]
    xt_out[...] = x.T
    send(xt_out, xt_far)
    q = nn(pooled_low, wq[...]) + qb
    k = nn(x, wk[...]).astype(BF)
    k_out[...] = k
    kt_out[...] = k.T
    send(k_out, k_far)
    send(kt_out, kt_far)
    v = (nn(x, wv[...]) + vb).astype(BF)
    v_out[...] = v
    send(v_out, v_far)
    vt_s[...] = v.T
    qc_out[...] = (q + cb).astype(BF) * 0.125
    hi, lo = split(q + pb)
    qht_out[...] = hi.T
    qlt_out[...] = lo.T
    send(qc_out, qc_far)
    send(qht_out, qht_far)
    send(qlt_out, qlt_far)
    sin4 = jnp.concatenate([near_q[:, :128]] * 2, axis=1)
    cos4 = jnp.concatenate([near_q[:, 128:]] * 2, axis=1)
    for g in range(3):
        at = slice(256 * g, 256 * g + 256)
        both = three(nn, hi[:, at], lo[:, at], wph[g], wpl[g])
        side = both[:, :256] * sin4 + both[:, 256:] * cos4
        qf_out[:, at] = side.astype(BF) * 0.125
    send(qf_out, qf_far)
    lane = lax.broadcasted_iota(jnp.int32, (256, 128), 1)
    zero = jnp.zeros((256, 128), BF)
    one_a = (lane == 64).astype(F32).astype(BF)
    one_b = (lane == 0).astype(F32).astype(BF)

    def one_pair(i, carry):
        at = pl.ds(pl.multiple_of(i * 128, 128), 128)
        k_pair = k_out[:, at]
        qc_pair = qc_out[:, at]
        qf_pair = qf_out[:, at]
        for s in range(2):
            mine = (lane < 64) if s == 0 else (lane >= 64)
            left = jnp.concatenate([k_pair, kf[r, s]], axis=1)
            right = jnp.concatenate(
                [jnp.where(mine, qc_pair, zero), jnp.where(mine, qf_pair, (one_a, one_b)[s])], axis=1
            )
            scores = nt(left, right)
            highest = jnp.max(scores, axis=0, keepdims=True)
            raised = jnp.exp(scores - highest)
            total = jnp.sum(raised, axis=0, keepdims=True)
            weights = (raised * (1.0 / total)).astype(BF)
            head = pl.ds(pl.multiple_of(i * 128 + s * 64, 64), 64)
            ctxt_out[head, :] = nn(vt_s[head, :], weights).astype(BF)
            lse_out[i * 2 + s] = highest + jnp.log(total)
        return carry

    lax.fori_loop(0, 6, one_pair, 0)
    ctx_out[...] = ctxt_out[...].T
    for copy in copies:
        copy.wait()


def attn_fwd(r, args, after=()):
    return call(
        functools.partial(attn_fwd_kernel, r), "attn_fwd", (), args,
        (
            b16(512, 768), b16(512, 768), b16(768, 512), b16(768, 512), b16(256, 768), b16(256, 768),
            b16(768, 256), b16(768, 256), b16(768, 256), f32(256, 768), b16(256, 768), b16(768, 256),
            f32(12, 1, 256),
        ),
        (
            vs(512, 768, dtype=BF), vs(768, 512, dtype=BF), vs(3, 256, 512, dtype=BF), vs(3, 256, 512, dtype=BF),
            vs(512, 768, dtype=BF), vs(512, 768, dtype=BF), vs(768, 512, dtype=BF), vs(768, 512, dtype=BF),
            vs(256, 768, dtype=BF), vs(256, 768, dtype=BF), vs(768, 256, dtype=BF), vs(768, 256, dtype=BF),
            vs(768, 256, dtype=BF), sems(9),
        ),
        after, mib=20, far_outs=range(9), flops=4 * 10**9, moved=12 * 10**6,
    )


def layer_stats(a):
    center = a - jnp.mean(a, axis=-1, keepdims=True)
    rs = lax.rsqrt(jnp.mean(center * center, axis=-1, keepdims=True) + 1e-05)
    return center * rs, rs


def layer_back(dn, n, rs):
    return rs * (dn - jnp.mean(dn, axis=-1, keepdims=True) - n * jnp.mean(dn * n, axis=-1, keepdims=True))


def put_blocks(source, near, far, me, slabs, first):
    for r in range(16):
        for half, out in enumerate((near, far)):
            place = (r ^ me) ^ (16 * half)
            row = pl.multiple_of((place // 2) * 48, 16)
            col = pl.multiple_of((place % 2) * 384, 128)
            for to, s in slabs:
                at = pl.ds(row + (s // 9 * 768 + s % 9 // 3 * 16), 16)
                out[r, first + to] = source[at, pl.ds(col + s % 3 * 128, 128)].astype(BF)


def ffn_down_kernel(
    masks, ctx0, ctx1, pooled0, pooled1, c0, c1, c2, c3, wo, wu, wd, vecs, ub,
    out0, out1, out23, d2_out, df_out, x1t_out, n1_out, rs_out, gp_out, near, far, vec_out,
    act_s, acc_s, x1_s, g_s,
):
    def chunk(c):
        return pl.ds(pl.multiple_of(c * CH, CH), CH)

    ob, ig, ish, db, og, osh = (vecs[i : i + 1, :] for i in range(4, 10))
    ctx = jnp.concatenate([ctx0[...], ctx1[...]], axis=0)
    pooled = jnp.concatenate([pooled0[...], pooled1[...]], axis=0)
    n1, rs1 = layer_stats(pooled + (nn(ctx, wo[...]) + ob))
    n1_out[...] = n1
    rs_out[...] = rs1
    x1 = n1 * ig + ish
    x1_s[...] = x1.astype(BF)
    x1t_out[...] = x1.astype(BF).T
    acc_s[...] = x1 + db

    def up_chunk(c, carry):
        at = chunk(c)
        z = nn(x1_s[...], wu[:, at]) + ub[:, at]
        phi = 0.5 + 0.5 * lax.erf(z * math.sqrt(0.5))
        gp_out[:, at] = phi + z * (jnp.exp(-0.5 * z * z) * (1.0 / math.sqrt(2.0 * math.pi)))
        act = (z * phi).astype(BF)
        act_s[:, at] = act
        acc_s[...] += nn(act, wd[at, :])
        return carry

    lax.fori_loop(0, 6, up_chunk, 0)
    n2, rs2 = layer_stats(acc_s[...])
    result = (n2 * og + osh).astype(BF)
    for d, out in enumerate((out0, out1, out23.at[0], out23.at[1])):
        for r in range(2):
            out[r] = result[r * 256 + d * 64 : r * 256 + d * 64 + 64, :]
    cot = jnp.concatenate([c[r] for r in range(2) for c in (c0, c1, c2, c3)], axis=0).astype(F32)
    vec_out[0:1, :] = jnp.sum(cot * n2, axis=0, keepdims=True)
    vec_out[1:2, :] = jnp.sum(cot, axis=0, keepdims=True)
    d2 = layer_back(cot * og, n2, rs2)
    df = d2.astype(BF)
    df_out[...] = df
    vec_out[2:3, :] = jnp.sum(df.astype(F32), axis=0, keepdims=True)
    d2_out[...] = d2

    def down_chunk(which, i, carry):
        c = which * 3 + i
        g_s[...] = tn(act_s[:, chunk(c)], df_out[...])
        slab = c * 6
        me = masks[2 + which]
        for r in range(32):
            row = pl.ds(pl.multiple_of((r ^ me) * 16, 16), 16)
            for j in range(6):
                (near, far)[r // 16][r % 16, slab + j] = g_s[row, j * 128 : j * 128 + 128].astype(BF)
        return carry

    for which in range(2):
        lax.fori_loop(0, 3, functools.partial(down_chunk, which), 0)


def ffn_down(masks, args, after=()):
    grad = b16(16, 36, 16, 128)
    return call(
        ffn_down_kernel, "ffn_down", (masks,), args,
        (
            b16(2, 64, 768), b16(2, 64, 768), b16(2, 2, 64, 768), f32(512, 768), b16(512, 768),
            b16(768, 512), f32(512, 768), f32(512, 1), f32(512, 3072), grad, grad, f32(8, 768),
        ),
        (vs(512, 3072, dtype=BF), vs(512, 768), vs(512, 768, dtype=BF), vs(512, 768)),
        after, mib=18, flops=8 * 10**9, moved=25 * 10**6,
    )


def hidden_back(masks, which, df_in, gp, x1t, wu, wd, near, far, upb_out, acc_s, u_s):
    me = masks[2 + which]

    def up_chunk(i, carry):
        at = pl.ds(pl.multiple_of((which * 3 + i) * CH, CH), CH)
        dz = (nt(df_in[...], wd[at, :]) * gp[:, at]).astype(BF)
        upb_out[:, pl.ds(pl.multiple_of(i * CH, CH), CH)] = jnp.sum(dz.astype(F32), axis=0, keepdims=True)
        acc_s[...] += nt(dz, wu[:, at])
        u_s[...] = nn(x1t[...], dz)
        slab = (which * 3 + i) * 6
        for r in range(32):
            place = r ^ me
            row = pl.multiple_of((place // 4) * 96, 32)
            col = pl.ds(pl.multiple_of((place % 4) * 128, 128), 128)
            for j in range(6):
                (near, far)[r // 16][r % 16, slab + j] = u_s[pl.ds(row + 16 * j, 16), col].astype(BF)
        return carry

    lax.fori_loop(0, 3, up_chunk, 0)


def ffn_up_a_kernel(masks, df_in, d2, gp, x1t, wu, wd, acc, near, far, upb_out, u_s):
    acc[...] = d2[...]
    hidden_back(masks, 0, df_in, gp, x1t, wu, wd, near, far, upb_out, acc, u_s)


def ffn_up_a(masks, args, after=()):
    return call(
        ffn_up_a_kernel, "ffn_up_a", (masks,), args,
        (f32(512, 768), b16(16, 45, 16, 128), b16(16, 45, 16, 128), f32(1, 1536)),
        (vs(768, 512),), after, mib=14, flops=4 * 10**9, moved=12 * 10**6,
    )


def ffn_up_b_kernel(
    masks, df_in, acc, gp, x1t, n1, rs, ctxt0, ctxt1, wo, wu, wd, vecs, near_in, far_in,
    d1_out, dctx_out, near, far, vec_out, upb_out,
    acc_s, u_s, o_s,
):
    ig = vecs[5:6, :]
    acc_s[...] = acc[...]
    hidden_back(masks, 1, df_in, gp, x1t, wu, wd, near, far, upb_out, acc_s, u_s)
    dx1 = acc_s[...]
    vec_out[0:1, :] = jnp.sum(dx1 * n1[...], axis=0, keepdims=True)
    vec_out[1:2, :] = jnp.sum(dx1, axis=0, keepdims=True)
    d1 = layer_back(dx1 * ig, n1[...], rs[...])
    d1_out[...] = d1
    do = d1.astype(BF)
    vec_out[2:3, :] = jnp.sum(do.astype(F32), axis=0, keepdims=True)
    dctx = nt(do, wo[...]).astype(BF)
    for r in range(2):
        dctx_out[r] = dctx[r * 256 : r * 256 + 256]
    o_s[...] = nn(ctxt0[...], do[:256]) + nn(ctxt1[...], do[256:])
    put_blocks(o_s, near, far, masks[3], [(i, i) for i in range(9)], 36)


def ffn_up_b(masks, args, after=()):
    return call(
        ffn_up_b_kernel, "ffn_up_b", (masks,), args,
        (f32(512, 768), b16(2, 256, 768), b16(16, 45, 16, 128), b16(16, 45, 16, 128), f32(8, 768), f32(1, 1536)),
        (vs(512, 768), vs(768, 512), vs(768, 768)),
        after, mib=16, flops=5 * 10**9, moved=14 * 10**6, aliases=((12, 2), (13, 3)),
    )


def attn_bwd_kernel(
    r,
    k, v, kt, qc, qf, qht, qlt, lse, dctx, kf, kst, far_q, pw,
    dk_out, dv_out, dq_out, pwg_out, vec_out,
    dqct_s, dpt_s, wph, wpl,
):
    spread_heads(pw, wph, wpl, 1)
    lane = lax.broadcasted_iota(jnp.int32, (256, 128), 1)
    zero = jnp.zeros((256, 128), BF)
    one_a = (lane == 64).astype(F32).astype(BF)
    one_b = (lane == 0).astype(F32).astype(BF)

    def one_pair(i, carry):
        at = pl.ds(pl.multiple_of(i * 128, 128), 128)
        k_pair = k[:, at]
        v_pair = v[:, at]
        qc_pair = qc[:, at]
        qf_pair = qf[:, at]
        dc_pair = dctx[r, :, at]
        for s in range(2):
            mine = (lane < 64) if s == 0 else (lane >= 64)
            left = jnp.concatenate([k_pair, kf[r, s]], axis=1)
            qc_mine = jnp.where(mine, qc_pair, zero)
            dc_mine = jnp.where(mine, dc_pair, zero)
            right = jnp.concatenate([qc_mine, jnp.where(mine, qf_pair, (one_a, one_b)[s])], axis=1)
            weights = jnp.exp(nt(left, right) - lse[i * 2 + s])
            dweights = nt(v_pair, dc_mine)
            inner = jnp.sum(weights * dweights, axis=0, keepdims=True)
            dscore = (weights * (dweights - inner)).astype(BF)
            dv_part = nn(weights.astype(BF), dc_mine)
            dk_part = nn(dscore, qc_mine)
            if s == 0:
                dv_first, dk_first = dv_part, dk_part
            head = pl.ds(pl.multiple_of(i * 128 + s * 64, 64), 64)
            side = nn(jnp.concatenate([kt[head, :], kst[...]], axis=0), dscore)
            dqct_s[head, :] = side[0:64] * 0.125
            dpt_s[head, :] = (side[64:128] * far_q[:64] + side[128:192] * far_q[64:]) * 0.125
        dv_out[:, at] = (dv_first + dv_part).astype(BF)
        dk_out[:, at] = (dk_first + dk_part).astype(BF)
        return carry

    lax.fori_loop(0, 6, one_pair, 0)
    ones = jnp.ones((8, 256), BF)
    for g in range(3):
        at = slice(256 * g, 256 * g + 256)
        hi, lo = split(dpt_s[at, :])
        pwg = three(nt, qht[at, :], qlt[at, :], hi, lo)
        early = lax.broadcasted_iota(jnp.int32, (64, 128), 1) < 64
        for i in range(2):
            m = 128 * i
            mixed = jnp.where(early, pwg[m : m + 64, m : m + 128], pwg[m + 64 : m + 128, m : m + 128])
            pwg_out[(2 * g + i) * 64 : (2 * g + i) * 64 + 64, :] = mixed
        shift = three(nn, wph[g], wpl[g], hi, lo)
        content = dqct_s[at, :]
        dq = (content + shift).T.astype(BF)
        dq_out[:, at] = dq
        shi, slo = split(shift)
        chi, clo = split(content)
        vec_out[0:1, at] = (nt(ones, chi) + nt(ones, clo))[0:1]
        vec_out[1:2, at] = (nt(ones, shi) + nt(ones, slo))[0:1]
        vec_out[2:3, at] = jnp.sum(dq.astype(F32), axis=0, keepdims=True)
    vec_out[3:4, :] = jnp.sum(dv_out[...].astype(F32), axis=0, keepdims=True)


def attn_bwd(r, args, after=()):
    return call(
        functools.partial(attn_bwd_kernel, r), "attn_bwd", (), args,
        (b16(512, 768), b16(512, 768), b16(256, 768), f32(384, 128), f32(8, 768)),
        (vs(768, 256), vs(768, 256), vs(3, 256, 256, dtype=BF), vs(3, 256, 256, dtype=BF)),
        after, mib=14, flops=8 * 10**9, moved=12 * 10**6,
    )


def tokens_back_kernel(dk0, dk1, dv0, dv1, dq0, dq1, d1, wq, wk, wv, t0, t1, t2, t3, tok_s):
    rows = lax.broadcasted_iota(jnp.int32, (512, 256), 0)
    cols = lax.broadcasted_iota(jnp.int32, (512, 256), 1)
    spread = jnp.where(rows // 2 == cols, 0.5, 0.0).astype(BF)
    for r, (dk, dv, dq) in enumerate(((dk0, dv0, dq0), (dk1, dv1, dq1))):
        hi, lo = split(d1[r * 256 : r * 256 + 256, :] + nt(dq[...], wq[...]))
        tok_s[...] = (nt(dk[...], wk[...]) + nt(dv[...], wv[...])) + (nn(spread, hi) + nn(spread, lo))
        for d, out in enumerate((t0, t1, t2, t3)):
            out[r] = tok_s[d * 128 : d * 128 + 128, :].astype(BF)


def weights_back_kernel(
    masks, xt0, xt1, pt0, pt1, dk0, dk1, dv0, dv1, dq0, dq1, pwg0, pwg1, av0, av1, vec_d, vec_u, upb_a, upb_b,
    near, far, g_s, smalls,
):
    smalls[0:384, :] = pwg0[...] + pwg1[...]
    attn = av0[...] + av1[...]
    lines = [vec_d[i : i + 1, :] for i in range(3)] + [vec_u[i : i + 1, :] for i in range(3)]
    lines += [upb[:, 768 * i : 768 * i + 768] for upb in (upb_a, upb_b) for i in range(2)] + [attn[i : i + 1, :] for i in range(4)]
    for i, line in enumerate(lines):
        for t in range(6):
            row = 384 + 6 * i + t
            smalls[row : row + 1, :] = line[:, 128 * t : 128 * t + 128]
    smalls[468:512, :] = jnp.zeros((44, 128), F32)
    g_s[0:768, :] = nn(pt0[...], dq0[...]) + nn(pt1[...], dq1[...])
    g_s[768:1536, :] = nn(xt0[...], dk0[...]) + nn(xt1[...], dk1[...])
    g_s[1536:2304, :] = nn(xt0[...], dv0[...]) + nn(xt1[...], dv1[...])
    put_blocks(g_s, near, far, masks[2], [(i, i) for i in range(NA)], 0)
    put_blocks(g_s, near, far, masks[3], [(i, i) for i in range(NA, 27)], 0)
    for r in range(16):
        for half, out in enumerate((near, far)):
            row = pl.ds(pl.multiple_of((r ^ masks[3] ^ (16 * half)) * 16, 16), 16)
            out[r, 27] = smalls[row, :].astype(BF)


def last_back_kernel(
    scalars, k, v, kt, qc, qf, qht, qlt, lse, dctx, kf, kst, far_q, pw, xt0, xt1, pt0, pt1, dk0, dv0, dq0, pwg0, av0, vec_d,
    vec_u, upb_a, upb_b, d1, wq, wk, wv,
    near, far, t0, t1, t2, t3,
    dqct_s, dpt_s, wph, wpl, dk1, dv1, dq1, pwg1, av1, g_s, smalls, tok_s,
):
    attn_bwd_kernel(
        1, k, v, kt, qc, qf, qht, qlt, lse, dctx, kf, kst, far_q, pw, dk1, dv1, dq1, pwg1, av1, dqct_s, dpt_s, wph, wpl
    )
    weights_back_kernel(
        scalars, xt0, xt1, pt0, pt1, dk0, dk1, dv0, dv1, dq0, dq1, pwg0, pwg1, av0, av1, vec_d, vec_u, upb_a, upb_b, near, far,
        g_s, smalls,
    )
    tokens_back_kernel(dk0, dk1, dv0, dv1, dq0, dq1, d1, wq, wk, wv, t0, t1, t2, t3, tok_s)


def last_back(scalars, args, after=()):
    grad = b16(16, 28, 16, 128)
    return call(
        last_back_kernel, "last_back", (scalars,), args,
        (grad, grad) + (b16(2, 128, 768),) * 4,
        (
            vs(768, 256), vs(768, 256), vs(3, 256, 256, dtype=BF), vs(3, 256, 256, dtype=BF), vs(512, 768, dtype=BF),
            vs(512, 768, dtype=BF), vs(256, 768, dtype=BF), vs(384, 128), vs(8, 768), vs(2304, 768), vs(512, 128),
            vs(512, 768),
        ),
        after, mib=28, flops=17 * 10**9, moved=30 * 10**6,
    )


def partner(x, bit):
    size = lax.axis_size("batch")
    return lax.ppermute(x, "batch", [(i, i ^ bit) for i in range(size)])


def add_kernel(step, cuts, parts, *refs):
    here, came, outs = refs[:parts], refs[parts : 2 * parts], refs[2 * parts :]
    if step < 5:
        pieces = 2 if step < 4 else 1
        at = 0
        for p in range(parts):
            rows, slabs = here[p].shape[:2]
            half = rows // pieces

            def add(r, carry, p=p, at=at, half=half, slabs=slabs):
                for h in range(pieces):
                    total = (here[p][h * half + r].astype(F32) + came[p][h * half + r].astype(F32)).astype(BF)
                    if len(outs) == pieces:
                        outs[h][r, at : at + slabs] = total
                    elif parts == 2:
                        outs[pieces * p + h][r] = total
                    else:
                        outs[h][r] = total[:cuts]
                        outs[pieces + h][r] = total[cuts:]
                return carry

            lax.fori_loop(0, half, add, 0)
            at += slabs
    else:
        at = 0
        for p in range(parts):
            rows, slabs = here[p].shape[:2]
            for source, to in ((here[p], slice(0, rows)), (came[p], slice(rows, 2 * rows))):
                if len(outs) == 1:
                    outs[0][to, at : at + slabs] = source[...]
                elif parts == 2:
                    outs[p][to] = source[...]
                else:
                    outs[0][to] = source[:, :cuts]
                    outs[1][to] = source[:, cuts:]
            at += slabs


class Order:
    def __init__(self):
        self.last = ()

    def run(self, function, *args, also=()):
        *results, token = function(*args, (*self.last, *also))
        self.last = (token,)
        return results


class Sum:
    def __init__(self, order, keep, sends, cuts, bits):
        core, first, second, third, fourth, self.others = bits
        self.bits = [(core,) * len(keep), (first, second), (second, first), (third,), (fourth,)]
        self.bits += [(fourth,), (third,), (second, first), (first, second), (core,)]
        self.cuts, self.slabs = cuts, sum(k.shape[1] for k in keep)
        self.order, self.keep, self.sends, self.step = order, keep, sends, 0

    def start(self):
        self.got = [partner(s, b) for s, b in zip(self.sends, self.bits[self.step])]
        return self

    def plan(self):
        step, a, b = self.step, self.cuts, self.slabs - self.cuts
        here = self.keep if step < 5 else self.sends
        rows = (8, 4, 2, 1, 1, 2, 4, 8, 16)[step]
        shapes = [(a,), (b,)] if step in (0, 1, 6, 7) else [(a + b,)]
        outs = [b16(rows, *s, 16, 128) for s in shapes for _ in range(2 if step < 4 else 1)]
        kernel = functools.partial(add_kernel, step, a, len(here))
        return kernel, (*here, *self.got), outs

    def take(self, outs):
        step = self.step
        if step < 4:
            self.keep, self.sends = outs[::2], outs[1::2]
        else:
            self.sends = outs
        if step == 4:
            for bit in self.others:
                self.sends = [(s.astype(F32) + partner(s, bit).astype(F32)).astype(BF) for s in self.sends]
        self.step += 1

    def finish(self):
        if self.step < 9:
            finish_together(self.order, (self,))
        else:
            self.sends = (*self.sends, *self.got)
            self.step += 1
        return self


def finish_together(order, sums, also=()):
    plans = [s.plan() for s in sums]
    args = [a for p in plans for a in p[1]]
    outs = [o for p in plans for o in p[2]]

    def kernel(*refs):
        here, there = 0, len(args)
        for step, taken, given in plans:
            step(*refs[here : here + len(taken)], *refs[there : there + len(given)])
            here, there = here + len(taken), there + len(given)

    results = order.run(
        lambda after: call(kernel, "sum_step", (), args, outs, after=after, mib=8, moved=10**6), also=also
    )
    for s, (_, _, given) in zip(sums, plans):
        s.take(results[: len(given)])
        results = results[len(given) :]


def get_blocks(me, halves, slabs, outs):
    for half, source in enumerate(halves):
        for r in range(16):
            place = (r ^ me) ^ (16 * half)
            row = pl.multiple_of((place // 2) * 48, 16)
            col = pl.multiple_of((place % 2) * 384, 128)
            for at, s in slabs:
                to = pl.ds(row + s % 9 // 3 * 16, 16)
                outs[s // 9][to, pl.ds(col + s % 3 * 128, 128)] = source[r, at].astype(F32)


def rows_kernel(masks, near, far, out):
    c = pl.program_id(0)
    me = masks[2 + c // 3]
    for r in range(32):
        row = pl.ds(pl.multiple_of((r ^ me) * 16, 16), 16)
        for j in range(6):
            out[row, j * 128 : j * 128 + 128] = (near, far)[r // 16][r % 16, c * 6 + j].astype(F32)


def assemble_rows(masks, halves, after=()):
    return call_grid(
        rows_kernel, "assemble_rows", 6, (masks,), halves, (f32(3072, 768),), (pl.BlockSpec((512, 768), lambda c: (c, 0)),),
        after, 24, 14 * 10**6,
    )


def up_kernel(masks, near, far, out, o_out):
    c = pl.program_id(0)
    me = masks[2 + c // 3]
    for r in range(32):
        place = r ^ me
        row = pl.multiple_of((place // 4) * 96, 32)
        col = pl.ds(pl.multiple_of((place % 4) * 128, 128), 128)
        for j in range(6):
            out[pl.ds(row + 16 * j, 16), col] = (near, far)[r // 16][r % 16, c * 6 + j].astype(F32)

    @pl.when(c == 0)
    def _():
        get_blocks(masks[3], (near, far), [(36 + i, i) for i in range(9)], (o_out,))


def assemble_up(masks, halves, after=()):
    return call_grid(
        up_kernel, "assemble_up", 6, (masks,), halves, (f32(768, 3072), f32(768, 768)),
        (pl.BlockSpec((768, 512), lambda c: (0, c)), VM), after, 28, 18 * 10**6,
    )


def three_kernel(masks, near, far, q_out, k_out, v_out, w_out, l_out, s_out):
    outs = (q_out, k_out, v_out)
    get_blocks(masks[2], (near, far), [(i, i) for i in range(NA)], outs)
    get_blocks(masks[3], (near, far), [(i, i) for i in range(NA, 27)], outs)
    for half, source in enumerate((near, far)):
        for r in range(16):
            row = pl.ds(pl.multiple_of((r ^ masks[3] ^ (16 * half)) * 16, 16), 16)
            s_out[row, :] = source[r, 27].astype(F32)
    for h in range(12):
        w_out[h] = s_out[h // 2 * 64 : h // 2 * 64 + 64, h % 2 * 64 : h % 2 * 64 + 64]
    for i in range(14):
        for t in range(6):
            row = 384 + 6 * i + t
            l_out[i : i + 1, 128 * t : 128 * t + 128] = s_out[row : row + 1, :]


def assemble_three(masks, halves, after=()):
    return call(
        three_kernel, "assemble_three", (masks,), halves, (f32(768, 768),) * 3 + (f32(12, 64, 64), f32(16, 768)),
        (vs(512, 128),), after, mib=36, moved=11 * 10**6, last=True,
    )


def owners_kernel(scalars, p0, p2, p13, out):
    j = scalars[0]
    out[j] = p0[...].astype(out.dtype)
    out[j ^ 2] = (p2[0] if len(p2.shape) > len(p0.shape) else p2[...]).astype(out.dtype)
    out[j ^ 1] = p13[0].astype(out.dtype)
    out[j ^ 3] = p13[1].astype(out.dtype)


def assemble_owners(name, dtype, scalars, pieces, after=()):
    shape = (4, *pieces[0].shape)
    return call(
        owners_kernel, name, (scalars,), pieces, (jax.ShapeDtypeStruct(shape, dtype),), after=after, moved=5 * 10**6,
        last=True,
    )


def join_pieces(own, came, after=()):
    def kernel(a, b, out):
        out[0] = a[...]
        out[1] = b[1] if len(b.shape) > len(a.shape) else b[...]

    shape = (2, *own.shape)
    return call(kernel, "join", (), (own, came), (jax.ShapeDtypeStruct(shape, own.dtype),), after=after, moved=10**6)


def pick_kernel(row, scalars, blocks, o0, o1, o2, o3, sem):
    copies = []
    for d, out in enumerate((o0, o1, o2, o3)):
        source = blocks.at[scalars[0] ^ d] if row is None else blocks.at[scalars[0] ^ d, row]
        copies.append(pltpu.make_async_copy(source, out, sem.at[d]))
        copies[-1].start()
    for copy in copies:
        copy.wait()


def pick(row, scalars, blocks, after=()):
    shape = blocks.shape[1:] if row is None else blocks.shape[2:]
    return call(
        functools.partial(pick_kernel, row), "pick", (scalars,), (blocks,), (b16(*shape),) * 4, (sems(4),), after=after,
        mib=4, moved=2 * 10**6, far_args=(0,),
    )


def on_device(
    tokens, lengths, cotangent, query_weight, query_bias, key_weight, value_weight, value_bias, content_bias,
    position_bias, position_weight, out_weight, out_bias, inner_gain, inner_shift, up_weight, up_bias, down_weight,
    down_bias, outer_gain, outer_shift,
):
    size = lax.axis_size("batch")
    me = lax.axis_index("batch").astype(jnp.int32)
    j = me % G
    core, first, second, third, fourth = 1, 2, 4, 8, 16
    others = [1 << b for b in range(5, size.bit_length() - 1)]
    bits = (core, first, second, third, fourth, others)
    has = lambda bit: (me // bit) % 2
    low = has(core) * 16 + has(third) * 2 + has(fourth)
    scalars = jnp.stack(
        [j, me // G * 8 + 2 * j, low + has(first) * 8 + has(second) * 4, low + has(second) * 8 + has(first) * 4]
    )
    order = Order()

    by_owner = tokens[0].reshape(4, 2, 128, 768)
    cot_owner = cotangent[0].reshape(4, 2, 64, 768)

    def trade(pieces):
        return [pieces[0]] + [partner(pieces[d], d) for d in (1, 2, 3)]

    x0 = trade(order.run(pick, 0, scalars, by_owner))
    lines = (
        query_bias, content_bias, position_bias, value_bias, out_bias, inner_gain, inner_shift, down_bias, outer_gain,
        outer_shift,
    )
    near_q, far_q, kst, kf, vecs = order.run(tables, scalars, lengths, lines, ())
    s1 = order.run(pick, 1, scalars, by_owner)
    sc = order.run(pick, None, scalars, cot_owner)
    x1 = trade(order.run(gate, s1, also=x0[1:]))

    def forward(r, x):
        return order.run(
            attn_fwd, r, (*x, query_weight, key_weight, value_weight, vecs, position_weight, near_q, kf)
        )

    fwd = [forward(0, x0)]
    cot = trade(order.run(gate, sc, also=x1[1:]))
    fwd.append(forward(1, x1))
    k, v, kt, xt, qc, qf, qht, qlt, pt, pooled, ctx, ctxt, lse = zip(*fwd)
    outs = order.run(
        ffn_down, scalars, (*ctx, *pooled, *cot, out_weight, up_weight, down_weight, vecs, up_bias[None, :])
    )
    out0, out1, out23, d2, df, x1t, n1, rs1, gp, near, far, vec_d = outs
    far, out23 = order.run(gate, (far, out23))
    down = Sum(order, (near,), (far,), 18, bits).start()
    back23 = partner(out23, 2)
    acc, near, far, upb_a = order.run(ffn_up_a, scalars, (df, d2, gp, x1t, up_weight, down_weight))
    down.finish().start()
    (out13,) = order.run(join_pieces, out1, back23)
    back13 = partner(out13, 1)
    d1, dctx, near, far, vec_u, upb_b = order.run(
        ffn_up_b, scalars, (df, acc, gp, x1t, n1, rs1, *ctxt, out_weight, up_weight, down_weight, vecs, near, far)
    )
    down.finish().start()
    (far,) = order.run(gate, (far,))
    up = Sum(order, (near,), (far,), 18, bits).start()

    def backward(r):
        return k[r], v[r], kt[r], qc[r], qf[r], qht[r], qlt[r], lse[r], dctx, kf, kst, far_q, position_weight

    dk, dv, dq, pwg, attn_vec = order.run(attn_bwd, 0, backward(0))
    finish_together(order, (down, up))
    down.start(), up.start()
    near, far, t0, t1, t2, t3 = order.run(
        last_back, scalars,
        (
            *backward(1), *xt, *pt, dk, dv, dq, pwg, attn_vec, vec_d, vec_u, upb_a, upb_b, d1, query_weight, key_weight,
            value_weight,
        ),
    )

    finish_together(order, (up, down))
    up.start(), down.start()
    (far,) = order.run(gate, (far,))
    three = Sum(order, (near,), (far,), NA, bits).start()
    finish_together(order, (up, down, three))
    up.start(), down.start(), three.start()
    finish_together(order, (up, down, three))
    up.start(), down.start(), three.start()
    (t3,) = order.run(gate, (t3,))
    u3 = partner(t3, 2)
    finish_together(order, (up, down, three), also=(u3,))
    up.start(), down.start(), three.start()
    (t2,) = order.run(gate, (t2,))
    u2 = partner(t2, 2)
    finish_together(order, (up, down, three), also=(u2,))
    up.start(), down.start(), three.start()
    (t13,) = order.run(join_pieces, t1, u3)
    u13 = partner(t13, 1)
    layer_output = order.run(assemble_owners, "layer_output", BF, scalars, (out0, back23, back13))[0]
    finish_together(order, (up, three, down))
    up.start(), three.start(), down.start()
    finish_together(order, (up, three))
    up.start(), three.start()
    down.finish()
    down_weight_grad = order.run(assemble_rows, scalars, down.sends)[0]
    finish_together(order, (three,))
    three.start()
    tokens_grad = order.run(assemble_owners, "tokens_grad", F32, scalars, (t0, u2, u13))[0]
    finish_together(order, (three,))
    three.start()
    finish_together(order, (up,))
    up.start()
    up.finish()
    up_weight_grad, out_weight_grad = order.run(assemble_up, scalars, up.sends)
    finish_together(order, (three,))
    three.start()
    three.finish()
    query_weight_grad, key_weight_grad, value_weight_grad, position_weight_grad, lines = order.run(
        assemble_three, scalars, three.sends
    )
    layer_output = layer_output.reshape(1, 8, 64, 768)
    tokens_grad = tokens_grad.reshape(1, 8, 128, 768)
    line = lambda i: lines[i]
    return (
        layer_output, tokens_grad, query_weight_grad, line(12), key_weight_grad, value_weight_grad, line(13), line(10),
        line(11), position_weight_grad, out_weight_grad, line(5), line(3), line(4),
        up_weight_grad, lines[6:10].reshape(3072), down_weight_grad, line(2), line(0), line(1),
    )


def solution(mesh):
    in_specs = (P("batch", None, None, None), P(), P("batch", None, None, None)) + (P(),) * 18
    out_specs = (P("batch", None, None, None),) * 2 + (P(),) * 18
    return jax.shard_map(on_device, mesh=mesh, in_specs=in_specs, out_specs=out_specs, check_vma=False)
```

```python
import functools
import math

import jax
import jax.numpy as jnp
from jax import lax
from jax.experimental import pallas as pl
from jax.experimental.pallas import tpu as pltpu
from jax.sharding import PartitionSpec as P

G = 4
F32 = jnp.float32
BF = jnp.bfloat16
VM = pl.BlockSpec(memory_space=pltpu.VMEM)
SM = pl.BlockSpec(memory_space=pltpu.SMEM)
ANY = pl.BlockSpec(memory_space=pl.ANY)
HBM = pl.BlockSpec(memory_space=pltpu.HBM)
BLK = 16
NA = 18
CH = 512


def nn(a, b):
    return lax.dot_general(a, b, (((1,), (0,)), ((), ())), preferred_element_type=F32)


def nt(a, b):
    return lax.dot_general(a, b, (((1,), (1,)), ((), ())), preferred_element_type=F32)


def tn(a, b):
    return lax.dot_general(a, b, (((0,), (0,)), ((), ())), preferred_element_type=F32)


def split(a):
    hi = a.astype(BF)
    return hi, (a - hi.astype(F32)).astype(BF)


def three(dot, a_hi, a_lo, b_hi, b_lo):
    return dot(a_hi, b_hi) + (dot(a_hi, b_lo) + dot(a_lo, b_hi))


def params(mib):
    return pltpu.CompilerParams(vmem_limit_bytes=mib << 20)


def cost(flops, bytes_accessed, transcendentals=0):
    return pl.CostEstimate(
        flops=flops, bytes_accessed=bytes_accessed, transcendentals=transcendentals
    )


def b16(*shape):
    return jax.ShapeDtypeStruct(shape, BF)


def f32(*shape):
    return jax.ShapeDtypeStruct(shape, F32)


TOKEN = (8, 128)


def call(
    kernel, name, scalars, args, outs, scratch=(), after=(), mib=16, flops=0, moved=0, far_outs=(), last=False, far_args=(),
    aliases=(), free=(),
):
    waits = len(after)
    at = waits + len(scalars) + len(args) + len(outs)

    def body(*refs):
        refs[at][...] = jnp.zeros(TOKEN, F32)
        kernel(*refs[waits:at], *refs[at + 1 :])

    place = lambda i, o: o if last else (pltpu.HBM if i in far_outs else pltpu.VMEM)(o.shape, o.dtype)
    space = lambda i: pltpu.HBM if i in far_args else pltpu.VMEM
    near = [a if last or i in free else pltpu.with_memory_space_constraint(a, space(i)) for i, a in enumerate(args)]
    return pl.pallas_call(
        body,
        out_shape=tuple(place(i, o) for i, o in enumerate(outs)) + (pltpu.VMEM(TOKEN, F32),),
        in_specs=[ANY] * waits + [SM] * len(scalars) + [HBM if i in far_args else VM for i in range(len(args))],
        out_specs=tuple(HBM if i in far_outs else VM for i in range(len(outs))) + (VM,),
        scratch_shapes=list(scratch),
        compiler_params=params(mib),
        cost_estimate=cost(flops, moved),
        input_output_aliases={waits + len(scalars) + i: o for i, o in aliases},
        name=name,
    )(*after, *scalars, *near)


def gate(arrays, after):
    n = len(arrays)
    outs = tuple(jax.ShapeDtypeStruct(a.shape, a.dtype) for a in arrays)
    return call(lambda *refs: None, "gate", (), arrays, outs, after=after, mib=4, aliases=[(i, i) for i in range(n)])


def call_grid(kernel, name, steps, scalars, args, outs, out_specs, after, mib, moved):
    waits = len(after)
    at = waits + len(scalars) + len(args) + len(outs)

    def body(*refs):
        refs[at][...] = jnp.zeros(TOKEN, F32)
        kernel(*refs[waits:at])

    return pl.pallas_call(
        body,
        out_shape=(*outs, pltpu.VMEM(TOKEN, F32)),
        grid=(steps,),
        in_specs=[ANY] * waits + [SM] * len(scalars) + [VM] * len(args),
        out_specs=(*out_specs, VM),
        compiler_params=params(mib),
        cost_estimate=cost(0, moved),
        name=name,
    )(*after, *scalars, *args)


def sems(n):
    return pltpu.SemaphoreType.DMA((n,))


def vs(*shape, dtype=F32):
    return pltpu.VMEM(shape, dtype)


def tables_kernel(count, scalars, lengths, *refs):
    lines, (near_q, far_q, kst, kf_out, vecs), near = refs[:10], refs[count : count + 5], refs[count + 5 : count + 15]
    copies = [pltpu.make_async_copy(a, b, refs[-1].at[i]) for i, (a, b) in enumerate(zip(lines, near))]
    for copy in copies:
        copy.start()
    j = scalars[0]
    exponent = -math.log(10000.0) / 32

    def positions(shape, size, step):
        row = lax.broadcasted_iota(jnp.int32, shape, 0)
        return step * (((row // size) ^ j) * size + row % size)

    def angles(shape, size, step):
        lane = lax.broadcasted_iota(jnp.int32, shape, 1)
        w = jnp.exp((lane % 32).astype(F32) * exponent)
        return positions(shape, size, step).astype(F32) * w, lane % 64 < 32

    theta, early = angles((256, 128), 64, 2)
    sin, cos = jnp.sin(theta), jnp.cos(theta)
    signed = jnp.where(early, cos, -cos)
    near_q[:, :128] = sin
    near_q[:, 128:] = signed
    far_q[:64] = sin.T[:64]
    far_q[64:] = -signed.T[:64]
    angle, early = angles((512, 128), 128, 1)
    sin, cos = jnp.sin(angle), jnp.cos(angle)
    kf = jnp.where(early, cos, sin)
    lane = lax.broadcasted_iota(jnp.int32, (512, 128), 1)
    kst[...] = jnp.where(lane < 64, kf, jnp.where(early, sin, cos)).astype(BF).T
    place = positions((512, 128), 128, 1)
    for r in range(2):
        bias = jnp.where(place < lengths[scalars[1] + r], 0.0, -1.0e9)
        kf_out[r, 0] = jnp.where(lane < 64, kf, jnp.where(lane == 64, bias, 0.0)).astype(BF)
        kf_out[r, 1] = jnp.where(lane >= 64, kf, jnp.where(lane == 0, bias, 0.0)).astype(BF)
    for i, copy in enumerate(copies):
        copy.wait()
        vecs[i : i + 1, :] = near[i][...].reshape(1, 768)


def tables(scalars, lengths, lines, weights, after):
    outs = (f32(256, 256), f32(128, 256), b16(128, 512), b16(2, 2, 512, 128), f32(10, 768))
    kernel = functools.partial(tables_kernel, 10 + len(weights))
    scratch = [vs(768) for _ in range(10)] + [sems(10)]
    return call(kernel, "tables", (scalars, lengths), (*lines, *weights), outs, scratch, after, far_args=range(10))


def spread_heads(weight, high, low, sides):
    for g in range(3):
        high[g] = jnp.zeros((256, 256 * sides), BF)
        low[g] = jnp.zeros((256, 256 * sides), BF)
        for a in range(4):
            hi, lo = split(weight[4 * g + a])
            at = slice(64 * a, 64 * a + 64)
            high[g, at, at] = hi
            low[g, at, at] = lo
            if sides == 2:
                there = slice(256 + 64 * a, 256 + 64 * a + 64)
                high[g, at, there] = jnp.concatenate([hi[:, 32:], hi[:, :32]], axis=1)
                low[g, at, there] = jnp.concatenate([lo[:, 32:], lo[:, :32]], axis=1)


def attn_fwd_kernel(
    r,
    x0, x1, x2, x3, wq, wk, wv, vecs, pw, near_q, kf,
    k_far, v_far, kt_far, xt_far, qc_far, qf_far, qht_far, qlt_far, pt_far, pooled_out, ctx_out, ctxt_out, lse_out,
    x_s, vt_s, wph, wpl, k_out, v_out, kt_out, xt_out, qc_out, qf_out, qht_out, qlt_out, pt_out, sem,
):
    copies = []

    def send(here, there):
        copies.append(pltpu.make_async_copy(here, there, sem.at[len(copies)]))
        copies[-1].start()

    qb, cb, pb, vb = (vecs[i : i + 1, :] for i in range(4))
    spread_heads(pw, wph, wpl, 2)
    rows = lax.broadcasted_iota(jnp.int32, (64, 128), 0)
    cols = lax.broadcasted_iota(jnp.int32, (64, 128), 1)
    pair = jnp.where(cols // 2 == rows, 0.5, 0.0).astype(BF)
    for d, piece in enumerate((x0, x1, x2, x3)):
        x_s[d * 128 : d * 128 + 128, :] = piece[...]
        pooled_out[d * 64 : d * 64 + 64, :] = nn(pair, piece[...])
    pooled_low = pooled_out[...].astype(BF)
    pt_out[...] = pooled_low.T
    send(pt_out, pt_far)
    x = x_s[...]
    xt_out[...] = x.T
    send(xt_out, xt_far)
    q = nn(pooled_low, wq[...]) + qb
    k = nn(x, wk[...]).astype(BF)
    k_out[...] = k
    kt_out[...] = k.T
    send(k_out, k_far)
    send(kt_out, kt_far)
    v = (nn(x, wv[...]) + vb).astype(BF)
    v_out[...] = v
    send(v_out, v_far)
    vt_s[...] = v.T
    qc_out[...] = (q + cb).astype(BF) * 0.125
    hi, lo = split(q + pb)
    qht_out[...] = hi.T
    qlt_out[...] = lo.T
    send(qc_out, qc_far)
    send(qht_out, qht_far)
    send(qlt_out, qlt_far)
    sin4 = jnp.concatenate([near_q[:, :128]] * 2, axis=1)
    cos4 = jnp.concatenate([near_q[:, 128:]] * 2, axis=1)
    for g in range(3):
        at = slice(256 * g, 256 * g + 256)
        both = three(nn, hi[:, at], lo[:, at], wph[g], wpl[g])
        side = both[:, :256] * sin4 + both[:, 256:] * cos4
        qf_out[:, at] = side.astype(BF) * 0.125
    send(qf_out, qf_far)
    lane = lax.broadcasted_iota(jnp.int32, (256, 128), 1)
    zero = jnp.zeros((256, 128), BF)
    one_a = (lane == 64).astype(F32).astype(BF)
    one_b = (lane == 0).astype(F32).astype(BF)

    def one_pair(i, carry):
        at = pl.ds(pl.multiple_of(i * 128, 128), 128)
        k_pair = k_out[:, at]
        qc_pair = qc_out[:, at]
        qf_pair = qf_out[:, at]
        for s in range(2):
            mine = (lane < 64) if s == 0 else (lane >= 64)
            left = jnp.concatenate([k_pair, kf[r, s]], axis=1)
            right = jnp.concatenate(
                [jnp.where(mine, qc_pair, zero), jnp.where(mine, qf_pair, (one_a, one_b)[s])], axis=1
            )
            scores = nt(left, right)
            highest = jnp.max(scores, axis=0, keepdims=True)
            raised = jnp.exp(scores - highest)
            total = jnp.sum(raised, axis=0, keepdims=True)
            weights = (raised * (1.0 / total)).astype(BF)
            head = pl.ds(pl.multiple_of(i * 128 + s * 64, 64), 64)
            ctxt_out[head, :] = nn(vt_s[head, :], weights).astype(BF)
            lse_out[i * 2 + s] = highest + jnp.log(total)
        return carry

    lax.fori_loop(0, 6, one_pair, 0, unroll=2)
    ctx_out[...] = ctxt_out[...].T
    for copy in copies:
        copy.wait()


def attn_fwd(r, args, after=()):
    return call(
        functools.partial(attn_fwd_kernel, r), "attn_fwd", (), args,
        (
            b16(512, 768), b16(512, 768), b16(768, 512), b16(768, 512), b16(256, 768), b16(256, 768),
            b16(768, 256), b16(768, 256), b16(768, 256), f32(256, 768), b16(256, 768), b16(768, 256),
            f32(12, 1, 256),
        ),
        (
            vs(512, 768, dtype=BF), vs(768, 512, dtype=BF), vs(3, 256, 512, dtype=BF), vs(3, 256, 512, dtype=BF),
            vs(512, 768, dtype=BF), vs(512, 768, dtype=BF), vs(768, 512, dtype=BF), vs(768, 512, dtype=BF),
            vs(256, 768, dtype=BF), vs(256, 768, dtype=BF), vs(768, 256, dtype=BF), vs(768, 256, dtype=BF),
            vs(768, 256, dtype=BF), sems(9),
        ),
        after, mib=20, far_outs=range(9), flops=4 * 10**9, moved=12 * 10**6,
    )


def layer_stats(a):
    center = a - jnp.mean(a, axis=-1, keepdims=True)
    rs = lax.rsqrt(jnp.mean(center * center, axis=-1, keepdims=True) + 1e-05)
    return center * rs, rs


def layer_back(dn, n, rs):
    return rs * (dn - jnp.mean(dn, axis=-1, keepdims=True) - n * jnp.mean(dn * n, axis=-1, keepdims=True))


def put_blocks(source, near, far, me, slabs, first):
    for r in range(16):
        for half, out in enumerate((near, far)):
            place = (r ^ me) ^ (16 * half)
            row = pl.multiple_of((place // 2) * 48, 16)
            col = pl.multiple_of((place % 2) * 384, 128)
            for to, s in slabs:
                at = pl.ds(row + (s // 9 * 768 + s % 9 // 3 * 16), 16)
                out[r, first + to] = source[at, pl.ds(col + s % 3 * 128, 128)].astype(BF)


def ffn_down_kernel(
    masks, ctx0, ctx1, pooled0, pooled1, c0, c1, c2, c3, wo, wu, wd, vecs, ub,
    out0, out1, out23, d2_out, df_out, x1t_out, n1_out, rs_out, gp_out, near, far, vec_out,
    act_s, acc_s, x1_s, g_s,
):
    def chunk(c):
        return pl.ds(pl.multiple_of(c * CH, CH), CH)

    ob, ig, ish, db, og, osh = (vecs[i : i + 1, :] for i in range(4, 10))
    ctx = jnp.concatenate([ctx0[...], ctx1[...]], axis=0)
    pooled = jnp.concatenate([pooled0[...], pooled1[...]], axis=0)
    n1, rs1 = layer_stats(pooled + (nn(ctx, wo[...]) + ob))
    n1_out[...] = n1
    rs_out[...] = rs1
    x1 = n1 * ig + ish
    x1_s[...] = x1.astype(BF)
    x1t_out[...] = x1.astype(BF).T
    acc_s[...] = x1 + db

    def up_chunk(c, carry):
        at = chunk(c)
        z = nn(x1_s[...], wu[:, at]) + ub[:, at]
        phi = 0.5 + 0.5 * lax.erf(z * math.sqrt(0.5))
        gp_out[:, at] = phi + z * (jnp.exp(-0.5 * z * z) * (1.0 / math.sqrt(2.0 * math.pi)))
        act = (z * phi).astype(BF)
        act_s[:, at] = act
        acc_s[...] += nn(act, wd[at, :])
        return carry

    lax.fori_loop(0, 6, up_chunk, 0, unroll=2)
    n2, rs2 = layer_stats(acc_s[...])
    result = (n2 * og + osh).astype(BF)
    for d, out in enumerate((out0, out1, out23.at[0], out23.at[1])):
        for r in range(2):
            out[r] = result[r * 256 + d * 64 : r * 256 + d * 64 + 64, :]
    cot = jnp.concatenate([c[r] for r in range(2) for c in (c0, c1, c2, c3)], axis=0).astype(F32)
    vec_out[0:1, :] = jnp.sum(cot * n2, axis=0, keepdims=True)
    vec_out[1:2, :] = jnp.sum(cot, axis=0, keepdims=True)
    d2 = layer_back(cot * og, n2, rs2)
    df = d2.astype(BF)
    df_out[...] = df
    vec_out[2:3, :] = jnp.sum(df.astype(F32), axis=0, keepdims=True)
    d2_out[...] = d2

    def down_chunk(which, i, carry):
        c = which * 3 + i
        g_s[...] = tn(act_s[:, chunk(c)], df_out[...])
        slab = c * 6
        me = masks[2 + which]
        for r in range(32):
            row = pl.ds(pl.multiple_of((r ^ me) * 16, 16), 16)
            for j in range(6):
                (near, far)[r // 16][r % 16, slab + j] = g_s[row, j * 128 : j * 128 + 128].astype(BF)
        return carry

    for which in range(2):
        lax.fori_loop(0, 3, functools.partial(down_chunk, which), 0, unroll=3)


def ffn_down(masks, args, after=()):
    grad = b16(16, 36, 16, 128)
    return call(
        ffn_down_kernel, "ffn_down", (masks,), args,
        (
            b16(2, 64, 768), b16(2, 64, 768), b16(2, 2, 64, 768), f32(512, 768), b16(512, 768),
            b16(768, 512), f32(512, 768), f32(512, 1), f32(512, 3072), grad, grad, f32(8, 768),
        ),
        (vs(512, 3072, dtype=BF), vs(512, 768), vs(512, 768, dtype=BF), vs(512, 768)),
        after, mib=18, flops=8 * 10**9, moved=25 * 10**6,
    )


def hidden_back(masks, which, df_in, gp, x1t, wu, wd, near, far, upb_out, acc_s, u_s):
    me = masks[2 + which]

    def up_chunk(i, carry):
        at = pl.ds(pl.multiple_of((which * 3 + i) * CH, CH), CH)
        dz = (nt(df_in[...], wd[at, :]) * gp[:, at]).astype(BF)
        upb_out[:, pl.ds(pl.multiple_of(i * CH, CH), CH)] = jnp.sum(dz.astype(F32), axis=0, keepdims=True)
        acc_s[...] += nt(dz, wu[:, at])
        u_s[...] = nn(x1t[...], dz)
        slab = (which * 3 + i) * 6
        for r in range(32):
            place = r ^ me
            row = pl.multiple_of((place // 4) * 96, 32)
            col = pl.ds(pl.multiple_of((place % 4) * 128, 128), 128)
            for j in range(6):
                (near, far)[r // 16][r % 16, slab + j] = u_s[pl.ds(row + 16 * j, 16), col].astype(BF)
        return carry

    lax.fori_loop(0, 3, up_chunk, 0, unroll=3)


def ffn_up_a_kernel(masks, df_in, d2, gp, x1t, wu, wd, acc, near, far, upb_out, u_s):
    acc[...] = d2[...]
    hidden_back(masks, 0, df_in, gp, x1t, wu, wd, near, far, upb_out, acc, u_s)


def ffn_up_a(masks, args, after=()):
    return call(
        ffn_up_a_kernel, "ffn_up_a", (masks,), args,
        (f32(512, 768), b16(16, 45, 16, 128), b16(16, 45, 16, 128), f32(1, 1536)),
        (vs(768, 512),), after, mib=14, flops=4 * 10**9, moved=12 * 10**6,
    )


def ffn_up_b_kernel(
    masks, df_in, acc, gp, x1t, n1, rs, ctxt0, ctxt1, wo, wu, wd, vecs, near_in, far_in,
    d1_out, dctx_out, near, far, vec_out, upb_out,
    acc_s, u_s, o_s,
):
    ig = vecs[5:6, :]
    acc_s[...] = acc[...]
    hidden_back(masks, 1, df_in, gp, x1t, wu, wd, near, far, upb_out, acc_s, u_s)
    dx1 = acc_s[...]
    vec_out[0:1, :] = jnp.sum(dx1 * n1[...], axis=0, keepdims=True)
    vec_out[1:2, :] = jnp.sum(dx1, axis=0, keepdims=True)
    d1 = layer_back(dx1 * ig, n1[...], rs[...])
    d1_out[...] = d1
    do = d1.astype(BF)
    vec_out[2:3, :] = jnp.sum(do.astype(F32), axis=0, keepdims=True)
    dctx = nt(do, wo[...]).astype(BF)
    for r in range(2):
        dctx_out[r] = dctx[r * 256 : r * 256 + 256]
    o_s[...] = nn(ctxt0[...], do[:256]) + nn(ctxt1[...], do[256:])
    put_blocks(o_s, near, far, masks[3], [(i, i) for i in range(9)], 36)


def ffn_up_b(masks, args, after=()):
    return call(
        ffn_up_b_kernel, "ffn_up_b", (masks,), args,
        (f32(512, 768), b16(2, 256, 768), b16(16, 45, 16, 128), b16(16, 45, 16, 128), f32(8, 768), f32(1, 1536)),
        (vs(512, 768), vs(768, 512), vs(768, 768)),
        after, mib=16, flops=5 * 10**9, moved=14 * 10**6, aliases=((12, 2), (13, 3)),
    )


def attn_bwd_kernel(
    r,
    k, v, kt, qc, qf, qht, qlt, lse, dctx, kf, kst, far_q, pw,
    dk_out, dv_out, dq_out, pwg_out, vec_out,
    dqct_s, dpt_s, wph, wpl,
):
    spread_heads(pw, wph, wpl, 1)
    lane = lax.broadcasted_iota(jnp.int32, (256, 128), 1)
    zero = jnp.zeros((256, 128), BF)
    one_a = (lane == 64).astype(F32).astype(BF)
    one_b = (lane == 0).astype(F32).astype(BF)

    def one_pair(i, carry):
        at = pl.ds(pl.multiple_of(i * 128, 128), 128)
        k_pair = k[:, at]
        v_pair = v[:, at]
        qc_pair = qc[:, at]
        qf_pair = qf[:, at]
        dc_pair = dctx[r, :, at]
        for s in range(2):
            mine = (lane < 64) if s == 0 else (lane >= 64)
            left = jnp.concatenate([k_pair, kf[r, s]], axis=1)
            qc_mine = jnp.where(mine, qc_pair, zero)
            dc_mine = jnp.where(mine, dc_pair, zero)
            right = jnp.concatenate([qc_mine, jnp.where(mine, qf_pair, (one_a, one_b)[s])], axis=1)
            weights = jnp.exp(nt(left, right) - lse[i * 2 + s])
            dweights = nt(v_pair, dc_mine)
            inner = jnp.sum(weights * dweights, axis=0, keepdims=True)
            dscore = (weights * (dweights - inner)).astype(BF)
            dv_part = nn(weights.astype(BF), dc_mine)
            dk_part = nn(dscore, qc_mine)
            if s == 0:
                dv_first, dk_first = dv_part, dk_part
            head = pl.ds(pl.multiple_of(i * 128 + s * 64, 64), 64)
            side = nn(jnp.concatenate([kt[head, :], kst[...]], axis=0), dscore)
            dqct_s[head, :] = side[0:64] * 0.125
            dpt_s[head, :] = (side[64:128] * far_q[:64] + side[128:192] * far_q[64:]) * 0.125
        dv_out[:, at] = (dv_first + dv_part).astype(BF)
        dk_out[:, at] = (dk_first + dk_part).astype(BF)
        return carry

    lax.fori_loop(0, 6, one_pair, 0, unroll=2)
    ones = jnp.ones((8, 256), BF)
    for g in range(3):
        at = slice(256 * g, 256 * g + 256)
        hi, lo = split(dpt_s[at, :])
        pwg = three(nt, qht[at, :], qlt[at, :], hi, lo)
        early = lax.broadcasted_iota(jnp.int32, (64, 128), 1) < 64
        for i in range(2):
            m = 128 * i
            mixed = jnp.where(early, pwg[m : m + 64, m : m + 128], pwg[m + 64 : m + 128, m : m + 128])
            pwg_out[(2 * g + i) * 64 : (2 * g + i) * 64 + 64, :] = mixed
        shift = three(nn, wph[g], wpl[g], hi, lo)
        content = dqct_s[at, :]
        dq = (content + shift).T.astype(BF)
        dq_out[:, at] = dq
        shi, slo = split(shift)
        chi, clo = split(content)
        vec_out[0:1, at] = (nt(ones, chi) + nt(ones, clo))[0:1]
        vec_out[1:2, at] = (nt(ones, shi) + nt(ones, slo))[0:1]
        vec_out[2:3, at] = jnp.sum(dq.astype(F32), axis=0, keepdims=True)
    vec_out[3:4, :] = jnp.sum(dv_out[...].astype(F32), axis=0, keepdims=True)


def attn_bwd(r, args, after=()):
    return call(
        functools.partial(attn_bwd_kernel, r), "attn_bwd", (), args,
        (b16(512, 768), b16(512, 768), b16(256, 768), f32(384, 128), f32(8, 768)),
        (vs(768, 256), vs(768, 256), vs(3, 256, 256, dtype=BF), vs(3, 256, 256, dtype=BF)),
        after, mib=14, flops=8 * 10**9, moved=12 * 10**6,
    )


def tokens_back_kernel(dk0, dk1, dv0, dv1, dq0, dq1, d1, wq, wk, wv, t0, t1, t2, t3, tok_s):
    rows = lax.broadcasted_iota(jnp.int32, (512, 256), 0)
    cols = lax.broadcasted_iota(jnp.int32, (512, 256), 1)
    spread = jnp.where(rows // 2 == cols, 0.5, 0.0).astype(BF)
    for r, (dk, dv, dq) in enumerate(((dk0, dv0, dq0), (dk1, dv1, dq1))):
        hi, lo = split(d1[r * 256 : r * 256 + 256, :] + nt(dq[...], wq[...]))
        tok_s[...] = (nt(dk[...], wk[...]) + nt(dv[...], wv[...])) + (nn(spread, hi) + nn(spread, lo))
        for d, out in enumerate((t0, t1, t2, t3)):
            out[r] = tok_s[d * 128 : d * 128 + 128, :].astype(BF)


def weights_back_kernel(
    masks, xt0, xt1, pt0, pt1, dk0, dk1, dv0, dv1, dq0, dq1, pwg0, pwg1, av0, av1, vec_d, vec_u, upb_a, upb_b,
    near, far, g_s, smalls,
):
    smalls[0:384, :] = pwg0[...] + pwg1[...]
    attn = av0[...] + av1[...]
    lines = [vec_d[i : i + 1, :] for i in range(3)] + [vec_u[i : i + 1, :] for i in range(3)]
    lines += [upb[:, 768 * i : 768 * i + 768] for upb in (upb_a, upb_b) for i in range(2)] + [attn[i : i + 1, :] for i in range(4)]
    for i, line in enumerate(lines):
        for t in range(6):
            row = 384 + 6 * i + t
            smalls[row : row + 1, :] = line[:, 128 * t : 128 * t + 128]
    smalls[468:512, :] = jnp.zeros((44, 128), F32)
    g_s[0:768, :] = nn(pt0[...], dq0[...]) + nn(pt1[...], dq1[...])
    g_s[768:1536, :] = nn(xt0[...], dk0[...]) + nn(xt1[...], dk1[...])
    g_s[1536:2304, :] = nn(xt0[...], dv0[...]) + nn(xt1[...], dv1[...])
    put_blocks(g_s, near, far, masks[2], [(i, i) for i in range(NA)], 0)
    put_blocks(g_s, near, far, masks[3], [(i, i) for i in range(NA, 27)], 0)
    for r in range(16):
        for half, out in enumerate((near, far)):
            row = pl.ds(pl.multiple_of((r ^ masks[3] ^ (16 * half)) * 16, 16), 16)
            out[r, 27] = smalls[row, :].astype(BF)


def last_back_kernel(
    scalars, k, v, kt, qc, qf, qht, qlt, lse, dctx, kf, kst, far_q, pw, xt0, xt1, pt0, pt1, dk0, dv0, dq0, pwg0, av0, vec_d,
    vec_u, upb_a, upb_b, d1, wq, wk, wv,
    near, far, t0, t1, t2, t3,
    dqct_s, dpt_s, wph, wpl, dk1, dv1, dq1, pwg1, av1, g_s, smalls, tok_s,
):
    attn_bwd_kernel(
        1, k, v, kt, qc, qf, qht, qlt, lse, dctx, kf, kst, far_q, pw, dk1, dv1, dq1, pwg1, av1, dqct_s, dpt_s, wph, wpl
    )
    weights_back_kernel(
        scalars, xt0, xt1, pt0, pt1, dk0, dk1, dv0, dv1, dq0, dq1, pwg0, pwg1, av0, av1, vec_d, vec_u, upb_a, upb_b, near, far,
        g_s, smalls,
    )
    tokens_back_kernel(dk0, dk1, dv0, dv1, dq0, dq1, d1, wq, wk, wv, t0, t1, t2, t3, tok_s)


def last_back(scalars, args, after=()):
    grad = b16(16, 28, 16, 128)
    return call(
        last_back_kernel, "last_back", (scalars,), args,
        (grad, grad) + (b16(2, 128, 768),) * 4,
        (
            vs(768, 256), vs(768, 256), vs(3, 256, 256, dtype=BF), vs(3, 256, 256, dtype=BF), vs(512, 768, dtype=BF),
            vs(512, 768, dtype=BF), vs(256, 768, dtype=BF), vs(384, 128), vs(8, 768), vs(2304, 768), vs(512, 128),
            vs(512, 768),
        ),
        after, mib=28, flops=17 * 10**9, moved=30 * 10**6,
    )


def partner(x, bit):
    size = lax.axis_size("batch")
    return lax.ppermute(x, "batch", [(i, i ^ bit) for i in range(size)])


def add_kernel(step, cuts, parts, *refs):
    here, came, outs = refs[:parts], refs[parts : 2 * parts], refs[2 * parts :]
    if step < 5:
        pieces = 2 if step < 4 else 1
        at = 0
        for p in range(parts):
            rows, slabs = here[p].shape[:2]
            half = rows // pieces

            def add(r, carry, p=p, at=at, half=half, slabs=slabs):
                for h in range(pieces):
                    total = (here[p][h * half + r].astype(F32) + came[p][h * half + r].astype(F32)).astype(BF)
                    if len(outs) == pieces:
                        outs[h][r, at : at + slabs] = total
                    elif parts == 2:
                        outs[pieces * p + h][r] = total
                    else:
                        outs[h][r] = total[:cuts]
                        outs[pieces + h][r] = total[cuts:]
                return carry

            lax.fori_loop(0, half, add, 0)
            at += slabs
    else:
        at = 0
        for p in range(parts):
            rows, slabs = here[p].shape[:2]
            for source, to in ((here[p], slice(0, rows)), (came[p], slice(rows, 2 * rows))):
                if len(outs) == 1:
                    outs[0][to, at : at + slabs] = source[...]
                elif parts == 2:
                    outs[p][to] = source[...]
                else:
                    outs[0][to] = source[:, :cuts]
                    outs[1][to] = source[:, cuts:]
            at += slabs


class Order:
    def __init__(self):
        self.last = ()

    def run(self, function, *args, also=()):
        *results, token = function(*args, (*self.last, *also))
        self.last = (token,)
        return results


class Sum:
    def __init__(self, order, keep, sends, cuts, bits):
        core, first, second, third, fourth, self.others = bits
        self.bits = [(core,) * len(keep), (first, second), (second, first), (third,), (fourth,)]
        self.bits += [(fourth,), (third,), (second, first), (first, second), (core,)]
        self.cuts, self.slabs = cuts, sum(k.shape[1] for k in keep)
        self.order, self.keep, self.sends, self.step = order, keep, sends, 0

    def start(self):
        self.got = [partner(s, b) for s, b in zip(self.sends, self.bits[self.step])]
        return self

    def plan(self):
        step, a, b = self.step, self.cuts, self.slabs - self.cuts
        here = self.keep if step < 5 else self.sends
        rows = (8, 4, 2, 1, 1, 2, 4, 8, 16)[step]
        shapes = [(a,), (b,)] if step in (0, 1, 6, 7) else [(a + b,)]
        outs = [b16(rows, *s, 16, 128) for s in shapes for _ in range(2 if step < 4 else 1)]
        kernel = functools.partial(add_kernel, step, a, len(here))
        return kernel, (*here, *self.got), outs

    def take(self, outs):
        step = self.step
        if step < 4:
            self.keep, self.sends = outs[::2], outs[1::2]
        else:
            self.sends = outs
        if step == 4:
            for bit in self.others:
                self.sends = [(s.astype(F32) + partner(s, bit).astype(F32)).astype(BF) for s in self.sends]
        self.step += 1

    def finish(self):
        if self.step < 9:
            finish_together(self.order, (self,))
        else:
            self.sends = (*self.sends, *self.got)
            self.step += 1
        return self


def finish_together(order, sums, also=()):
    plans = [s.plan() for s in sums]
    args = [a for p in plans for a in p[1]]
    outs = [o for p in plans for o in p[2]]

    def kernel(*refs):
        here, there = 0, len(args)
        for step, taken, given in plans:
            step(*refs[here : here + len(taken)], *refs[there : there + len(given)])
            here, there = here + len(taken), there + len(given)

    results = order.run(
        lambda after: call(kernel, "sum_step", (), args, outs, after=after, mib=8, moved=10**6), also=also
    )
    for s, (_, _, given) in zip(sums, plans):
        s.take(results[: len(given)])
        results = results[len(given) :]


def get_blocks(me, halves, slabs, outs):
    for half, source in enumerate(halves):
        for r in range(16):
            place = (r ^ me) ^ (16 * half)
            row = pl.multiple_of((place // 2) * 48, 16)
            col = pl.multiple_of((place % 2) * 384, 128)
            for at, s in slabs:
                to = pl.ds(row + s % 9 // 3 * 16, 16)
                outs[s // 9][to, pl.ds(col + s % 3 * 128, 128)] = source[r, at].astype(F32)


def rows_kernel(masks, near, far, out):
    c = pl.program_id(0)
    me = masks[2 + c // 3]
    for r in range(32):
        row = pl.ds(pl.multiple_of((r ^ me) * 16, 16), 16)
        for j in range(6):
            out[row, j * 128 : j * 128 + 128] = (near, far)[r // 16][r % 16, c * 6 + j].astype(F32)


def assemble_rows(masks, halves, after=()):
    return call_grid(
        rows_kernel, "assemble_rows", 6, (masks,), halves, (f32(3072, 768),), (pl.BlockSpec((512, 768), lambda c: (c, 0)),),
        after, 24, 14 * 10**6,
    )


def up_kernel(masks, near, far, out, o_out):
    c = pl.program_id(0)
    me = masks[2 + c // 3]
    for r in range(32):
        place = r ^ me
        row = pl.multiple_of((place // 4) * 96, 32)
        col = pl.ds(pl.multiple_of((place % 4) * 128, 128), 128)
        for j in range(6):
            out[pl.ds(row + 16 * j, 16), col] = (near, far)[r // 16][r % 16, c * 6 + j].astype(F32)

    @pl.when(c == 0)
    def _():
        get_blocks(masks[3], (near, far), [(36 + i, i) for i in range(9)], (o_out,))


def assemble_up(masks, halves, after=()):
    return call_grid(
        up_kernel, "assemble_up", 6, (masks,), halves, (f32(768, 3072), f32(768, 768)),
        (pl.BlockSpec((768, 512), lambda c: (0, c)), VM), after, 28, 18 * 10**6,
    )


def three_kernel(masks, near, far, q_out, k_out, v_out, w_out, l_out, s_out):
    outs = (q_out, k_out, v_out)
    get_blocks(masks[2], (near, far), [(i, i) for i in range(NA)], outs)
    get_blocks(masks[3], (near, far), [(i, i) for i in range(NA, 27)], outs)
    for half, source in enumerate((near, far)):
        for r in range(16):
            row = pl.ds(pl.multiple_of((r ^ masks[3] ^ (16 * half)) * 16, 16), 16)
            s_out[row, :] = source[r, 27].astype(F32)
    for h in range(12):
        w_out[h] = s_out[h // 2 * 64 : h // 2 * 64 + 64, h % 2 * 64 : h % 2 * 64 + 64]
    for i in range(14):
        for t in range(6):
            row = 384 + 6 * i + t
            l_out[i : i + 1, 128 * t : 128 * t + 128] = s_out[row : row + 1, :]


def assemble_three(masks, halves, after=()):
    return call(
        three_kernel, "assemble_three", (masks,), halves, (f32(768, 768),) * 3 + (f32(12, 64, 64), f32(16, 768)),
        (vs(512, 128),), after, mib=36, moved=11 * 10**6, last=True,
    )


def owners_kernel(scalars, p0, p2, p13, out):
    j = scalars[0]
    out[j] = p0[...].astype(out.dtype)
    out[j ^ 2] = (p2[0] if len(p2.shape) > len(p0.shape) else p2[...]).astype(out.dtype)
    out[j ^ 1] = p13[0].astype(out.dtype)
    out[j ^ 3] = p13[1].astype(out.dtype)


def assemble_owners(name, dtype, scalars, pieces, after=()):
    shape = (4, *pieces[0].shape)
    return call(
        owners_kernel, name, (scalars,), pieces, (jax.ShapeDtypeStruct(shape, dtype),), after=after, moved=5 * 10**6,
        last=True,
    )


def join_pieces(own, came, after=()):
    def kernel(a, b, out):
        out[0] = a[...]
        out[1] = b[1] if len(b.shape) > len(a.shape) else b[...]

    shape = (2, *own.shape)
    return call(kernel, "join", (), (own, came), (jax.ShapeDtypeStruct(shape, own.dtype),), after=after, moved=10**6)


def pick_kernel(row, scalars, blocks, o0, o1, o2, o3, sem):
    copies = []
    for d, out in enumerate((o0, o1, o2, o3)):
        source = blocks.at[scalars[0] ^ d] if row is None else blocks.at[scalars[0] ^ d, row]
        copies.append(pltpu.make_async_copy(source, out, sem.at[d]))
        copies[-1].start()
    for copy in copies:
        copy.wait()


def pick(row, scalars, blocks, after=()):
    shape = blocks.shape[1:] if row is None else blocks.shape[2:]
    return call(
        functools.partial(pick_kernel, row), "pick", (scalars,), (blocks,), (b16(*shape),) * 4, (sems(4),), after=after,
        mib=4, moved=2 * 10**6, far_args=(0,),
    )


def on_device(
    tokens, lengths, cotangent, query_weight, query_bias, key_weight, value_weight, value_bias, content_bias,
    position_bias, position_weight, out_weight, out_bias, inner_gain, inner_shift, up_weight, up_bias, down_weight,
    down_bias, outer_gain, outer_shift,
):
    size = lax.axis_size("batch")
    me = lax.axis_index("batch").astype(jnp.int32)
    j = me % G
    core, first, second, third, fourth = 1, 2, 4, 8, 16
    others = [1 << b for b in range(5, size.bit_length() - 1)]
    bits = (core, first, second, third, fourth, others)
    has = lambda bit: (me // bit) % 2
    low = has(core) * 16 + has(third) * 2 + has(fourth)
    scalars = jnp.stack(
        [j, me // G * 8 + 2 * j, low + has(first) * 8 + has(second) * 4, low + has(second) * 8 + has(first) * 4]
    )
    order = Order()

    by_owner = tokens[0].reshape(4, 2, 128, 768)
    cot_owner = cotangent[0].reshape(4, 2, 64, 768)

    def trade(pieces):
        return [pieces[0]] + [partner(pieces[d], d) for d in (1, 2, 3)]

    x0 = trade(order.run(pick, 0, scalars, by_owner))
    lines = (
        query_bias, content_bias, position_bias, value_bias, out_bias, inner_gain, inner_shift, down_bias, outer_gain,
        outer_shift,
    )
    near_q, far_q, kst, kf, vecs = order.run(tables, scalars, lengths, lines, ())
    s1 = order.run(pick, 1, scalars, by_owner)
    sc = order.run(pick, None, scalars, cot_owner)
    x1 = trade(order.run(gate, s1, also=x0[1:]))

    def forward(r, x):
        return order.run(
            attn_fwd, r, (*x, query_weight, key_weight, value_weight, vecs, position_weight, near_q, kf)
        )

    fwd = [forward(0, x0)]
    cot = trade(order.run(gate, sc, also=x1[1:]))
    fwd.append(forward(1, x1))
    k, v, kt, xt, qc, qf, qht, qlt, pt, pooled, ctx, ctxt, lse = zip(*fwd)
    outs = order.run(
        ffn_down, scalars, (*ctx, *pooled, *cot, out_weight, up_weight, down_weight, vecs, up_bias[None, :])
    )
    out0, out1, out23, d2, df, x1t, n1, rs1, gp, near, far, vec_d = outs
    far, out23 = order.run(gate, (far, out23))
    down = Sum(order, (near,), (far,), 18, bits).start()
    back23 = partner(out23, 2)
    acc, near, far, upb_a = order.run(ffn_up_a, scalars, (df, d2, gp, x1t, up_weight, down_weight))
    down.finish().start()
    (out13,) = order.run(join_pieces, out1, back23)
    back13 = partner(out13, 1)
    d1, dctx, near, far, vec_u, upb_b = order.run(
        ffn_up_b, scalars, (df, acc, gp, x1t, n1, rs1, *ctxt, out_weight, up_weight, down_weight, vecs, near, far)
    )
    down.finish().start()
    (far,) = order.run(gate, (far,))
    up = Sum(order, (near,), (far,), 18, bits).start()

    def backward(r):
        return k[r], v[r], kt[r], qc[r], qf[r], qht[r], qlt[r], lse[r], dctx, kf, kst, far_q, position_weight

    dk, dv, dq, pwg, attn_vec = order.run(attn_bwd, 0, backward(0))
    finish_together(order, (down, up))
    down.start(), up.start()
    near, far, t0, t1, t2, t3 = order.run(
        last_back, scalars,
        (
            *backward(1), *xt, *pt, dk, dv, dq, pwg, attn_vec, vec_d, vec_u, upb_a, upb_b, d1, query_weight, key_weight,
            value_weight,
        ),
    )

    finish_together(order, (up, down))
    up.start(), down.start()
    (far,) = order.run(gate, (far,))
    three = Sum(order, (near,), (far,), NA, bits).start()
    finish_together(order, (up, down, three))
    up.start(), down.start(), three.start()
    finish_together(order, (up, down, three))
    up.start(), down.start(), three.start()
    (t3,) = order.run(gate, (t3,))
    u3 = partner(t3, 2)
    finish_together(order, (up, down, three), also=(u3,))
    up.start(), down.start(), three.start()
    (t2,) = order.run(gate, (t2,))
    u2 = partner(t2, 2)
    finish_together(order, (up, down, three), also=(u2,))
    up.start(), down.start(), three.start()
    (t13,) = order.run(join_pieces, t1, u3)
    u13 = partner(t13, 1)
    layer_output = order.run(assemble_owners, "layer_output", BF, scalars, (out0, back23, back13))[0]
    finish_together(order, (up, three, down))
    up.start(), three.start(), down.start()
    finish_together(order, (up, three))
    up.start(), three.start()
    down.finish()
    down_weight_grad = order.run(assemble_rows, scalars, down.sends)[0]
    finish_together(order, (three,))
    three.start()
    tokens_grad = order.run(assemble_owners, "tokens_grad", F32, scalars, (t0, u2, u13))[0]
    finish_together(order, (three,))
    three.start()
    finish_together(order, (up,))
    up.start()
    up.finish()
    up_weight_grad, out_weight_grad = order.run(assemble_up, scalars, up.sends)
    finish_together(order, (three,))
    three.start()
    three.finish()
    query_weight_grad, key_weight_grad, value_weight_grad, position_weight_grad, lines = order.run(
        assemble_three, scalars, three.sends
    )
    layer_output = layer_output.reshape(1, 8, 64, 768)
    tokens_grad = tokens_grad.reshape(1, 8, 128, 768)
    line = lambda i: lines[i]
    return (
        layer_output, tokens_grad, query_weight_grad, line(12), key_weight_grad, value_weight_grad, line(13), line(10),
        line(11), position_weight_grad, out_weight_grad, line(5), line(3), line(4),
        up_weight_grad, lines[6:10].reshape(3072), down_weight_grad, line(2), line(0), line(1),
    )


def solution(mesh):
    in_specs = (P("batch", None, None, None), P(), P("batch", None, None, None)) + (P(),) * 18
    out_specs = (P("batch", None, None, None),) * 2 + (P(),) * 18
    return jax.shard_map(on_device, mesh=mesh, in_specs=in_specs, out_specs=out_specs, check_vma=False)
```

```python
import functools
import math

import jax
import jax.numpy as jnp
from jax import lax
from jax.experimental import pallas as pl
from jax.experimental.pallas import tpu as pltpu
from jax.sharding import PartitionSpec as P

G = 4
F32 = jnp.float32
BF = jnp.bfloat16
VM = pl.BlockSpec(memory_space=pltpu.VMEM)
SM = pl.BlockSpec(memory_space=pltpu.SMEM)
ANY = pl.BlockSpec(memory_space=pl.ANY)
HBM = pl.BlockSpec(memory_space=pltpu.HBM)
BLK = 16
NA = 18
CH = 512


def nn(a, b):
    return lax.dot_general(a, b, (((1,), (0,)), ((), ())), preferred_element_type=F32)


def nt(a, b):
    return lax.dot_general(a, b, (((1,), (1,)), ((), ())), preferred_element_type=F32)


def tn(a, b):
    return lax.dot_general(a, b, (((0,), (0,)), ((), ())), preferred_element_type=F32)


def split(a):
    hi = a.astype(BF)
    return hi, (a - hi.astype(F32)).astype(BF)


def three(dot, a_hi, a_lo, b_hi, b_lo):
    return dot(a_hi, b_hi) + (dot(a_hi, b_lo) + dot(a_lo, b_hi))


def params(mib):
    return pltpu.CompilerParams(vmem_limit_bytes=mib << 20)


def cost(flops, bytes_accessed, transcendentals=0):
    return pl.CostEstimate(
        flops=flops, bytes_accessed=bytes_accessed, transcendentals=transcendentals
    )


def b16(*shape):
    return jax.ShapeDtypeStruct(shape, BF)


def f32(*shape):
    return jax.ShapeDtypeStruct(shape, F32)


TOKEN = (8, 128)


def call(
    kernel, name, scalars, args, outs, scratch=(), after=(), mib=16, flops=0, moved=0, far_outs=(), last=False, far_args=(),
    aliases=(), free=(),
):
    waits = len(after)
    at = waits + len(scalars) + len(args) + len(outs)

    def body(*refs):
        refs[at][...] = jnp.zeros(TOKEN, F32)
        kernel(*refs[waits:at], *refs[at + 1 :])

    place = lambda i, o: o if last else (pltpu.HBM if i in far_outs else pltpu.VMEM)(o.shape, o.dtype)
    space = lambda i: pltpu.HBM if i in far_args else pltpu.VMEM
    near = [a if last or i in free else pltpu.with_memory_space_constraint(a, space(i)) for i, a in enumerate(args)]
    return pl.pallas_call(
        body,
        out_shape=tuple(place(i, o) for i, o in enumerate(outs)) + (pltpu.VMEM(TOKEN, F32),),
        in_specs=[ANY] * waits + [SM] * len(scalars) + [HBM if i in far_args else VM for i in range(len(args))],
        out_specs=tuple(HBM if i in far_outs else VM for i in range(len(outs))) + (VM,),
        scratch_shapes=list(scratch),
        compiler_params=params(mib),
        cost_estimate=cost(flops, moved),
        input_output_aliases={waits + len(scalars) + i: o for i, o in aliases},
        name=name,
    )(*after, *scalars, *near)


def gate(arrays, after):
    n = len(arrays)
    outs = tuple(jax.ShapeDtypeStruct(a.shape, a.dtype) for a in arrays)
    return call(lambda *refs: None, "gate", (), arrays, outs, after=after, mib=4, aliases=[(i, i) for i in range(n)])


def call_grid(kernel, name, steps, scalars, args, outs, out_specs, after, mib, moved):
    waits = len(after)
    at = waits + len(scalars) + len(args) + len(outs)

    def body(*refs):
        refs[at][...] = jnp.zeros(TOKEN, F32)
        kernel(*refs[waits:at])

    return pl.pallas_call(
        body,
        out_shape=(*outs, pltpu.VMEM(TOKEN, F32)),
        grid=(steps,),
        in_specs=[ANY] * waits + [SM] * len(scalars) + [VM] * len(args),
        out_specs=(*out_specs, VM),
        compiler_params=params(mib),
        cost_estimate=cost(0, moved),
        name=name,
    )(*after, *scalars, *args)


def sems(n):
    return pltpu.SemaphoreType.DMA((n,))


def vs(*shape, dtype=F32):
    return pltpu.VMEM(shape, dtype)


def tables_kernel(count, scalars, lengths, *refs):
    lines, (near_q, far_q, kst, kf_out, vecs), near = refs[:10], refs[count : count + 5], refs[count + 5 : count + 15]
    copies = [pltpu.make_async_copy(a, b, refs[-1].at[i]) for i, (a, b) in enumerate(zip(lines, near))]
    for copy in copies:
        copy.start()
    j = scalars[0]
    exponent = -math.log(10000.0) / 32

    def positions(shape, size, step):
        row = lax.broadcasted_iota(jnp.int32, shape, 0)
        return step * (((row // size) ^ j) * size + row % size)

    def angles(shape, size, step):
        lane = lax.broadcasted_iota(jnp.int32, shape, 1)
        w = jnp.exp((lane % 32).astype(F32) * exponent)
        return positions(shape, size, step).astype(F32) * w, lane % 64 < 32

    theta, early = angles((256, 128), 64, 2)
    sin, cos = jnp.sin(theta), jnp.cos(theta)
    signed = jnp.where(early, cos, -cos)
    near_q[:, :128] = sin
    near_q[:, 128:] = signed
    far_q[:64] = sin.T[:64]
    far_q[64:] = -signed.T[:64]
    angle, early = angles((512, 128), 128, 1)
    sin, cos = jnp.sin(angle), jnp.cos(angle)
    kf = jnp.where(early, cos, sin)
    lane = lax.broadcasted_iota(jnp.int32, (512, 128), 1)
    kst[...] = jnp.where(lane < 64, kf, jnp.where(early, sin, cos)).astype(BF).T
    place = positions((512, 128), 128, 1)
    for r in range(2):
        bias = jnp.where(place < lengths[scalars[1] + r], 0.0, -1.0e9)
        kf_out[r, 0] = jnp.where(lane < 64, kf, jnp.where(lane == 64, bias, 0.0)).astype(BF)
        kf_out[r, 1] = jnp.where(lane >= 64, kf, jnp.where(lane == 0, bias, 0.0)).astype(BF)
    for i, copy in enumerate(copies):
        copy.wait()
        vecs[i : i + 1, :] = near[i][...].reshape(1, 768)


def tables(scalars, lengths, lines, weights, after):
    outs = (f32(256, 256), f32(128, 256), b16(128, 512), b16(2, 2, 512, 128), f32(10, 768))
    kernel = functools.partial(tables_kernel, 10 + len(weights))
    scratch = [vs(768) for _ in range(10)] + [sems(10)]
    return call(kernel, "tables", (scalars, lengths), (*lines, *weights), outs, scratch, after, far_args=range(10))


def spread_heads(weight, high, low, sides):
    for g in range(3):
        high[g] = jnp.zeros((256, 256 * sides), BF)
        low[g] = jnp.zeros((256, 256 * sides), BF)
        for a in range(4):
            hi, lo = split(weight[4 * g + a])
            at = slice(64 * a, 64 * a + 64)
            high[g, at, at] = hi
            low[g, at, at] = lo
            if sides == 2:
                there = slice(256 + 64 * a, 256 + 64 * a + 64)
                high[g, at, there] = jnp.concatenate([hi[:, 32:], hi[:, :32]], axis=1)
                low[g, at, there] = jnp.concatenate([lo[:, 32:], lo[:, :32]], axis=1)


def attn_fwd_kernel(
    r,
    x0, x1, x2, x3, wq, wk, wv, vecs, pw, near_q, kf,
    k_far, v_far, kt_far, xt_far, qc_far, qf_far, qht_far, qlt_far, pt_far, pooled_out, ctx_out, ctxt_out, lse_out,
    x_s, vt_s, wph, wpl, k_out, v_out, kt_out, xt_out, qc_out, qf_out, qht_out, qlt_out, pt_out, sem,
):
    copies = []

    def send(here, there):
        copies.append(pltpu.make_async_copy(here, there, sem.at[len(copies)]))
        copies[-1].start()

    qb, cb, pb, vb = (vecs[i : i + 1, :] for i in range(4))
    spread_heads(pw, wph, wpl, 2)
    rows = lax.broadcasted_iota(jnp.int32, (64, 128), 0)
    cols = lax.broadcasted_iota(jnp.int32, (64, 128), 1)
    pair = jnp.where(cols // 2 == rows, 0.5, 0.0).astype(BF)
    for d, piece in enumerate((x0, x1, x2, x3)):
        x_s[d * 128 : d * 128 + 128, :] = piece[...]
        pooled_out[d * 64 : d * 64 + 64, :] = nn(pair, piece[...])
    pooled_low = pooled_out[...].astype(BF)
    pt_out[...] = pooled_low.T
    send(pt_out, pt_far)
    x = x_s[...]
    xt_out[...] = x.T
    send(xt_out, xt_far)
    q = nn(pooled_low, wq[...]) + qb
    k = nn(x, wk[...]).astype(BF)
    k_out[...] = k
    kt_out[...] = k.T
    send(k_out, k_far)
    send(kt_out, kt_far)
    v = (nn(x, wv[...]) + vb).astype(BF)
    v_out[...] = v
    send(v_out, v_far)
    vt_s[...] = v.T
    qc_out[...] = (q + cb).astype(BF) * 0.125
    hi, lo = split(q + pb)
    qht_out[...] = hi.T
    qlt_out[...] = lo.T
    send(qc_out, qc_far)
    send(qht_out, qht_far)
    send(qlt_out, qlt_far)
    sin4 = jnp.concatenate([near_q[:, :128]] * 2, axis=1)
    cos4 = jnp.concatenate([near_q[:, 128:]] * 2, axis=1)
    for g in range(3):
        at = slice(256 * g, 256 * g + 256)
        both = three(nn, hi[:, at], lo[:, at], wph[g], wpl[g])
        side = both[:, :256] * sin4 + both[:, 256:] * cos4
        qf_out[:, at] = side.astype(BF) * 0.125
    send(qf_out, qf_far)
    lane = lax.broadcasted_iota(jnp.int32, (256, 128), 1)
    zero = jnp.zeros((256, 128), BF)
    one_a = (lane == 64).astype(F32).astype(BF)
    one_b = (lane == 0).astype(F32).astype(BF)

    def one_pair(i, carry):
        at = pl.ds(pl.multiple_of(i * 128, 128), 128)
        k_pair = k_out[:, at]
        qc_pair = qc_out[:, at]
        qf_pair = qf_out[:, at]
        for s in range(2):
            mine = (lane < 64) if s == 0 else (lane >= 64)
            left = jnp.concatenate([k_pair, kf[r, s]], axis=1)
            right = jnp.concatenate(
                [jnp.where(mine, qc_pair, zero), jnp.where(mine, qf_pair, (one_a, one_b)[s])], axis=1
            )
            scores = nt(left, right)
            highest = jnp.max(scores, axis=0, keepdims=True)
            raised = jnp.exp(scores - highest)
            total = jnp.sum(raised, axis=0, keepdims=True)
            weights = (raised * (1.0 / total)).astype(BF)
            head = pl.ds(pl.multiple_of(i * 128 + s * 64, 64), 64)
            ctxt_out[head, :] = nn(vt_s[head, :], weights).astype(BF)
            lse_out[i * 2 + s] = highest + jnp.log(total)
        return carry

    lax.fori_loop(0, 6, one_pair, 0, unroll=2)
    ctx_out[...] = ctxt_out[...].T
    for copy in copies:
        copy.wait()


def attn_fwd(r, args, after=()):
    return call(
        functools.partial(attn_fwd_kernel, r), "attn_fwd", (), args,
        (
            b16(512, 768), b16(512, 768), b16(768, 512), b16(768, 512), b16(256, 768), b16(256, 768),
            b16(768, 256), b16(768, 256), b16(768, 256), f32(256, 768), b16(256, 768), b16(768, 256),
            f32(12, 1, 256),
        ),
        (
            vs(512, 768, dtype=BF), vs(768, 512, dtype=BF), vs(3, 256, 512, dtype=BF), vs(3, 256, 512, dtype=BF),
            vs(512, 768, dtype=BF), vs(512, 768, dtype=BF), vs(768, 512, dtype=BF), vs(768, 512, dtype=BF),
            vs(256, 768, dtype=BF), vs(256, 768, dtype=BF), vs(768, 256, dtype=BF), vs(768, 256, dtype=BF),
            vs(768, 256, dtype=BF), sems(9),
        ),
        after, mib=20, far_outs=range(9), flops=4 * 10**9, moved=12 * 10**6,
    )


def layer_stats(a):
    center = a - jnp.mean(a, axis=-1, keepdims=True)
    rs = lax.rsqrt(jnp.mean(center * center, axis=-1, keepdims=True) + 1e-05)
    return center * rs, rs


def layer_back(dn, n, rs):
    return rs * (dn - jnp.mean(dn, axis=-1, keepdims=True) - n * jnp.mean(dn * n, axis=-1, keepdims=True))


def put_blocks(source, near, far, me, slabs, first):
    for r in range(16):
        for half, out in enumerate((near, far)):
            place = (r ^ me) ^ (16 * half)
            row = pl.multiple_of((place // 2) * 48, 16)
            col = pl.multiple_of((place % 2) * 384, 128)
            for to, s in slabs:
                at = pl.ds(row + (s // 9 * 768 + s % 9 // 3 * 16), 16)
                out[r, first + to] = source[at, pl.ds(col + s % 3 * 128, 128)].astype(BF)


def ffn_down_kernel(
    masks, ctx0, ctx1, pooled0, pooled1, c0, c1, c2, c3, wo, wu, wd, vecs, ub,
    out0, out1, out23, d2_out, df_out, x1t_out, n1_out, rs_out, gp_out, near, far, vec_out,
    act_s, acc_s, x1_s, g_s,
):
    def chunk(c):
        return pl.ds(pl.multiple_of(c * CH, CH), CH)

    ob, ig, ish, db, og, osh = (vecs[i : i + 1, :] for i in range(4, 10))
    ctx = jnp.concatenate([ctx0[...], ctx1[...]], axis=0)
    pooled = jnp.concatenate([pooled0[...], pooled1[...]], axis=0)
    n1, rs1 = layer_stats(pooled + (nn(ctx, wo[...]) + ob))
    n1_out[...] = n1
    rs_out[...] = rs1
    x1 = n1 * ig + ish
    x1_s[...] = x1.astype(BF)
    x1t_out[...] = x1.astype(BF).T
    acc_s[...] = x1 + db

    def up_chunk(c, carry):
        at = chunk(c)
        z = nn(x1_s[...], wu[:, at]) + ub[:, at]
        phi = 0.5 + 0.5 * lax.erf(z * math.sqrt(0.5))
        gp_out[:, at] = phi + z * (jnp.exp(-0.5 * z * z) * (1.0 / math.sqrt(2.0 * math.pi)))
        act = (z * phi).astype(BF)
        act_s[:, at] = act
        acc_s[...] += nn(act, wd[at, :])
        return carry

    lax.fori_loop(0, 6, up_chunk, 0, unroll=2)
    n2, rs2 = layer_stats(acc_s[...])
    result = (n2 * og + osh).astype(BF)
    for d, out in enumerate((out0, out1, out23.at[0], out23.at[1])):
        for r in range(2):
            out[r] = result[r * 256 + d * 64 : r * 256 + d * 64 + 64, :]
    cot = jnp.concatenate([c[r] for r in range(2) for c in (c0, c1, c2, c3)], axis=0).astype(F32)
    vec_out[0:1, :] = jnp.sum(cot * n2, axis=0, keepdims=True)
    vec_out[1:2, :] = jnp.sum(cot, axis=0, keepdims=True)
    d2 = layer_back(cot * og, n2, rs2)
    df = d2.astype(BF)
    df_out[...] = df
    vec_out[2:3, :] = jnp.sum(df.astype(F32), axis=0, keepdims=True)
    d2_out[...] = d2

    def down_chunk(which, i, carry):
        c = which * 3 + i
        g_s[...] = tn(act_s[:, chunk(c)], df_out[...])
        slab = c * 6
        me = masks[2 + which]
        for r in range(32):
            row = pl.ds(pl.multiple_of((r ^ me) * 16, 16), 16)
            for j in range(6):
                (near, far)[r // 16][r % 16, slab + j] = g_s[row, j * 128 : j * 128 + 128].astype(BF)
        return carry

    for which in range(2):
        lax.fori_loop(0, 3, functools.partial(down_chunk, which), 0, unroll=3)


def ffn_down(masks, args, after=()):
    grad = b16(16, 36, 16, 128)
    return call(
        ffn_down_kernel, "ffn_down", (masks,), args,
        (
            b16(2, 64, 768), b16(2, 64, 768), b16(2, 2, 64, 768), f32(512, 768), b16(512, 768),
            b16(768, 512), f32(512, 768), f32(512, 1), f32(512, 3072), grad, grad, f32(8, 768),
        ),
        (vs(512, 3072, dtype=BF), vs(512, 768), vs(512, 768, dtype=BF), vs(512, 768)),
        after, mib=18, flops=8 * 10**9, moved=25 * 10**6,
    )


def hidden_back(masks, which, df_in, gp, x1t, wu, wd, near, far, upb_out, acc_s, u_s):
    me = masks[2 + which]

    def up_chunk(i, carry):
        at = pl.ds(pl.multiple_of((which * 3 + i) * CH, CH), CH)
        dz = (nt(df_in[...], wd[at, :]) * gp[:, at]).astype(BF)
        upb_out[:, pl.ds(pl.multiple_of(i * CH, CH), CH)] = jnp.sum(dz.astype(F32), axis=0, keepdims=True)
        acc_s[...] += nt(dz, wu[:, at])
        u_s[...] = nn(x1t[...], dz)
        slab = (which * 3 + i) * 6
        for r in range(32):
            place = r ^ me
            row = pl.multiple_of((place // 4) * 96, 32)
            col = pl.ds(pl.multiple_of((place % 4) * 128, 128), 128)
            for j in range(6):
                (near, far)[r // 16][r % 16, slab + j] = u_s[pl.ds(row + 16 * j, 16), col].astype(BF)
        return carry

    lax.fori_loop(0, 3, up_chunk, 0, unroll=3)


def ffn_up_a_kernel(masks, df_in, d2, gp, x1t, wu, wd, acc, near, far, upb_out, u_s):
    acc[...] = d2[...]
    hidden_back(masks, 0, df_in, gp, x1t, wu, wd, near, far, upb_out, acc, u_s)


def ffn_up_a(masks, args, after=()):
    return call(
        ffn_up_a_kernel, "ffn_up_a", (masks,), args,
        (f32(512, 768), b16(16, 45, 16, 128), b16(16, 45, 16, 128), f32(1, 1536)),
        (vs(768, 512),), after, mib=14, flops=4 * 10**9, moved=12 * 10**6,
    )


def ffn_up_b_kernel(
    masks, df_in, acc, gp, x1t, n1, rs, ctxt0, ctxt1, wo, wu, wd, vecs, near_in, far_in,
    d1_out, dctx_out, near, far, vec_out, upb_out,
    acc_s, u_s, o_s,
):
    ig = vecs[5:6, :]
    acc_s[...] = acc[...]
    hidden_back(masks, 1, df_in, gp, x1t, wu, wd, near, far, upb_out, acc_s, u_s)
    dx1 = acc_s[...]
    vec_out[0:1, :] = jnp.sum(dx1 * n1[...], axis=0, keepdims=True)
    vec_out[1:2, :] = jnp.sum(dx1, axis=0, keepdims=True)
    d1 = layer_back(dx1 * ig, n1[...], rs[...])
    d1_out[...] = d1
    do = d1.astype(BF)
    vec_out[2:3, :] = jnp.sum(do.astype(F32), axis=0, keepdims=True)
    dctx = nt(do, wo[...]).astype(BF)
    for r in range(2):
        dctx_out[r] = dctx[r * 256 : r * 256 + 256]
    o_s[...] = nn(ctxt0[...], do[:256]) + nn(ctxt1[...], do[256:])
    put_blocks(o_s, near, far, masks[3], [(i, i) for i in range(9)], 36)


def ffn_up_b(masks, args, after=()):
    return call(
        ffn_up_b_kernel, "ffn_up_b", (masks,), args,
        (f32(512, 768), b16(2, 256, 768), b16(16, 45, 16, 128), b16(16, 45, 16, 128), f32(8, 768), f32(1, 1536)),
        (vs(512, 768), vs(768, 512), vs(768, 768)),
        after, mib=16, flops=5 * 10**9, moved=14 * 10**6, aliases=((12, 2), (13, 3)),
    )


def attn_bwd_kernel(
    r,
    k, v, kt, qc, qf, qht, qlt, lse, dctx, kf, kst, far_q, pw,
    dk_out, dv_out, dq_out, pwg_out, vec_out,
    dqct_s, dpt_s, wph, wpl,
):
    spread_heads(pw, wph, wpl, 1)
    lane = lax.broadcasted_iota(jnp.int32, (256, 128), 1)
    zero = jnp.zeros((256, 128), BF)
    one_a = (lane == 64).astype(F32).astype(BF)
    one_b = (lane == 0).astype(F32).astype(BF)

    def one_pair(i, carry):
        at = pl.ds(pl.multiple_of(i * 128, 128), 128)
        k_pair = k[:, at]
        v_pair = v[:, at]
        qc_pair = qc[:, at]
        qf_pair = qf[:, at]
        dc_pair = dctx[r, :, at]
        for s in range(2):
            mine = (lane < 64) if s == 0 else (lane >= 64)
            left = jnp.concatenate([k_pair, kf[r, s]], axis=1)
            qc_mine = jnp.where(mine, qc_pair, zero)
            dc_mine = jnp.where(mine, dc_pair, zero)
            right = jnp.concatenate([qc_mine, jnp.where(mine, qf_pair, (one_a, one_b)[s])], axis=1)
            weights = jnp.exp(nt(left, right) - lse[i * 2 + s])
            dweights = nt(v_pair, dc_mine)
            inner = jnp.sum(weights * dweights, axis=0, keepdims=True)
            dscore = (weights * (dweights - inner)).astype(BF)
            dv_part = nn(weights.astype(BF), dc_mine)
            dk_part = nn(dscore, qc_mine)
            if s == 0:
                dv_first, dk_first = dv_part, dk_part
            head = pl.ds(pl.multiple_of(i * 128 + s * 64, 64), 64)
            side = nn(jnp.concatenate([kt[head, :], kst[...]], axis=0), dscore)
            dqct_s[head, :] = side[0:64] * 0.125
            dpt_s[head, :] = (side[64:128] * far_q[:64] + side[128:192] * far_q[64:]) * 0.125
        dv_out[:, at] = (dv_first + dv_part).astype(BF)
        dk_out[:, at] = (dk_first + dk_part).astype(BF)
        return carry

    lax.fori_loop(0, 6, one_pair, 0, unroll=2)
    ones = jnp.ones((8, 256), BF)
    for g in range(3):
        at = slice(256 * g, 256 * g + 256)
        hi, lo = split(dpt_s[at, :])
        pwg = three(nt, qht[at, :], qlt[at, :], hi, lo)
        early = lax.broadcasted_iota(jnp.int32, (64, 128), 1) < 64
        for i in range(2):
            m = 128 * i
            mixed = jnp.where(early, pwg[m : m + 64, m : m + 128], pwg[m + 64 : m + 128, m : m + 128])
            pwg_out[(2 * g + i) * 64 : (2 * g + i) * 64 + 64, :] = mixed
        shift = three(nn, wph[g], wpl[g], hi, lo)
        content = dqct_s[at, :]
        dq = (content + shift).T.astype(BF)
        dq_out[:, at] = dq
        shi, slo = split(shift)
        chi, clo = split(content)
        vec_out[0:1, at] = (nt(ones, chi) + nt(ones, clo))[0:1]
        vec_out[1:2, at] = (nt(ones, shi) + nt(ones, slo))[0:1]
        vec_out[2:3, at] = jnp.sum(dq.astype(F32), axis=0, keepdims=True)
    vec_out[3:4, :] = jnp.sum(dv_out[...].astype(F32), axis=0, keepdims=True)


def attn_bwd(r, args, after=()):
    return call(
        functools.partial(attn_bwd_kernel, r), "attn_bwd", (), args,
        (b16(512, 768), b16(512, 768), b16(256, 768), f32(384, 128), f32(8, 768)),
        (vs(768, 256), vs(768, 256), vs(3, 256, 256, dtype=BF), vs(3, 256, 256, dtype=BF)),
        after, mib=14, flops=8 * 10**9, moved=12 * 10**6,
    )


def tokens_back_kernel(dk0, dk1, dv0, dv1, dq0, dq1, d1, wq, wk, wv, t0, t1, t2, t3, tok_s):
    rows = lax.broadcasted_iota(jnp.int32, (512, 256), 0)
    cols = lax.broadcasted_iota(jnp.int32, (512, 256), 1)
    spread = jnp.where(rows // 2 == cols, 0.5, 0.0).astype(BF)
    for r, (dk, dv, dq) in enumerate(((dk0, dv0, dq0), (dk1, dv1, dq1))):
        hi, lo = split(d1[r * 256 : r * 256 + 256, :] + nt(dq[...], wq[...]))
        tok_s[...] = (nt(dk[...], wk[...]) + nt(dv[...], wv[...])) + (nn(spread, hi) + nn(spread, lo))
        for d, out in enumerate((t0, t1, t2, t3)):
            out[r] = tok_s[d * 128 : d * 128 + 128, :].astype(BF)


def weights_back_kernel(
    masks, xt0, xt1, pt0, pt1, dk0, dk1, dv0, dv1, dq0, dq1, pwg0, pwg1, av0, av1, vec_d, vec_u, upb_a, upb_b,
    near, far, g_s, smalls,
):
    smalls[0:384, :] = pwg0[...] + pwg1[...]
    attn = av0[...] + av1[...]
    lines = [vec_d[i : i + 1, :] for i in range(3)] + [vec_u[i : i + 1, :] for i in range(3)]
    lines += [upb[:, 768 * i : 768 * i + 768] for upb in (upb_a, upb_b) for i in range(2)] + [attn[i : i + 1, :] for i in range(4)]
    for i, line in enumerate(lines):
        for t in range(6):
            row = 384 + 6 * i + t
            smalls[row : row + 1, :] = line[:, 128 * t : 128 * t + 128]
    smalls[468:512, :] = jnp.zeros((44, 128), F32)
    g_s[0:768, :] = nn(pt0[...], dq0[...]) + nn(pt1[...], dq1[...])
    g_s[768:1536, :] = nn(xt0[...], dk0[...]) + nn(xt1[...], dk1[...])
    g_s[1536:2304, :] = nn(xt0[...], dv0[...]) + nn(xt1[...], dv1[...])
    put_blocks(g_s, near, far, masks[2], [(i, i) for i in range(NA)], 0)
    put_blocks(g_s, near, far, masks[3], [(i, i) for i in range(NA, 27)], 0)
    for r in range(16):
        for half, out in enumerate((near, far)):
            row = pl.ds(pl.multiple_of((r ^ masks[3] ^ (16 * half)) * 16, 16), 16)
            out[r, 27] = smalls[row, :].astype(BF)


def last_back_kernel(
    scalars, k, v, kt, qc, qf, qht, qlt, lse, dctx, kf, kst, far_q, pw, xt0, xt1, pt0, pt1, dk0, dv0, dq0, pwg0, av0, vec_d,
    vec_u, upb_a, upb_b, d1, wq, wk, wv,
    near, far, t0, t1, t2, t3,
    dqct_s, dpt_s, wph, wpl, dk1, dv1, dq1, pwg1, av1, g_s, smalls, tok_s,
):
    attn_bwd_kernel(
        1, k, v, kt, qc, qf, qht, qlt, lse, dctx, kf, kst, far_q, pw, dk1, dv1, dq1, pwg1, av1, dqct_s, dpt_s, wph, wpl
    )
    weights_back_kernel(
        scalars, xt0, xt1, pt0, pt1, dk0, dk1, dv0, dv1, dq0, dq1, pwg0, pwg1, av0, av1, vec_d, vec_u, upb_a, upb_b, near, far,
        g_s, smalls,
    )
    tokens_back_kernel(dk0, dk1, dv0, dv1, dq0, dq1, d1, wq, wk, wv, t0, t1, t2, t3, tok_s)


def last_back(scalars, args, after=()):
    grad = b16(16, 28, 16, 128)
    return call(
        last_back_kernel, "last_back", (scalars,), args,
        (grad, grad) + (b16(2, 128, 768),) * 4,
        (
            vs(768, 256), vs(768, 256), vs(3, 256, 256, dtype=BF), vs(3, 256, 256, dtype=BF), vs(512, 768, dtype=BF),
            vs(512, 768, dtype=BF), vs(256, 768, dtype=BF), vs(384, 128), vs(8, 768), vs(2304, 768), vs(512, 128),
            vs(512, 768),
        ),
        after, mib=28, flops=17 * 10**9, moved=30 * 10**6,
    )


def partner(x, bit):
    size = lax.axis_size("batch")
    return lax.ppermute(x, "batch", [(i, i ^ bit) for i in range(size)])


def add_kernel(step, cuts, parts, *refs):
    here, came, outs = refs[:parts], refs[parts : 2 * parts], refs[2 * parts :]
    if step < 5:
        pieces = 2 if step < 4 else 1
        at = 0
        for p in range(parts):
            rows, slabs = here[p].shape[:2]
            half = rows // pieces

            def add(r, carry, p=p, at=at, half=half, slabs=slabs):
                for h in range(pieces):
                    total = (here[p][h * half + r].astype(F32) + came[p][h * half + r].astype(F32)).astype(BF)
                    if len(outs) == pieces:
                        outs[h][r, at : at + slabs] = total
                    elif parts == 2:
                        outs[pieces * p + h][r] = total
                    else:
                        outs[h][r] = total[:cuts]
                        outs[pieces + h][r] = total[cuts:]
                return carry

            lax.fori_loop(0, half, add, 0)
            at += slabs
    else:
        at = 0
        for p in range(parts):
            rows, slabs = here[p].shape[:2]
            for source, to in ((here[p], slice(0, rows)), (came[p], slice(rows, 2 * rows))):
                if len(outs) == 1:
                    outs[0][to, at : at + slabs] = source[...]
                elif parts == 2:
                    outs[p][to] = source[...]
                else:
                    outs[0][to] = source[:, :cuts]
                    outs[1][to] = source[:, cuts:]
            at += slabs


class Order:
    def __init__(self):
        self.last = ()

    def run(self, function, *args, also=()):
        *results, token = function(*args, (*self.last, *also))
        self.last = (token,)
        return results


class Sum:
    def __init__(self, order, keep, sends, cuts, bits):
        core, first, second, third, fourth, self.others = bits
        self.bits = [(core,) * len(keep), (first, second), (second, first), (third,), (fourth,)]
        self.bits += [(fourth,), (third,), (second, first), (first, second), (core,)]
        self.cuts, self.slabs = cuts, sum(k.shape[1] for k in keep)
        self.order, self.keep, self.sends, self.step = order, keep, sends, 0

    def start(self):
        self.got = [partner(s, b) for s, b in zip(self.sends, self.bits[self.step])]
        return self

    def plan(self):
        step, a, b = self.step, self.cuts, self.slabs - self.cuts
        here = self.keep if step < 5 else self.sends
        rows = (8, 4, 2, 1, 1, 2, 4, 8, 16)[step]
        shapes = [(a,), (b,)] if step in (0, 1, 6, 7) else [(a + b,)]
        outs = [b16(rows, *s, 16, 128) for s in shapes for _ in range(2 if step < 4 else 1)]
        kernel = functools.partial(add_kernel, step, a, len(here))
        return kernel, (*here, *self.got), outs

    def take(self, outs):
        step = self.step
        if step < 4:
            self.keep, self.sends = outs[::2], outs[1::2]
        else:
            self.sends = outs
        if step == 4:
            for bit in self.others:
                self.sends = [(s.astype(F32) + partner(s, bit).astype(F32)).astype(BF) for s in self.sends]
        self.step += 1

    def finish(self):
        if self.step < 9:
            finish_together(self.order, (self,))
        else:
            self.sends = (*self.sends, *self.got)
            self.step += 1
        return self


def finish_together(order, sums, also=()):
    plans = [s.plan() for s in sums]
    args = [a for p in plans for a in p[1]]
    outs = [o for p in plans for o in p[2]]

    def kernel(*refs):
        here, there = 0, len(args)
        for step, taken, given in plans:
            step(*refs[here : here + len(taken)], *refs[there : there + len(given)])
            here, there = here + len(taken), there + len(given)

    results = order.run(
        lambda after: call(kernel, "sum_step", (), args, outs, after=after, mib=8, moved=10**6), also=also
    )
    for s, (_, _, given) in zip(sums, plans):
        s.take(results[: len(given)])
        results = results[len(given) :]


def get_blocks(me, halves, slabs, outs):
    for half, source in enumerate(halves):
        for r in range(16):
            place = (r ^ me) ^ (16 * half)
            row = pl.multiple_of((place // 2) * 48, 16)
            col = pl.multiple_of((place % 2) * 384, 128)
            for at, s in slabs:
                to = pl.ds(row + s % 9 // 3 * 16, 16)
                outs[s // 9][to, pl.ds(col + s % 3 * 128, 128)] = source[r, at].astype(F32)


def rows_kernel(masks, near, far, out):
    c = pl.program_id(0)
    me = masks[2 + c // 3]
    for r in range(32):
        row = pl.ds(pl.multiple_of((r ^ me) * 16, 16), 16)
        for j in range(6):
            out[row, j * 128 : j * 128 + 128] = (near, far)[r // 16][r % 16, c * 6 + j].astype(F32)


def assemble_rows(masks, halves, after=()):
    return call_grid(
        rows_kernel, "assemble_rows", 6, (masks,), halves, (f32(3072, 768),), (pl.BlockSpec((512, 768), lambda c: (c, 0)),),
        after, 24, 14 * 10**6,
    )


def up_kernel(masks, near, far, out, o_out):
    c = pl.program_id(0)
    me = masks[2 + c // 3]
    for r in range(32):
        place = r ^ me
        row = pl.multiple_of((place // 4) * 96, 32)
        col = pl.ds(pl.multiple_of((place % 4) * 128, 128), 128)
        for j in range(6):
            out[pl.ds(row + 16 * j, 16), col] = (near, far)[r // 16][r % 16, c * 6 + j].astype(F32)

    @pl.when(c == 0)
    def _():
        get_blocks(masks[3], (near, far), [(36 + i, i) for i in range(9)], (o_out,))


def assemble_up(masks, halves, after=()):
    return call_grid(
        up_kernel, "assemble_up", 6, (masks,), halves, (f32(768, 3072), f32(768, 768)),
        (pl.BlockSpec((768, 512), lambda c: (0, c)), VM), after, 28, 18 * 10**6,
    )


def three_kernel(masks, near, far, q_out, k_out, v_out, w_out, l_out, s_out):
    outs = (q_out, k_out, v_out)
    get_blocks(masks[2], (near, far), [(i, i) for i in range(NA)], outs)
    get_blocks(masks[3], (near, far), [(i, i) for i in range(NA, 27)], outs)
    for half, source in enumerate((near, far)):
        for r in range(16):
            row = pl.ds(pl.multiple_of((r ^ masks[3] ^ (16 * half)) * 16, 16), 16)
            s_out[row, :] = source[r, 27].astype(F32)
    for h in range(12):
        w_out[h] = s_out[h // 2 * 64 : h // 2 * 64 + 64, h % 2 * 64 : h % 2 * 64 + 64]
    for i in range(14):
        for t in range(6):
            row = 384 + 6 * i + t
            l_out[i : i + 1, 128 * t : 128 * t + 128] = s_out[row : row + 1, :]


def assemble_three(masks, halves, after=()):
    return call(
        three_kernel, "assemble_three", (masks,), halves, (f32(768, 768),) * 3 + (f32(12, 64, 64), f32(16, 768)),
        (vs(512, 128),), after, mib=36, moved=11 * 10**6, last=True,
    )


def owners_kernel(scalars, p0, p2, p13, out):
    j = scalars[0]
    out[j] = p0[...].astype(out.dtype)
    out[j ^ 2] = (p2[0] if len(p2.shape) > len(p0.shape) else p2[...]).astype(out.dtype)
    out[j ^ 1] = p13[0].astype(out.dtype)
    out[j ^ 3] = p13[1].astype(out.dtype)


def assemble_owners(name, dtype, scalars, pieces, after=()):
    shape = (4, *pieces[0].shape)
    return call(
        owners_kernel, name, (scalars,), pieces, (jax.ShapeDtypeStruct(shape, dtype),), after=after, moved=5 * 10**6,
        last=True,
    )


def join_pieces(own, came, after=()):
    def kernel(a, b, out):
        out[0] = a[...]
        out[1] = b[1] if len(b.shape) > len(a.shape) else b[...]

    shape = (2, *own.shape)
    return call(kernel, "join", (), (own, came), (jax.ShapeDtypeStruct(shape, own.dtype),), after=after, moved=10**6)


def pick_kernel(row, scalars, blocks, o0, o1, o2, o3, sem):
    copies = []
    for d, out in enumerate((o0, o1, o2, o3)):
        source = blocks.at[scalars[0] ^ d] if row is None else blocks.at[scalars[0] ^ d, row]
        copies.append(pltpu.make_async_copy(source, out, sem.at[d]))
        copies[-1].start()
    for copy in copies:
        copy.wait()


def pick(row, scalars, blocks, after=()):
    shape = blocks.shape[1:] if row is None else blocks.shape[2:]
    return call(
        functools.partial(pick_kernel, row), "pick", (scalars,), (blocks,), (b16(*shape),) * 4, (sems(4),), after=after,
        mib=4, moved=2 * 10**6, far_args=(0,),
    )


def on_device(
    tokens, lengths, cotangent, query_weight, query_bias, key_weight, value_weight, value_bias, content_bias,
    position_bias, position_weight, out_weight, out_bias, inner_gain, inner_shift, up_weight, up_bias, down_weight,
    down_bias, outer_gain, outer_shift,
):
    size = lax.axis_size("batch")
    me = lax.axis_index("batch").astype(jnp.int32)
    j = me % G
    core, first, second, third, fourth = 1, 2, 4, 8, 16
    others = [1 << b for b in range(5, size.bit_length() - 1)]
    bits = (core, first, second, third, fourth, others)
    has = lambda bit: (me // bit) % 2
    low = has(core) * 16 + has(third) * 2 + has(fourth)
    scalars = jnp.stack(
        [j, me // G * 8 + 2 * j, low + has(first) * 8 + has(second) * 4, low + has(second) * 8 + has(first) * 4]
    )
    order = Order()

    by_owner = tokens[0].reshape(4, 2, 128, 768)
    cot_owner = cotangent[0].reshape(4, 2, 64, 768)

    def trade(pieces):
        return [pieces[0]] + [partner(pieces[d], d) for d in (1, 2, 3)]

    x0 = trade(order.run(pick, 0, scalars, by_owner))
    lines = (
        query_bias, content_bias, position_bias, value_bias, out_bias, inner_gain, inner_shift, down_bias, outer_gain,
        outer_shift,
    )
    near_q, far_q, kst, kf, vecs = order.run(tables, scalars, lengths, lines, ())
    s1 = order.run(pick, 1, scalars, by_owner)
    sc = order.run(pick, None, scalars, cot_owner)
    x1 = trade(order.run(gate, s1, also=x0[1:]))

    def forward(r, x):
        return order.run(
            attn_fwd, r, (*x, query_weight, key_weight, value_weight, vecs, position_weight, near_q, kf)
        )

    fwd = [forward(0, x0)]
    cot = trade(order.run(gate, sc, also=x1[1:]))
    fwd.append(forward(1, x1))
    k, v, kt, xt, qc, qf, qht, qlt, pt, pooled, ctx, ctxt, lse = zip(*fwd)
    outs = order.run(
        ffn_down, scalars, (*ctx, *pooled, *cot, out_weight, up_weight, down_weight, vecs, up_bias[None, :])
    )
    out0, out1, out23, d2, df, x1t, n1, rs1, gp, near, far, vec_d = outs
    far, out23 = order.run(gate, (far, out23))
    down = Sum(order, (near,), (far,), 18, bits).start()
    back23 = partner(out23, 2)
    acc, near, far, upb_a = order.run(ffn_up_a, scalars, (df, d2, gp, x1t, up_weight, down_weight))
    down.finish().start()
    (out13,) = order.run(join_pieces, out1, back23)
    back13 = partner(out13, 1)
    d1, dctx, near, far, vec_u, upb_b = order.run(
        ffn_up_b, scalars, (df, acc, gp, x1t, n1, rs1, *ctxt, out_weight, up_weight, down_weight, vecs, near, far)
    )
    down.finish().start()
    (far,) = order.run(gate, (far,))
    up = Sum(order, (near,), (far,), 18, bits).start()

    def backward(r):
        return k[r], v[r], kt[r], qc[r], qf[r], qht[r], qlt[r], lse[r], dctx, kf, kst, far_q, position_weight

    dk, dv, dq, pwg, attn_vec = order.run(attn_bwd, 0, backward(0))
    finish_together(order, (down, up))
    down.start(), up.start()
    near, far, t0, t1, t2, t3 = order.run(
        last_back, scalars,
        (
            *backward(1), *xt, *pt, dk, dv, dq, pwg, attn_vec, vec_d, vec_u, upb_a, upb_b, d1, query_weight, key_weight,
            value_weight,
        ),
    )

    finish_together(order, (up, down))
    up.start(), down.start()
    (far,) = order.run(gate, (far,))
    three = Sum(order, (near,), (far,), NA, bits).start()
    finish_together(order, (up, down, three))
    up.start(), down.start(), three.start()
    finish_together(order, (up, down, three))
    up.start(), down.start(), three.start()
    (t3,) = order.run(gate, (t3,))
    u3 = partner(t3, 2)
    finish_together(order, (up, down, three), also=(u3,))
    up.start(), down.start(), three.start()
    (t2,) = order.run(gate, (t2,))
    u2 = partner(t2, 2)
    finish_together(order, (up, down, three), also=(u2,))
    up.start(), down.start(), three.start()
    (t13,) = order.run(join_pieces, t1, u3)
    u13 = partner(t13, 1)
    layer_output = order.run(assemble_owners, "layer_output", BF, scalars, (out0, back23, back13))[0]
    finish_together(order, (up, three, down))
    up.start(), three.start(), down.start()
    finish_together(order, (up, three))
    up.start(), three.start()
    finish_together(order, (three,))
    three.start()
    down.finish()
    down_weight_grad = order.run(assemble_rows, scalars, down.sends)[0]
    tokens_grad = order.run(assemble_owners, "tokens_grad", F32, scalars, (t0, u2, u13))[0]
    finish_together(order, (three,))
    three.start()
    finish_together(order, (up,))
    up.start()
    up.finish()
    up_weight_grad, out_weight_grad = order.run(assemble_up, scalars, up.sends)
    finish_together(order, (three,))
    three.start()
    three.finish()
    query_weight_grad, key_weight_grad, value_weight_grad, position_weight_grad, lines = order.run(
        assemble_three, scalars, three.sends
    )
    layer_output = layer_output.reshape(1, 8, 64, 768)
    tokens_grad = tokens_grad.reshape(1, 8, 128, 768)
    line = lambda i: lines[i]
    return (
        layer_output, tokens_grad, query_weight_grad, line(12), key_weight_grad, value_weight_grad, line(13), line(10),
        line(11), position_weight_grad, out_weight_grad, line(5), line(3), line(4),
        up_weight_grad, lines[6:10].reshape(3072), down_weight_grad, line(2), line(0), line(1),
    )


def solution(mesh):
    in_specs = (P("batch", None, None, None), P(), P("batch", None, None, None)) + (P(),) * 18
    out_specs = (P("batch", None, None, None),) * 2 + (P(),) * 18
    return jax.shard_map(on_device, mesh=mesh, in_specs=in_specs, out_specs=out_specs, check_vma=False)
```
